32 devices in a mesh: group: 2 (over x), expert: 8 (over z, y), tensor: 2 (over core).
Axes of the slice: x: 2, y: 2, z: 4, core: 2. Of those that a mesh axis runs over, the one named last changes fastest.
Arguments:
- tokens: bfloat16 [2048, 4096], P(('group', 'expert'), 'tensor'), parts along dimension 0, may hold values from -6 to 6
- down_weight: bfloat16 [4096, 1024], P('tensor', 'expert'), may hold values from -0.09375 to 0.09375
- up_weight: bfloat16 [4096, 1024], P('tensor', 'expert'), may hold values from -0.1875 to 0.1875
- gate_proj: bfloat16 [32, 1024, 768], P('expert', None, 'tensor'), may hold values from -0.1875 to 0.1875
- up_proj: bfloat16 [32, 1024, 768], P('expert', None, 'tensor'), may hold values from -0.1875 to 0.1875
- down_proj: bfloat16 [32, 768, 1024], P('expert', 'tensor'), may hold values from -0.21875 to 0.21875
- routes: int32 [2048, 16], P('group'), parts along dimension 0, may hold values from 0 to 31, all different within a row; in each aligned block of 128 rows (0 to 127, 128 to 255, ...) at most 80 rows name the same one
- gates: int32 [2048, 16], P('group'), parts along dimension 0, may hold values from 1 to 16384
- cotangent: bfloat16 [2048, 4096], P(('group', 'expert'), 'tensor'), parts along dimension 0, may hold values from -6 to 6
Outputs:
- out: bfloat16 [2048, 4096], P(('group', 'expert'), 'tensor'), parts along dimension 0
- tokens_grad: bfloat16 [2048, 4096], P(('group', 'expert'), 'tensor'), parts along dimension 0
- gate_proj_grad: bfloat16 [64, 1024, 768], P(('group', 'expert'), None, 'tensor'), parts along dimension 0
- up_proj_grad: bfloat16 [64, 1024, 768], P(('group', 'expert'), None, 'tensor'), parts along dimension 0
- down_proj_grad: bfloat16 [64, 768, 1024], P(('group', 'expert'), 'tensor'), parts along dimension 0
- down_grad: float32 [8192, 1024], P(('group', 'tensor'), 'expert'), parts along dimension 0
- up_grad: float32 [8192, 1024], P(('group', 'tensor'), 'expert'), parts along dimension 0
The draws below stay inside these ranges and needn't reach their ends.
There are 2 independent parts, one for each index of `group`. The reference program is written for one: setup_inputs(seed, part) draws one part's arguments, and reference() takes and returns one part's arrays. A program takes and returns all parts, laid end to end along the dimension named above; an argument that names none is the same for every part. Nothing has to cross between parts.
Inputs may be any that keep to these rules, and one draw needn't show every extreme that they name: `routes`: each row names 16 different experts. In each aligned block of 128 rows (the tokens of one index of expert) no expert is named by more than 80 rows, and in every draw some expert is named by exactly 80 rows of one block.
All inputs are finite; a program needn't handle non-finite values.
Results may differ from the reference program's by a relative error of at most 0.025.
Values may be sent and summed in bfloat16 or wider, within the bound.
No kernel may reach another device: no remote copies, remote signals or barrier semaphores. Data moves between devices by JAX's collectives and lax.ppermute only.
A program may use at most 192 MiB of HBM per device.

```python
import math
import jax
import jax.numpy as jnp
import numpy as np

D = 4096
L = 1024
H = 768
TOPK = 16
TOK_DEV = 128
EXPERTS = 32
TOKENS = 1024
HALF = 384
CAP = 80
N_EXPERT = 8
N_TENSOR = 2


def with_ends(values, stream_key, smallest, high):
    shape = values.shape
    place = [jax.random.randint(jax.random.fold_in(stream_key, axis), (), 0, shape[axis]) for axis in range(len(shape))]
    values = values.at[tuple(place)].set(smallest)
    longest = shape.index(max(shape))
    place[longest] = (place[longest] + 1) % shape[longest]
    return values.at[tuple(place)].set(high)


def block_scale(rng, dims, split, smallest, high):
    def one(dim, shards_of):
        draws = jax.random.uniform(jax.random.fold_in(jax.random.fold_in(rng, 6), dim), (shards_of,), jnp.float32, smallest / len(split), high / len(split))
        return jnp.repeat(jnp.exp(draws), dims[dim] // shards_of).reshape((-1,) + (1,) * (len(dims) - dim - 1))

    gain = one(*split[0])
    for cut in split[1:]:
        gain = gain * one(*cut)
    return gain


def assign_block(stream_key, own, number, rows, count, top, limit, skew):
    ranking = jax.random.permutation(stream_key, count)
    crowded, usual = shares(count, rows * top, limit, skew, True), shares(count, rows * top, limit, skew, False)
    places = jnp.arange(count)

    def named(sizes, offset_by):
        used = int((sizes > 0).sum())
        fixed = max(1, used // 4)
        passed = fixed + (places - fixed + offset_by * (used - fixed)) % max(1, count - fixed)
        return jnp.zeros((count,), jnp.int32).at[ranking[jnp.where(places < fixed, places, passed)]].set(jnp.asarray(sizes, jnp.int32))

    sizes = jnp.where(number % 4 == 0, named(crowded, number // 4), named(usual, number - number // 4 - 1))
    mixed = jax.random.permutation(jax.random.fold_in(own, 3), count)
    donor, receiver = mixed[0:count // 2 * 2:2], mixed[1:count // 2 * 2:2]
    slack = jnp.minimum(sizes[donor] - 1, limit - sizes[receiver]) // 2
    slack = jnp.where((donor == ranking[0]) | (receiver == ranking[0]) | (sizes[receiver] == 0), 0, jnp.maximum(slack, 0))
    passed = jax.random.randint(jax.random.fold_in(own, 4), (count // 2,), 0, 1 << 20) % (slack + 1)
    sizes = sizes.at[donor].add(-passed).at[receiver].add(passed)
    items = jnp.searchsorted(jnp.cumsum(sizes), jnp.arange(rows * top), side="right").astype(jnp.int32)
    grid = items.reshape(top, rows).T
    grid = grid[jax.random.permutation(jax.random.fold_in(own, 1), rows)]
    offset_by = jax.random.randint(jax.random.fold_in(own, 2), (rows, 1), 0, top)
    return jnp.take_along_axis(grid, (jnp.arange(top)[None, :] + offset_by) % top, axis=1)


def shares(number_of, total, bound, lean, full):
    loads = [(1 << 20) // math.isqrt(rank ** lean) + 1 for rank in range(1, number_of + 1)]
    largest = bound if full else min(bound, max(-(-total // number_of), total * loads[0] // sum(loads)))
    least = 1 if total - largest >= number_of - 1 else 0
    holding, surplus = [largest] + [least] * (number_of - 1), total - largest - least * (number_of - 1)
    while surplus > 0:
        free = [i for i in range(1, number_of) if holding[i] < largest] or [i for i in range(1, number_of) if holding[i] < bound]
        whole, budget = sum([loads[i] for i in free]), surplus
        for i in free:
            addition = min(bound - holding[i], max(1, budget * loads[i] // whole), surplus)
            holding[i] = holding[i] + addition
            surplus = surplus - addition
    return np.array(holding)


def scatter_about(stream_key, extent, scale, limit, split=(), held_as=jnp.bfloat16):
    loudness = block_scale(stream_key, extent, split, -0.22, 0.18) if split else 1.0
    entries = jax.random.normal(stream_key, extent, jnp.float32) * scale * loudness
    return jnp.minimum(jnp.maximum(entries, -limit), limit).astype(held_as)


def setup_inputs(seed: int = 0, part: int = 0) -> dict:
    arg_keys = jax.random.split(jax.random.key(seed), 10)
    part_keys = jax.random.split(jax.random.fold_in(arg_keys[9], part), 10)
    tokens = scatter_about(part_keys[0], (TOKENS, D), 1.0, 6.0, ((0, 8), (1, 2)))
    down_weight = scatter_about(arg_keys[1], (D, L), D ** -0.5, 0.09375, ((0, 2), (1, 8)))
    up_weight = scatter_about(arg_keys[2], (D, L), L ** -0.5, 0.1875, ((0, 2), (1, 8)))
    gate_proj = scatter_about(arg_keys[3], (EXPERTS, L, H), L ** -0.5, 0.1875, ((0, 8), (2, 2)))
    up_proj = scatter_about(arg_keys[4], (EXPERTS, L, H), L ** -0.5, 0.1875, ((0, 8), (2, 2)))
    down_proj = scatter_about(arg_keys[5], (EXPERTS, H, L), H ** -0.5, 0.21875, ((0, 8), (1, 2)))
    routes_keys = jax.random.split(jax.random.fold_in(part_keys[6], 1), TOKENS // TOK_DEV)
    routes_turns = jax.random.permutation(jax.random.fold_in(part_keys[6], 3), TOKENS // TOK_DEV)
    routes = jax.vmap(lambda own, number: assign_block(jax.random.fold_in(part_keys[6], 2), own, number, TOK_DEV, EXPERTS, TOPK, CAP, 1))(routes_keys, routes_turns).reshape((TOKENS, TOPK))
    gates = with_ends(jax.random.randint(part_keys[7], (TOKENS, TOPK), 1, 16385), jax.random.fold_in(part_keys[7], 1), 1, 16384).astype(jnp.int32)
    cotangent = scatter_about(part_keys[8], (TOKENS, D), 1.0, 6.0, ((0, 8), (1, 2)))
    return {"tokens": tokens, "down_weight": down_weight, "up_weight": up_weight, "gate_proj": gate_proj, "up_proj": up_proj, "down_proj": down_proj, "routes": routes, "gates": gates, "cotangent": cotangent}


gate_unit = 2.0 ** -15


def block_slots(block_routes, expert_total, capacity):
    choose = (block_routes[:, :, None] == jnp.arange(expert_total, dtype=jnp.int32)[None, None, :]).astype(jnp.int32)
    token_hits = jnp.sum(choose, axis=1)
    before = jnp.cumsum(token_hits, axis=0) - token_hits
    position = jnp.sum(choose * before[:, None, :], axis=2)
    return block_routes * capacity + position


def reference(tokens, down_weight, up_weight, gate_proj, up_proj, down_proj, routes, gates, cotangent):
    blocks = N_EXPERT
    slot_span = blocks * CAP
    gate_value = gates.astype(jnp.float32) * gate_unit
    latent_in = jnp.dot(tokens, down_weight, preferred_element_type=jnp.float32).astype(jnp.bfloat16)
    routed = routes.reshape(blocks, TOK_DEV, TOPK)
    slots = jax.vmap(lambda block_routes: block_slots(block_routes, EXPERTS, CAP))(routed)
    position = slots - routed * CAP
    slot_where = routed * slot_span + jnp.arange(blocks, dtype=jnp.int32)[:, None, None] * CAP + position
    slot_where = slot_where.reshape(-1)
    owner_ids = jnp.broadcast_to(jnp.arange(TOKENS, dtype=jnp.int32)[:, None], (TOKENS, TOPK)).reshape(-1)
    slot_token = jnp.full((EXPERTS * slot_span,), TOKENS, jnp.int32).at[slot_where].set(owner_ids)
    slot_gate = jnp.zeros((EXPERTS * slot_span,), jnp.float32).at[slot_where].set(gate_value.reshape(-1))
    padded = jnp.concatenate([latent_in, jnp.zeros((1, L), jnp.bfloat16)], axis=0)
    expert_in = jnp.take(padded, slot_token, axis=0).reshape(EXPERTS, slot_span, L).astype(jnp.float32)
    gate_f = gate_proj.astype(jnp.float32)
    up_f = up_proj.astype(jnp.float32)
    down_f = down_proj.astype(jnp.float32)
    gate_pre = jnp.einsum("erl,elh->erh", expert_in, gate_f)
    up_pre = jnp.einsum("erl,elh->erh", expert_in, up_f)
    sigmoid_gate = jax.nn.sigmoid(gate_pre)
    activated = gate_pre * sigmoid_gate
    hidden = (activated * up_pre).astype(jnp.bfloat16).astype(jnp.float32)
    hidden_blocks = hidden.reshape(EXPERTS, slot_span, N_TENSOR, HALF)
    down_blocks = down_f.reshape(EXPERTS, N_TENSOR, HALF, L)
    pieces = jnp.einsum("erjh,ejhl->erjl", hidden_blocks, down_blocks).astype(jnp.bfloat16).astype(jnp.float32)
    weighted = jnp.sum(pieces, axis=2) * slot_gate.reshape(EXPERTS, slot_span, 1)
    latent_sum = jax.ops.segment_sum(weighted.reshape(-1, L), slot_token, num_segments=TOKENS + 1)[:TOKENS]
    latent_out = latent_sum.astype(jnp.bfloat16)
    out = jnp.dot(latent_out, up_weight.T, preferred_element_type=jnp.float32).astype(jnp.bfloat16)
    latent_grad = jnp.dot(cotangent, up_weight, preferred_element_type=jnp.float32).astype(jnp.bfloat16)
    grad_padded = jnp.concatenate([latent_grad, jnp.zeros((1, L), jnp.bfloat16)], axis=0)
    arrived = jnp.take(grad_padded, slot_token, axis=0).reshape(EXPERTS, slot_span, L).astype(jnp.float32)
    route_grad = (arrived * slot_gate.reshape(EXPERTS, slot_span, 1)).astype(jnp.bfloat16).astype(jnp.float32)
    hidden_grad = jnp.einsum("erl,ehl->erh", route_grad, down_f)
    gate_pre_grad = (hidden_grad * up_pre * sigmoid_gate * (1.0 + gate_pre * (1.0 - sigmoid_gate))).astype(jnp.bfloat16).astype(jnp.float32)
    up_pre_grad = (hidden_grad * activated).astype(jnp.bfloat16).astype(jnp.float32)
    down_proj_grad = jnp.einsum("erh,erl->ehl", hidden, route_grad).astype(jnp.bfloat16)
    gate_proj_grad = jnp.einsum("erl,erh->elh", expert_in, gate_pre_grad).astype(jnp.bfloat16)
    up_proj_grad = jnp.einsum("erl,erh->elh", expert_in, up_pre_grad).astype(jnp.bfloat16)
    gate_grad_blocks = gate_pre_grad.reshape(EXPERTS, slot_span, N_TENSOR, HALF)
    up_grad_blocks = up_pre_grad.reshape(EXPERTS, slot_span, N_TENSOR, HALF)
    gate_w_blocks = gate_f.reshape(EXPERTS, L, N_TENSOR, HALF)
    up_w_blocks = up_f.reshape(EXPERTS, L, N_TENSOR, HALF)
    input_piece = (jnp.einsum("erjh,eljh->erjl", gate_grad_blocks, gate_w_blocks)
                   + jnp.einsum("erjh,eljh->erjl", up_grad_blocks, up_w_blocks)).astype(jnp.bfloat16).astype(jnp.float32)
    in_terms = jnp.sum(input_piece, axis=2).reshape(-1, L)
    latent_in_grad = jax.ops.segment_sum(in_terms, slot_token, num_segments=TOKENS + 1)[:TOKENS].astype(jnp.bfloat16)
    tokens_grad = jnp.dot(latent_in_grad, down_weight.T, preferred_element_type=jnp.float32).astype(jnp.bfloat16)
    down_grad = jnp.dot(tokens.T, latent_in_grad, preferred_element_type=jnp.float32)
    up_grad = jnp.dot(cotangent.T, latent_out, preferred_element_type=jnp.float32)
    return (out, tokens_grad, gate_proj_grad, up_proj_grad, down_proj_grad, down_grad, up_grad)
```

```python
import jax
import jax.numpy as jnp
from jax import lax
from jax.experimental import pallas as pl
from jax.experimental.pallas import tpu as pltpu
from jax.sharding import PartitionSpec as P

gate_unit = 2.0 ** (-15)
bf16 = jnp.bfloat16
f32 = jnp.float32

NN = (((1,), (0,)), ((), ()))
NT = (((1,), (1,)), ((), ()))
TN = (((0,), (0,)), ((), ()))


def dot(a, b, dims=NN):
    return lax.dot_general(a, b, dims, preferred_element_type=f32)


def expert_kernel(
    x_ref, y_ref, g_ref, wg_ref, wu_ref, wd_ref,
    dwg_ref, dwu_ref, dwd_ref, lo_ref, lig_ref,
    wgu, hs, dpu, lo_acc, lig_acc,
):
    step = pl.program_id(0)
    steps = pl.num_programs(0)
    rows_total, latent = x_ref.shape
    pair, _, width = wg_ref.shape
    block = 256

    for j in range(pair):
        wgu[:, 2 * j * width : (2 * j + 1) * width] = wg_ref[j]
        wgu[:, (2 * j + 1) * width : (2 * j + 2) * width] = wu_ref[j]

    @pl.when(step == 0)
    def _():
        lo_acc[...] = jnp.zeros_like(lo_acc)
        lig_acc[...] = jnp.zeros_like(lig_acc)

    def row_block(i, _):
        rows = pl.ds(pl.multiple_of(i * block, block), block)
        x = x_ref[rows, :]
        hidden_grad = dot(y_ref[rows, :], wd_ref[...], NT)
        for j in range(pair):
            both = dot(x, wgu[:, 2 * j * width : (2 * j + 2) * width])
            gate_pre, up_pre = both[:, :width], both[:, width:]
            gate = g_ref[0, rows, j : j + 1]
            sig = jax.nn.sigmoid(gate_pre)
            act = gate_pre * sig
            hg = hidden_grad[:, j * width : (j + 1) * width] * gate
            hs[rows, j * width : (j + 1) * width] = (act * up_pre * gate).astype(bf16)
            dp = hg * up_pre * (sig * (1.0 + gate_pre * (1.0 - sig)))
            dpu[rows, 2 * j * width : (2 * j + 1) * width] = dp.astype(bf16)
            dpu[rows, (2 * j + 1) * width : (2 * j + 2) * width] = (hg * act).astype(bf16)
        lo_acc[rows, :] += dot(hs[rows, :], wd_ref[...])
        lig_acc[rows, :] += dot(dpu[rows, :], wgu[...], NT)
        return 0

    lax.fori_loop(0, rows_total // block, row_block, 0)

    def col_block(i, _):
        cols = pl.ds(pl.multiple_of(i * block, block), block)
        grads = dot(x_ref[:, cols], dpu[...], TN)
        for j in range(pair):
            dwg_ref[j, cols, :] = grads[:, 2 * j * width : (2 * j + 1) * width].astype(bf16)
            dwu_ref[j, cols, :] = grads[:, (2 * j + 1) * width : (2 * j + 2) * width].astype(bf16)
        return 0

    lax.fori_loop(0, latent // block, col_block, 0)
    dwd_ref[...] = dot(hs[...], y_ref[...], TN).astype(bf16)

    @pl.when(step == steps - 1)
    def _():
        lo_ref[...] = lo_acc[...].astype(bf16)
        lig_ref[...] = lig_acc[...].astype(bf16)


def experts(x, y, gate_columns, gate_proj, up_proj, down_proj):
    rows, latent = x.shape
    count, _, width = gate_proj.shape
    pair = 2 if rows <= 1024 and count % 2 == 0 else 1
    whole = lambda i: (0, 0)
    per_step = lambda i: (i, 0, 0)
    columns = gate_columns.reshape(rows, count // pair, pair).transpose(1, 0, 2)
    dwg, dwu, dwd, lo, lig = pl.pallas_call(
        expert_kernel,
        grid=(count // pair,),
        in_specs=[
            pl.BlockSpec((rows, latent), whole),
            pl.BlockSpec((rows, latent), whole),
            pl.BlockSpec((1, rows, pair), per_step),
            pl.BlockSpec((pair, latent, width), per_step),
            pl.BlockSpec((pair, latent, width), per_step),
            pl.BlockSpec((pair * width, latent), lambda i: (i, 0)),
        ],
        out_specs=[
            pl.BlockSpec((pair, latent, width), per_step),
            pl.BlockSpec((pair, latent, width), per_step),
            pl.BlockSpec((pair * width, latent), lambda i: (i, 0)),
            pl.BlockSpec((rows, latent), whole),
            pl.BlockSpec((rows, latent), whole),
        ],
        out_shape=[
            jax.ShapeDtypeStruct(gate_proj.shape, bf16),
            jax.ShapeDtypeStruct(up_proj.shape, bf16),
            jax.ShapeDtypeStruct((count * width, latent), bf16),
            jax.ShapeDtypeStruct((rows, latent), bf16),
            jax.ShapeDtypeStruct((rows, latent), bf16),
        ],
        scratch_shapes=[
            pltpu.VMEM((latent, 2 * pair * width), bf16),
            pltpu.VMEM((rows, pair * width), bf16),
            pltpu.VMEM((rows, 2 * pair * width), bf16),
            pltpu.VMEM((rows, latent), f32),
            pltpu.VMEM((rows, latent), f32),
        ],
        compiler_params=pltpu.CompilerParams(vmem_limit_bytes=(40 if rows <= 1024 else 60) * 1024 * 1024),
        cost_estimate=pl.CostEstimate(
            flops=18 * rows * latent * width * count,
            bytes_accessed=12 * latent * width * count + 8 * rows * latent,
            transcendentals=rows * width * count,
        ),
    )(x, y, columns, gate_proj, up_proj, down_proj.reshape(count * width, latent))
    return dwg, dwu, dwd.reshape(down_proj.shape), lo, lig


def local(tokens, down_weight, up_weight, gate_proj, up_proj, down_proj, routes, gates, cotangent):
    n_expert = lax.axis_size("expert")
    nz = n_expert // 2
    own = lax.axis_index("expert")
    z, y = own // 2, own % 2
    t = lax.axis_index("tensor")
    tok_rows = tokens.shape[0]
    half_rows = tok_rows // 2
    half_d = tokens.shape[1] // 2
    latent = gate_proj.shape[1]
    exp_local = gate_proj.shape[0]
    shard = down_weight.shape[1]

    y_perm = [(e, e ^ 1) for e in range(n_expert)]
    z_up = [(e, (e + 2) % n_expert) for e in range(n_expert)]
    z_down = [((e + 2) % n_expert, e) for e in range(n_expert)]
    y_swap = lambda v: lax.ppermute(v, "expert", y_perm)
    t_swap = lambda v: lax.ppermute(v, "tensor", [(0, 1), (1, 0)])

    def add(a, b):
        return (a.astype(f32) + b.astype(f32)).astype(bf16)

    def turn(v, axis):
        blocks = jnp.split(v, nz, axis=axis)
        orders = [
            jnp.concatenate([blocks[(c - k) % nz] for k in range(nz)], axis=axis)
            for c in range(nz)
        ]
        result = orders[0]
        for c in range(1, nz):
            result = jnp.where(z == c, orders[c], result)
        return result

    def flip(v, index, axis):
        first, second = jnp.split(v, 2, axis=axis)
        return jnp.where(index == 0, v, jnp.concatenate([second, first], axis=axis))

    def gather_z(v):
        parts = [v]
        for _ in range(nz - 1):
            parts.append(lax.ppermute(parts[-1], "expert", z_up))
        return parts

    def scatter_z(parts):
        total = parts[nz - 1]
        for k in range(nz - 2, -1, -1):
            total = add(lax.ppermute(total, "expert", z_down), parts[k])
        return total

    def plane_rows(v):
        halves = v.reshape(tok_rows, 2, half_d)
        mine = lax.dynamic_index_in_dim(halves, y, 1, keepdims=False)
        other = lax.dynamic_index_in_dim(halves, 1 - y, 1, keepdims=False)
        return jnp.concatenate([mine, y_swap(other)], axis=0)

    def plane_weight(v):
        halves = v.reshape(2, half_d, shard)
        mine = lax.dynamic_index_in_dim(halves, y, 0, keepdims=False)
        received = y_swap(lax.dynamic_index_in_dim(halves, 1 - y, 0, keepdims=False))
        first = jnp.where(y == 0, mine, received)
        second = jnp.where(y == 0, received, mine)
        return jnp.concatenate([first, second], axis=1)

    def project(rows, weights):
        part = jnp.concatenate([dot(rows, w).astype(bf16) for w in weights], axis=1)
        part = part.reshape(2, 2, half_rows, latent)
        mine = lax.dynamic_index_in_dim(part, t, 1, keepdims=False)
        part = add(mine, t_swap(lax.dynamic_index_in_dim(part, 1 - t, 1, keepdims=False)))
        part = add(part[0], y_swap(part[1]))
        part = turn(part, 1)
        part = jnp.stack(gather_z(part))
        part = jnp.stack([part, y_swap(part)])
        part = jnp.stack([part, t_swap(part)])
        return part.reshape(4 * nz * half_rows, latent)

    def collect(part):
        part = part.reshape(2, 2, nz, half_rows, latent)
        part = add(part[0], t_swap(part[1]))
        part = add(part[0], y_swap(part[1]))
        part = scatter_z([part[k] for k in range(nz)])
        part = turn(part, 1)
        part = jnp.stack([part, y_swap(part)])
        part = flip(jnp.stack([part, t_swap(part)], axis=1), t, 1)
        return part.reshape(2 * tok_rows, latent)

    def finish(part, rows, weights):
        cols = latent // nz
        whole = sum(
            dot(part[:, k * cols : (k + 1) * cols], weights[k], NT) for k in range(nz)
        ).astype(bf16)
        theirs = y_swap(whole[tok_rows:])
        result = jnp.where(
            y == 0,
            jnp.concatenate([whole[:tok_rows], theirs], axis=1),
            jnp.concatenate([theirs, whole[:tok_rows]], axis=1),
        )
        grad = scatter_z(
            [dot(rows, part[:, k * cols : (k + 1) * cols], TN).astype(bf16) for k in range(nz)]
        )
        grad = grad.reshape(half_d, 2, shard)
        mine = lax.dynamic_index_in_dim(grad, y, 1, keepdims=False)
        theirs = y_swap(lax.dynamic_index_in_dim(grad, 1 - y, 1, keepdims=False))
        grad = jnp.where(
            y == 0,
            jnp.concatenate([mine, theirs], axis=0),
            jnp.concatenate([theirs, mine], axis=0),
        ).astype(f32)
        return result, grad

    local_ids = own * exp_local + jnp.arange(exp_local, dtype=jnp.int32)
    hit = routes[:, :, None] == local_ids[None, None, :]
    gate_all = jnp.sum(jnp.where(hit, gates[:, :, None], 0), axis=1).astype(f32) * gate_unit
    gate_all = turn(gate_all.reshape(nz, 2, 2, half_rows, exp_local), 0)
    gate_all = flip(flip(gate_all, y, 1), t, 2)
    gate_columns = gate_all.transpose(2, 1, 0, 3, 4).reshape(-1, exp_local)

    down_parts = gather_z(plane_weight(down_weight))
    up_parts = gather_z(plane_weight(up_weight))
    token_rows = plane_rows(tokens)
    cot_rows = plane_rows(cotangent)
    latent_in = project(token_rows, down_parts)
    latent_grad = project(cot_rows, up_parts)

    gate_proj_grad, up_proj_grad, down_proj_grad, out_part, in_part = experts(
        latent_in, latent_grad, gate_columns, gate_proj, up_proj, down_proj
    )

    latent_out = collect(out_part)
    latent_in_grad = collect(in_part)
    out, up_grad = finish(latent_out, cot_rows, up_parts)
    tokens_grad, down_grad = finish(latent_in_grad, token_rows, down_parts)
    return (out, tokens_grad, gate_proj_grad, up_proj_grad, down_proj_grad, down_grad, up_grad)


def solution(mesh):
    in_specs = (
        P(("group", "expert"), "tensor"),
        P("tensor", "expert"),
        P("tensor", "expert"),
        P("expert", None, "tensor"),
        P("expert", None, "tensor"),
        P("expert", "tensor", None),
        P("group", None),
        P("group", None),
        P(("group", "expert"), "tensor"),
    )
    out_specs = (
        P(("group", "expert"), "tensor"),
        P(("group", "expert"), "tensor"),
        P(("group", "expert"), None, "tensor"),
        P(("group", "expert"), None, "tensor"),
        P(("group", "expert"), "tensor", None),
        P(("group", "tensor"), "expert"),
        P(("group", "tensor"), "expert"),
    )
    return jax.shard_map(local, mesh=mesh, in_specs=in_specs, out_specs=out_specs, check_vma=False)
```

```python
import jax
import jax.numpy as jnp
from jax import lax
from jax.experimental import pallas as pl
from jax.experimental.pallas import tpu as pltpu
from jax.sharding import PartitionSpec as P

gate_unit = 2.0 ** (-15)
bf16 = jnp.bfloat16
f32 = jnp.float32

NN = (((1,), (0,)), ((), ()))
NT = (((1,), (1,)), ((), ()))
TN = (((0,), (0,)), ((), ()))


def dot(a, b, dims=NN):
    return lax.dot_general(a, b, dims, preferred_element_type=f32)


def join_projections(wg_ref, wu_ref, wgu):
    pair, _, width = wg_ref.shape
    for j in range(pair):
        wgu[:, 2 * j * width : (2 * j + 1) * width] = wg_ref[j]
        wgu[:, (2 * j + 1) * width : (2 * j + 2) * width] = wu_ref[j]


def forward_kernel(
    x_ref, g_ref, wg_ref, wu_ref, wd_ref, hs_ref, cp_ref, cu_ref, lo_ref, wgu, lo_acc
):
    step = pl.program_id(0)
    pair, _, width = wg_ref.shape
    block = 256
    join_projections(wg_ref, wu_ref, wgu)

    @pl.when(step == 0)
    def _():
        lo_acc[...] = jnp.zeros_like(lo_acc)

    def row_block(i, _):
        rows = pl.ds(pl.multiple_of(i * block, block), block)
        x = x_ref[rows, :]
        for j in range(pair):
            cols = slice(j * width, (j + 1) * width)
            both = dot(x, wgu[:, 2 * j * width : (2 * j + 2) * width])
            gate_pre, up_pre = both[:, :width], both[:, width:]
            gate = g_ref[0, rows, j : j + 1]
            sig = jax.nn.sigmoid(gate_pre)
            act = gate_pre * sig * gate
            hs_ref[rows, cols] = (act * up_pre).astype(bf16)
            cu_ref[rows, cols] = act.astype(bf16)
            slope = up_pre * (sig * (1.0 + gate_pre * (1.0 - sig)))
            cp_ref[rows, cols] = (slope * gate).astype(bf16)
        lo_acc[rows, :] += dot(hs_ref[rows, :], wd_ref[...])
        return 0

    lax.fori_loop(0, x_ref.shape[0] // block, row_block, 0)

    @pl.when(step == pl.num_programs(0) - 1)
    def _():
        lo_ref[...] = lo_acc[...].astype(bf16)


def backward_kernel(
    y_ref, cp_ref, cu_ref, wg_ref, wu_ref, wd_ref, dpu_ref, lig_ref, wgu, lig_acc
):
    step = pl.program_id(0)
    pair, _, width = wg_ref.shape
    block = 256
    join_projections(wg_ref, wu_ref, wgu)

    @pl.when(step == 0)
    def _():
        lig_acc[...] = jnp.zeros_like(lig_acc)

    def row_block(i, _):
        rows = pl.ds(pl.multiple_of(i * block, block), block)
        hidden_grad = dot(y_ref[rows, :], wd_ref[...], NT)
        for j in range(pair):
            cols = slice(j * width, (j + 1) * width)
            hg = hidden_grad[:, cols]
            dp = hg * cp_ref[rows, cols].astype(f32)
            du = hg * cu_ref[rows, cols].astype(f32)
            dpu_ref[rows, 2 * j * width : (2 * j + 1) * width] = dp.astype(bf16)
            dpu_ref[rows, (2 * j + 1) * width : (2 * j + 2) * width] = du.astype(bf16)
        lig_acc[rows, :] += dot(dpu_ref[rows, :], wgu[...], NT)
        return 0

    lax.fori_loop(0, y_ref.shape[0] // block, row_block, 0)

    @pl.when(step == pl.num_programs(0) - 1)
    def _():
        lig_ref[...] = lig_acc[...].astype(bf16)


def down_grad_kernel(hs_ref, y_ref, dwd_ref):
    dwd_ref[...] = dot(hs_ref[...], y_ref[...], TN).astype(bf16)


def input_grad_kernel(x_ref, dpu_ref, dwg_ref, dwu_ref):
    pair, latent, width = dwg_ref.shape
    block = 256

    def col_block(i, _):
        cols = pl.ds(pl.multiple_of(i * block, block), block)
        grads = dot(x_ref[:, cols], dpu_ref[...], TN)
        for j in range(pair):
            dwg_ref[j, cols, :] = grads[:, 2 * j * width : (2 * j + 1) * width].astype(bf16)
            dwu_ref[j, cols, :] = grads[:, (2 * j + 1) * width : (2 * j + 2) * width].astype(bf16)
        return 0

    lax.fori_loop(0, latent // block, col_block, 0)


def shaped(*shape):
    return jax.ShapeDtypeStruct(shape, bf16)


def expert_calls(rows, latent, count, width):
    pair = 2 if rows <= 1024 and count % 2 == 0 else 1
    whole = pl.BlockSpec((rows, latent), lambda i: (0, 0))
    col_proj = pl.BlockSpec((pair, latent, width), lambda i: (i, 0, 0))
    row_proj = pl.BlockSpec((pair * width, latent), lambda i: (i, 0))
    hidden = pl.BlockSpec((rows, pair * width), lambda i: (0, i))
    hidden2 = pl.BlockSpec((rows, 2 * pair * width), lambda i: (0, i))
    gate_spec = pl.BlockSpec((1, rows, pair), lambda i: (i, 0, 0))
    joined = pltpu.VMEM((latent, 2 * pair * width), bf16)
    total = pltpu.VMEM((rows, latent), f32)
    units = 2 * rows * latent * width * count
    weight_bytes = 2 * latent * width * count
    hidden_bytes = 2 * rows * width * count
    latent_bytes = 2 * rows * latent

    def call(kernel, ins, outs, out_shape, scratch, parts, moved, exps=0):
        return pl.pallas_call(
            kernel,
            grid=(count // pair,),
            in_specs=ins,
            out_specs=outs,
            out_shape=out_shape,
            scratch_shapes=scratch,
            compiler_params=pltpu.CompilerParams(
                vmem_limit_bytes=(40 if rows <= 1024 else 56) * 1024 * 1024
            ),
            cost_estimate=pl.CostEstimate(
                flops=parts * units, bytes_accessed=moved, transcendentals=exps
            ),
        )

    hid = shaped(rows, count * width)
    lat = shaped(rows, latent)
    col = shaped(count, latent, width)
    forward = call(
        forward_kernel,
        [whole, gate_spec, col_proj, col_proj, row_proj],
        [hidden, hidden, hidden, whole],
        [hid, hid, hid, lat],
        [joined, total],
        3,
        3 * weight_bytes + 3 * hidden_bytes + 2 * latent_bytes,
        rows * width * count,
    )
    backward = call(
        backward_kernel,
        [whole, hidden, hidden, col_proj, col_proj, row_proj],
        [hidden2, whole],
        [shaped(rows, 2 * count * width), lat],
        [joined, total],
        3,
        3 * weight_bytes + 4 * hidden_bytes + 2 * latent_bytes,
    )
    down_grads = call(
        down_grad_kernel,
        [hidden, whole],
        row_proj,
        shaped(count * width, latent),
        [],
        1,
        weight_bytes + hidden_bytes + latent_bytes,
    )
    input_grads = call(
        input_grad_kernel,
        [whole, hidden2],
        [col_proj, col_proj],
        [col, col],
        [],
        2,
        2 * weight_bytes + 2 * hidden_bytes + latent_bytes,
    )

    def gate_blocks(gate_columns):
        return gate_columns.reshape(rows, count // pair, pair).transpose(1, 0, 2)

    return forward, backward, down_grads, input_grads, gate_blocks


def local(tokens, down_weight, up_weight, gate_proj, up_proj, down_proj, routes, gates, cotangent):
    n_expert = lax.axis_size("expert")
    n_group = lax.axis_size("group")
    own = lax.axis_index("expert")
    t = lax.axis_index("tensor")
    tok_rows = tokens.shape[0]
    half_rows = tok_rows // 2
    quarter_d = tokens.shape[1] // 4
    exp_local, latent, width = gate_proj.shape
    shard = down_weight.shape[1]

    nh = n_expert // 4
    h, c, y = own // 4, own // 2 % 2, own % 2
    shared = n_group % 2 == 0
    g = lax.axis_index("group") % 2

    def swapper(axis, size, bit):
        perm = [(i, i ^ bit) for i in range(size)]
        return lambda v: lax.ppermute(v, axis, perm)

    y_swap = swapper("expert", n_expert, 1)
    c_swap = swapper("expert", n_expert, 2)
    t_swap = swapper("tensor", 2, 1)
    g_swap = swapper("group", n_group, 1)
    h_up = [(e, (e + 4) % n_expert) for e in range(n_expert)]
    h_down = [((e + 4) % n_expert, e) for e in range(n_expert)]

    def add(a, b):
        return (a.astype(f32) + b.astype(f32)).astype(bf16)

    def turn(v, axis):
        blocks = jnp.split(v, nh, axis=axis)
        orders = [
            jnp.concatenate([blocks[(i - k) % nh] for k in range(nh)], axis=axis)
            for i in range(nh)
        ]
        result = orders[0]
        for i in range(1, nh):
            result = jnp.where(h == i, orders[i], result)
        return result

    def flip(v, index, axis):
        first, second = jnp.split(v, 2, axis=axis)
        return jnp.where(index == 0, v, jnp.concatenate([second, first], axis=axis))

    def pick(v, index, axis):
        mine = lax.dynamic_index_in_dim(v, index, axis, keepdims=False)
        other = lax.dynamic_index_in_dim(v, 1 - index, axis, keepdims=False)
        return mine, other

    def gather_h(v):
        parts = [v]
        for _ in range(nh - 1):
            parts.append(lax.ppermute(parts[-1], "expert", h_up))
        return parts

    def scatter_h(parts):
        total = parts[nh - 1]
        for k in range(nh - 2, -1, -1):
            total = add(lax.ppermute(total, "expert", h_down), parts[k])
        return total

    def square_rows(v):
        mine, other = pick(v.reshape(tok_rows, 2, 2 * quarter_d), c, 1)
        v = jnp.concatenate([mine, c_swap(other)], axis=0)
        mine, other = pick(v.reshape(2 * tok_rows, 2, quarter_d), y, 1)
        received = y_swap(other)
        parts = [mine[:tok_rows], received[:tok_rows], mine[tok_rows:], received[tok_rows:]]
        return jnp.concatenate(parts, axis=0)

    def square_weight(v):
        mine, other = pick(v.reshape(2, 2, quarter_d, shard), y, 1)
        v = flip(jnp.concatenate([mine, y_swap(other)], axis=2), y, 2)
        mine, other = pick(v, c, 0)
        block = flip(jnp.concatenate([mine, c_swap(other)], axis=1), c, 1)
        if not shared:
            return gather_h(block)
        mine, _ = pick(block.reshape(2, quarter_d // 2, 4 * shard), g, 0)
        parts = [block]
        for _ in range(nh - 1):
            mine = lax.ppermute(mine, "expert", h_up)
            parts.append(flip(jnp.concatenate([mine, g_swap(mine)], axis=0), g, 0))
        return parts

    def project(rows, weights):
        part = jnp.concatenate([dot(rows, w).astype(bf16) for w in weights], axis=1)
        mine, other = pick(part.reshape(2, 2, 2, half_rows, latent), t, 2)
        part = add(mine, t_swap(other))
        part = add(part[0], c_swap(part[1]))
        part = add(part[0], y_swap(part[1]))
        return turn(part, 1)

    def gather_first(part):
        part = jnp.stack(gather_h(part))
        part = jnp.stack([part, c_swap(part)])
        part = jnp.stack([part, y_swap(part)])
        part = jnp.stack([part, t_swap(part)])
        return part.reshape(-1, latent)

    def gather_second(part):
        part = jnp.stack([part, y_swap(part)])
        part = jnp.stack(gather_h(part), axis=1)
        part = jnp.stack([part, c_swap(part)], axis=1)
        part = jnp.stack([part, t_swap(part)])
        return part.reshape(-1, latent)

    def collect(part):
        part = part.reshape(2, 2, 2, nh, half_rows, latent)
        part = add(part[0], t_swap(part[1]))
        part = add(part[0], y_swap(part[1]))
        part = add(part[0], c_swap(part[1]))
        part = turn(scatter_h([part[k] for k in range(nh)]), 1)
        part = jnp.stack([part, y_swap(part)])
        part = jnp.stack([part, c_swap(part)])
        part = flip(jnp.stack([part, t_swap(part)], axis=2), t, 2)
        return part.reshape(4 * tok_rows, latent)

    def finish(part, rows, weights):
        cols = latent // nh
        grads = [dot(rows, part[:, k * cols : (k + 1) * cols], TN).astype(bf16) for k in range(nh)]
        grad = scatter_h(grads)
        mine, other = pick(grad.reshape(quarter_d, 2, 2 * shard), c, 1)
        grad = jnp.stack([mine, c_swap(other)])
        mine, other = pick(grad.reshape(2, quarter_d, 2, shard), y, 2)
        grad = jnp.stack([mine, y_swap(other)], axis=1)
        grad = flip(flip(grad, c, 0), y, 1).reshape(4 * quarter_d, shard).astype(f32)

        whole = sum(dot(part[:, k * cols : (k + 1) * cols], weights[k], NT) for k in range(nh))
        whole = whole.astype(bf16)
        theirs = c_swap(whole[2 * tok_rows :])
        pieces = [whole[:tok_rows], theirs[:tok_rows]]
        sent = jnp.concatenate([whole[tok_rows : 2 * tok_rows], theirs[tok_rows:]], axis=1)
        received = y_swap(sent)
        result = [
            flip(jnp.concatenate([p, r], axis=1), y, 1)
            for p, r in zip(pieces, jnp.split(received, 2, axis=1))
        ]
        return flip(jnp.concatenate(result, axis=1), c, 1), grad

    local_ids = own * exp_local + jnp.arange(exp_local, dtype=jnp.int32)
    hit = routes[:, :, None] == local_ids[None, None, :]
    gate_all = jnp.sum(jnp.where(hit, gates[:, :, None], 0), axis=1).astype(f32) * gate_unit
    gate_all = turn(gate_all.reshape(nh, 2, 2, 2, half_rows, exp_local), 0)
    gate_all = flip(flip(flip(gate_all, c, 1), y, 2), t, 3)
    gate_columns = gate_all.transpose(3, 2, 1, 0, 4, 5).reshape(-1, exp_local)

    group_rows = n_expert * tok_rows
    forward, backward, down_grads, input_grads, gate_blocks = expert_calls(
        group_rows, latent, exp_local, width
    )
    down_rows = down_proj.reshape(exp_local * width, latent)

    down_parts = square_weight(down_weight)
    up_parts = square_weight(up_weight)
    token_rows = square_rows(tokens)
    cot_rows = square_rows(cotangent)
    latent_in = gather_first(project(token_rows, down_parts))
    latent_grad = gather_second(project(cot_rows, up_parts))

    hs, cp, cu, out_part = forward(
        latent_in, gate_blocks(gate_columns), gate_proj, up_proj, down_rows
    )
    dpu, in_part = backward(latent_grad, cp, cu, gate_proj, up_proj, down_rows)
    down_proj_grad = down_grads(hs, latent_grad).reshape(down_proj.shape)
    gate_proj_grad, up_proj_grad = input_grads(latent_in, dpu)

    out, up_grad = finish(collect(out_part), cot_rows, up_parts)
    tokens_grad, down_grad = finish(collect(in_part), token_rows, down_parts)
    return (out, tokens_grad, gate_proj_grad, up_proj_grad, down_proj_grad, down_grad, up_grad)


def solution(mesh):
    in_specs = (
        P(("group", "expert"), "tensor"),
        P("tensor", "expert"),
        P("tensor", "expert"),
        P("expert", None, "tensor"),
        P("expert", None, "tensor"),
        P("expert", "tensor", None),
        P("group", None),
        P("group", None),
        P(("group", "expert"), "tensor"),
    )
    out_specs = (
        P(("group", "expert"), "tensor"),
        P(("group", "expert"), "tensor"),
        P(("group", "expert"), None, "tensor"),
        P(("group", "expert"), None, "tensor"),
        P(("group", "expert"), "tensor", None),
        P(("group", "tensor"), "expert"),
        P(("group", "tensor"), "expert"),
    )
    return jax.shard_map(local, mesh=mesh, in_specs=in_specs, out_specs=out_specs, check_vma=False)
```

```python
import jax
import jax.numpy as jnp
from jax import lax
from jax.experimental import pallas as pl
from jax.experimental.pallas import tpu as pltpu
from jax.sharding import PartitionSpec as P

gate_unit = 2.0 ** (-15)
bf16 = jnp.bfloat16
f32 = jnp.float32

NN = (((1,), (0,)), ((), ()))
NT = (((1,), (1,)), ((), ()))
TN = (((0,), (0,)), ((), ()))


def dot(a, b, dims=NN):
    return lax.dot_general(a, b, dims, preferred_element_type=f32)


def join_projections(wg_ref, wu_ref, wgu):
    pair, _, width = wg_ref.shape
    for j in range(pair):
        wgu[:, 2 * j * width : (2 * j + 1) * width] = wg_ref[j]
        wgu[:, (2 * j + 1) * width : (2 * j + 2) * width] = wu_ref[j]


def forward_kernel(
    x_ref, g_ref, wg_ref, wu_ref, wd_ref, hs_ref, cp_ref, cu_ref, lo_ref, wgu, lo_acc
):
    step = pl.program_id(0)
    pair, _, width = wg_ref.shape
    block = 256
    join_projections(wg_ref, wu_ref, wgu)

    @pl.when(step == 0)
    def _():
        lo_acc[...] = jnp.zeros_like(lo_acc)

    def row_block(i, _):
        rows = pl.ds(pl.multiple_of(i * block, block), block)
        x = x_ref[rows, :]
        for j in range(pair):
            cols = slice(j * width, (j + 1) * width)
            both = dot(x, wgu[:, 2 * j * width : (2 * j + 2) * width])
            gate_pre, up_pre = both[:, :width], both[:, width:]
            gate = g_ref[0, rows, j : j + 1]
            sig = jax.nn.sigmoid(gate_pre)
            act = gate_pre * sig * gate
            hs_ref[rows, cols] = (act * up_pre).astype(bf16)
            cu_ref[rows, cols] = act.astype(bf16)
            slope = up_pre * (sig * (1.0 + gate_pre * (1.0 - sig)))
            cp_ref[rows, cols] = (slope * gate).astype(bf16)
        lo_acc[rows, :] += dot(hs_ref[rows, :], wd_ref[...])
        return 0

    lax.fori_loop(0, x_ref.shape[0] // block, row_block, 0)

    @pl.when(step == pl.num_programs(0) - 1)
    def _():
        lo_ref[...] = lo_acc[...].astype(bf16)


def backward_kernel(
    y_ref, cp_ref, cu_ref, wg_ref, wu_ref, wd_ref, dpu_ref, lig_ref, wgu, lig_acc
):
    step = pl.program_id(0)
    pair, _, width = wg_ref.shape
    block = 256
    join_projections(wg_ref, wu_ref, wgu)

    @pl.when(step == 0)
    def _():
        lig_acc[...] = jnp.zeros_like(lig_acc)

    def row_block(i, _):
        rows = pl.ds(pl.multiple_of(i * block, block), block)
        hidden_grad = dot(y_ref[rows, :], wd_ref[...], NT)
        for j in range(pair):
            cols = slice(j * width, (j + 1) * width)
            hg = hidden_grad[:, cols]
            dp = hg * cp_ref[rows, cols].astype(f32)
            du = hg * cu_ref[rows, cols].astype(f32)
            dpu_ref[rows, 2 * j * width : (2 * j + 1) * width] = dp.astype(bf16)
            dpu_ref[rows, (2 * j + 1) * width : (2 * j + 2) * width] = du.astype(bf16)
        lig_acc[rows, :] += dot(dpu_ref[rows, :], wgu[...], NT)
        return 0

    lax.fori_loop(0, y_ref.shape[0] // block, row_block, 0)

    @pl.when(step == pl.num_programs(0) - 1)
    def _():
        lig_ref[...] = lig_acc[...].astype(bf16)


def down_grad_kernel(hs_ref, y_ref, dwd_ref):
    dwd_ref[...] = dot(hs_ref[...], y_ref[...], TN).astype(bf16)


def input_grad_kernel(x_ref, dpu_ref, dwg_ref, dwu_ref):
    pair, latent, width = dwg_ref.shape
    block = 256

    def col_block(i, _):
        cols = pl.ds(pl.multiple_of(i * block, block), block)
        grads = dot(x_ref[:, cols], dpu_ref[...], TN)
        for j in range(pair):
            dwg_ref[j, cols, :] = grads[:, 2 * j * width : (2 * j + 1) * width].astype(bf16)
            dwu_ref[j, cols, :] = grads[:, (2 * j + 1) * width : (2 * j + 2) * width].astype(bf16)
        return 0

    lax.fori_loop(0, latent // block, col_block, 0)


def shaped(*shape):
    return jax.ShapeDtypeStruct(shape, bf16)


def expert_calls(rows, latent, count, width):
    pair = 2 if rows <= 1024 and count % 2 == 0 else 1
    whole = pl.BlockSpec((rows, latent), lambda i: (0, 0))
    col_proj = pl.BlockSpec((pair, latent, width), lambda i: (i, 0, 0))
    row_proj = pl.BlockSpec((pair * width, latent), lambda i: (i, 0))
    hidden = pl.BlockSpec((rows, pair * width), lambda i: (0, i))
    hidden2 = pl.BlockSpec((rows, 2 * pair * width), lambda i: (0, i))
    gate_spec = pl.BlockSpec((1, rows, pair), lambda i: (i, 0, 0))
    joined = pltpu.VMEM((latent, 2 * pair * width), bf16)
    total = pltpu.VMEM((rows, latent), f32)
    units = 2 * rows * latent * width * count
    weight_bytes = 2 * latent * width * count
    hidden_bytes = 2 * rows * width * count
    latent_bytes = 2 * rows * latent

    def call(kernel, ins, outs, out_shape, scratch, parts, moved, exps=0):
        return pl.pallas_call(
            kernel,
            grid=(count // pair,),
            in_specs=ins,
            out_specs=outs,
            out_shape=out_shape,
            scratch_shapes=scratch,
            compiler_params=pltpu.CompilerParams(
                vmem_limit_bytes=(40 if rows <= 1024 else 56) * 1024 * 1024
            ),
            cost_estimate=pl.CostEstimate(
                flops=parts * units, bytes_accessed=moved, transcendentals=exps
            ),
        )

    hid = shaped(rows, count * width)
    lat = shaped(rows, latent)
    col = shaped(count, latent, width)
    forward = call(
        forward_kernel,
        [whole, gate_spec, col_proj, col_proj, row_proj],
        [hidden, hidden, hidden, whole],
        [hid, hid, hid, lat],
        [joined, total],
        3,
        3 * weight_bytes + 3 * hidden_bytes + 2 * latent_bytes,
        rows * width * count,
    )
    backward = call(
        backward_kernel,
        [whole, hidden, hidden, col_proj, col_proj, row_proj],
        [hidden2, whole],
        [shaped(rows, 2 * count * width), lat],
        [joined, total],
        3,
        3 * weight_bytes + 4 * hidden_bytes + 2 * latent_bytes,
    )
    down_grads = call(
        down_grad_kernel,
        [hidden, whole],
        row_proj,
        shaped(count * width, latent),
        [],
        1,
        weight_bytes + hidden_bytes + latent_bytes,
    )
    input_grads = call(
        input_grad_kernel,
        [whole, hidden2],
        [col_proj, col_proj],
        [col, col],
        [],
        2,
        2 * weight_bytes + 2 * hidden_bytes + latent_bytes,
    )

    def gate_blocks(gate_columns):
        return gate_columns.reshape(rows, count // pair, pair).transpose(1, 0, 2)

    return forward, backward, down_grads, input_grads, gate_blocks


def local(tokens, down_weight, up_weight, gate_proj, up_proj, down_proj, routes, gates, cotangent):
    n_expert = lax.axis_size("expert")
    n_group = lax.axis_size("group")
    own = lax.axis_index("expert")
    t = lax.axis_index("tensor")
    tok_rows = tokens.shape[0]
    half_rows = tok_rows // 2
    quarter_d = tokens.shape[1] // 4
    exp_local, latent, width = gate_proj.shape
    shard = down_weight.shape[1]

    nh = n_expert // 4
    h, c, y = own // 4, own // 2 % 2, own % 2
    shared = n_group % 2 == 0
    g = lax.axis_index("group") % 2

    def swapper(axis, size, bit):
        perm = [(i, i ^ bit) for i in range(size)]
        return lambda v: lax.ppermute(v, axis, perm)

    y_swap = swapper("expert", n_expert, 1)
    c_swap = swapper("expert", n_expert, 2)
    t_swap = swapper("tensor", 2, 1)
    g_swap = swapper("group", n_group, 1)
    h_up = [(e, (e + 4) % n_expert) for e in range(n_expert)]
    h_down = [((e + 4) % n_expert, e) for e in range(n_expert)]

    def add(a, b):
        return (a.astype(f32) + b.astype(f32)).astype(bf16)

    def after(v, *done):
        return lax.optimization_barrier((v, *done))[0]

    def turn(blocks):
        result = []
        for k in range(nh):
            block = blocks[-k % nh]
            for i in range(1, nh):
                block = jnp.where(h == i, blocks[(i - k) % nh], block)
            result.append(block)
        return result

    def flip(v, index, axis):
        first, second = jnp.split(v, 2, axis=axis)
        return jnp.where(index == 0, v, jnp.concatenate([second, first], axis=axis))

    def pick(v, index, axis):
        mine = lax.dynamic_index_in_dim(v, index, axis, keepdims=False)
        other = lax.dynamic_index_in_dim(v, 1 - index, axis, keepdims=False)
        return mine, other

    def pick_halves(v, index):
        size = v.shape[-1] // 2
        mine = lax.dynamic_slice_in_dim(v, index * size, size, v.ndim - 1)
        other = lax.dynamic_slice_in_dim(v, (1 - index) * size, size, v.ndim - 1)
        return mine, other

    def pick_quarters(v, index):
        pairs = [pick_halves(half, index) for half in jnp.split(v, 2, axis=-1)]
        return tuple(jnp.concatenate(p, axis=-1) for p in zip(*pairs))

    def gather_h(v):
        parts = [v]
        for _ in range(nh - 1):
            parts.append(lax.ppermute(parts[-1], "expert", h_up))
        return parts

    def scatter_h(parts):
        total = parts[nh - 1]
        for k in range(nh - 2, -1, -1):
            total = add(lax.ppermute(total, "expert", h_down), parts[k])
        return total

    def square_rows(v, y_first):
        if y_first:
            mine, other = pick_quarters(v, y)
            mine, other = pick_halves(jnp.concatenate([mine, y_swap(other)], axis=0), c)
            return jnp.concatenate([mine, c_swap(other)], axis=0)
        mine, other = pick_halves(v, c)
        mine, other = pick_halves(jnp.concatenate([mine, c_swap(other)], axis=0), y)
        received = y_swap(other)
        parts = [mine[:tok_rows], received[:tok_rows], mine[tok_rows:], received[tok_rows:]]
        return jnp.concatenate(parts, axis=0)

    def square_weight(v, y_first, wait):
        v = v.reshape(2, 2, quarter_d, shard)
        if shared:
            v, _ = pick(v.reshape(2, 2, 2, quarter_d // 2, shard), g, 2)
        if y_first:
            mine, other = pick(v, y, 1)
            v = flip(jnp.concatenate([mine, y_swap(other)], axis=2), y, 2)
            mine, other = pick(v, c, 0)
            last = c_swap(other)
            block = flip(jnp.concatenate([mine, last], axis=1), c, 1)
        else:
            mine, other = pick(v, c, 0)
            v = flip(jnp.concatenate([mine, c_swap(other)], axis=2), c, 2)
            mine, other = pick(v, y, 0)
            last = y_swap(other)
            pair = flip(jnp.concatenate([mine, last], axis=1), y, 1)
            block = jnp.concatenate(
                [pair[:, i * shard : (i + 1) * shard] for i in (0, 2, 1, 3)], axis=1
            )
        parts = gather_h(after(block, *wait))
        parts[0] = block
        arrived = parts[-1]
        if shared:
            parts = [flip(jnp.concatenate([p, g_swap(p)], axis=0), g, 0) for p in parts]
        return parts, last, arrived

    def project(rows, weights, y_first):
        blocks = []
        for k, weight in enumerate(weights):
            part = dot(rows, weight).astype(bf16).reshape(2, 2, 2, half_rows, latent // nh)
            mine, other = pick(part, t, 2)
            part = add(mine, t_swap(other))
            if k % 2 == int(y_first):
                part = add(part[0], c_swap(part[1]))
                part = add(part[0], y_swap(part[1]))
            else:
                part = add(part[:, 0], y_swap(part[:, 1]))
                part = add(part[0], c_swap(part[1]))
            blocks.append(part)
        return turn(blocks)

    def gather(blocks, y_first):
        whole = []
        for j, part in enumerate(blocks):
            part = jnp.stack(gather_h(part))
            if j % 2 == int(y_first):
                part = jnp.stack([part, c_swap(part)])
                part = jnp.stack([part, y_swap(part)])
            else:
                part = jnp.stack([part, y_swap(part)])
                part = jnp.stack([part, c_swap(part)], axis=1)
            part = jnp.stack([part, t_swap(part)])
            whole.append(part.reshape(-1, part.shape[-1]))
        return jnp.concatenate(whole, axis=1)

    def collect(part):
        part = part.reshape(2, 2, 2, nh, half_rows, latent)
        part = add(part[0], t_swap(part[1]))
        blocks = []
        for j, block in enumerate(jnp.split(part, nh, axis=-1)):
            if j % 2 == 0:
                block = add(block[0], y_swap(block[1]))
                block = add(block[0], c_swap(block[1]))
            else:
                block = add(block[:, 0], c_swap(block[:, 1]))
                block = add(block[0], y_swap(block[1]))
            blocks.append(scatter_h([block[k] for k in range(nh)]))
        whole = []
        for k, block in enumerate(turn(blocks)):
            if k % 2 == 0:
                block = jnp.stack([block, y_swap(block)])
                block = jnp.stack([block, c_swap(block)])
            else:
                block = jnp.stack([block, c_swap(block)])
                block = jnp.stack([block, y_swap(block)], axis=1)
            block = flip(jnp.stack([block, t_swap(block)], axis=2), t, 2)
            whole.append(block.reshape(4 * tok_rows, -1))
        return whole, part

    def finish(blocks, rows, weights):
        grads = [dot(rows, block, TN).astype(bf16) for block in blocks]
        first, second = jnp.split(scatter_h(grads), 2, axis=0)
        mine, other = pick_halves(first, c)
        first = jnp.stack([mine, c_swap(other)])
        mine, other = pick_halves(first, y)
        first = jnp.stack([mine, y_swap(other)], axis=1)
        mine, other = pick_quarters(second, y)
        second = jnp.stack([mine, y_swap(other)])
        mine, other = pick_halves(second, c)
        second = jnp.stack([mine, c_swap(other)])
        grad = jnp.concatenate([first, second], axis=2)
        grad = flip(flip(grad, c, 0), y, 1).reshape(4 * quarter_d, shard).astype(f32)

        whole = sum(dot(block, weight, NT) for block, weight in zip(blocks, weights))
        whole = whole.astype(bf16)
        theirs = c_swap(whole[2 * tok_rows :])
        pieces = [whole[:tok_rows], theirs[:tok_rows]]
        sent = jnp.concatenate([whole[tok_rows : 2 * tok_rows], theirs[tok_rows:]], axis=1)
        received = y_swap(sent)
        result = [
            flip(jnp.concatenate([p, r], axis=1), y, 1)
            for p, r in zip(pieces, jnp.split(received, 2, axis=1))
        ]
        return flip(jnp.concatenate(result, axis=1), c, 1), grad

    local_ids = own * exp_local + jnp.arange(exp_local, dtype=jnp.int32)
    hit = routes[:, :, None] == local_ids[None, None, :]
    gate_all = jnp.sum(jnp.where(hit, gates[:, :, None], 0), axis=1).astype(f32) * gate_unit
    gate_all = jnp.stack(turn(list(gate_all.reshape(nh, 2, 2, 2, half_rows, exp_local))))
    gate_all = flip(flip(flip(gate_all, c, 1), y, 2), t, 3)
    gate_columns = gate_all.transpose(3, 2, 1, 0, 4, 5).reshape(-1, exp_local)

    group_rows = n_expert * tok_rows
    forward, backward, down_grads, input_grads, gate_blocks = expert_calls(
        group_rows, latent, exp_local, width
    )
    down_rows = down_proj.reshape(exp_local * width, latent)

    down_parts, down_last, down_far = square_weight(down_weight, True, ())
    up_parts, up_last, _ = square_weight(up_weight, False, (down_far,))
    token_rows = square_rows(after(tokens, up_last), True)
    cot_rows = square_rows(after(cotangent, down_last), False)
    latent_in = gather(project(token_rows, down_parts, False), False)
    latent_grad = gather(project(cot_rows, up_parts, True), True)

    hs, cp, cu, out_part = forward(
        latent_in, gate_blocks(gate_columns), gate_proj, up_proj, down_rows
    )
    down_proj_grad = down_grads(hs, latent_grad)
    latent_out, out_half = collect(out_part)
    dpu, in_part = backward(
        after(latent_grad, down_proj_grad, out_half), cp, cu, gate_proj, up_proj, down_rows
    )
    down_proj_grad = down_proj_grad.reshape(down_proj.shape)
    gate_proj_grad, up_proj_grad = input_grads(latent_in, dpu)

    out, up_grad = finish(latent_out, cot_rows, up_parts)
    latent_in_grad, _ = collect(in_part)
    tokens_grad, down_grad = finish(latent_in_grad, token_rows, down_parts)
    return (out, tokens_grad, gate_proj_grad, up_proj_grad, down_proj_grad, down_grad, up_grad)


def solution(mesh):
    in_specs = (
        P(("group", "expert"), "tensor"),
        P("tensor", "expert"),
        P("tensor", "expert"),
        P("expert", None, "tensor"),
        P("expert", None, "tensor"),
        P("expert", "tensor", None),
        P("group", None),
        P("group", None),
        P(("group", "expert"), "tensor"),
    )
    out_specs = (
        P(("group", "expert"), "tensor"),
        P(("group", "expert"), "tensor"),
        P(("group", "expert"), None, "tensor"),
        P(("group", "expert"), None, "tensor"),
        P(("group", "expert"), "tensor", None),
        P(("group", "tensor"), "expert"),
        P(("group", "tensor"), "expert"),
    )
    return jax.shard_map(local, mesh=mesh, in_specs=in_specs, out_specs=out_specs, check_vma=False)
```

```python
import jax
import jax.numpy as jnp
from jax import lax
from jax.experimental import pallas as pl
from jax.experimental.pallas import tpu as pltpu
from jax.sharding import PartitionSpec as P

gate_unit = 2.0 ** (-15)
bf16 = jnp.bfloat16
f32 = jnp.float32

NN = (((1,), (0,)), ((), ()))
NT = (((1,), (1,)), ((), ()))
TN = (((0,), (0,)), ((), ()))


def dot(a, b, dims=NN):
    return lax.dot_general(a, b, dims, preferred_element_type=f32)


def join_projections(wg_ref, wu_ref, wgu):
    pair, _, width = wg_ref.shape
    for j in range(pair):
        wgu[:, 2 * j * width : (2 * j + 1) * width] = wg_ref[j]
        wgu[:, (2 * j + 1) * width : (2 * j + 2) * width] = wu_ref[j]


def forward_kernel(
    x_ref, g_ref, wg_ref, wu_ref, wd_ref, hs_ref, cp_ref, cu_ref, lo_ref, wgu, lo_acc
):
    step = pl.program_id(0)
    pair, _, width = wg_ref.shape
    block = 256
    join_projections(wg_ref, wu_ref, wgu)

    @pl.when(step == 0)
    def _():
        lo_acc[...] = jnp.zeros_like(lo_acc)

    def row_block(i, _):
        rows = pl.ds(pl.multiple_of(i * block, block), block)
        x = x_ref[rows, :]
        for j in range(pair):
            cols = slice(j * width, (j + 1) * width)
            both = dot(x, wgu[:, 2 * j * width : (2 * j + 2) * width])
            gate_pre, up_pre = both[:, :width], both[:, width:]
            gate = g_ref[0, rows, j : j + 1]
            sig = jax.nn.sigmoid(gate_pre)
            act = gate_pre * sig * gate
            hs_ref[rows, cols] = (act * up_pre).astype(bf16)
            cu_ref[rows, cols] = act.astype(bf16)
            slope = up_pre * (sig * (1.0 + gate_pre * (1.0 - sig)))
            cp_ref[rows, cols] = (slope * gate).astype(bf16)
        lo_acc[rows, :] += dot(hs_ref[rows, :], wd_ref[...])
        return 0

    lax.fori_loop(0, x_ref.shape[0] // block, row_block, 0)

    @pl.when(step == pl.num_programs(0) - 1)
    def _():
        lo_ref[...] = lo_acc[...].astype(bf16)


def backward_kernel(
    y_ref, cp_ref, cu_ref, wg_ref, wu_ref, wd_ref, dpu_ref, lig_ref, wgu, lig_acc
):
    step = pl.program_id(0)
    pair, _, width = wg_ref.shape
    block = 256
    join_projections(wg_ref, wu_ref, wgu)

    @pl.when(step == 0)
    def _():
        lig_acc[...] = jnp.zeros_like(lig_acc)

    def row_block(i, _):
        rows = pl.ds(pl.multiple_of(i * block, block), block)
        hidden_grad = dot(y_ref[rows, :], wd_ref[...], NT)
        for j in range(pair):
            cols = slice(j * width, (j + 1) * width)
            hg = hidden_grad[:, cols]
            dp = hg * cp_ref[rows, cols].astype(f32)
            du = hg * cu_ref[rows, cols].astype(f32)
            dpu_ref[rows, 2 * j * width : (2 * j + 1) * width] = dp.astype(bf16)
            dpu_ref[rows, (2 * j + 1) * width : (2 * j + 2) * width] = du.astype(bf16)
        lig_acc[rows, :] += dot(dpu_ref[rows, :], wgu[...], NT)
        return 0

    lax.fori_loop(0, y_ref.shape[0] // block, row_block, 0)

    @pl.when(step == pl.num_programs(0) - 1)
    def _():
        lig_ref[...] = lig_acc[...].astype(bf16)


def down_grad_kernel(hs_ref, y_ref, dwd_ref):
    dwd_ref[...] = dot(hs_ref[...], y_ref[...], TN).astype(bf16)


def input_grad_kernel(x_ref, dpu_ref, dwg_ref, dwu_ref):
    pair, latent, width = dwg_ref.shape
    block = 256

    def col_block(i, _):
        cols = pl.ds(pl.multiple_of(i * block, block), block)
        grads = dot(x_ref[:, cols], dpu_ref[...], TN)
        for j in range(pair):
            dwg_ref[j, cols, :] = grads[:, 2 * j * width : (2 * j + 1) * width].astype(bf16)
            dwu_ref[j, cols, :] = grads[:, (2 * j + 1) * width : (2 * j + 2) * width].astype(bf16)
        return 0

    lax.fori_loop(0, latent // block, col_block, 0)


def shaped(*shape):
    return jax.ShapeDtypeStruct(shape, bf16)


def expert_calls(rows, latent, count, width):
    pair = 2 if rows <= 1024 and count % 2 == 0 else 1
    whole = pl.BlockSpec((rows, latent), lambda i: (0, 0))
    col_proj = pl.BlockSpec((pair, latent, width), lambda i: (i, 0, 0))
    row_proj = pl.BlockSpec((pair * width, latent), lambda i: (i, 0))
    hidden = pl.BlockSpec((rows, pair * width), lambda i: (0, i))
    hidden2 = pl.BlockSpec((rows, 2 * pair * width), lambda i: (0, i))
    gate_spec = pl.BlockSpec((1, rows, pair), lambda i: (i, 0, 0))
    joined = pltpu.VMEM((latent, 2 * pair * width), bf16)
    total = pltpu.VMEM((rows, latent), f32)
    units = 2 * rows * latent * width * count
    weight_bytes = 2 * latent * width * count
    hidden_bytes = 2 * rows * width * count
    latent_bytes = 2 * rows * latent

    def call(kernel, ins, outs, out_shape, scratch, parts, moved, exps=0):
        return pl.pallas_call(
            kernel,
            grid=(count // pair,),
            in_specs=ins,
            out_specs=outs,
            out_shape=out_shape,
            scratch_shapes=scratch,
            compiler_params=pltpu.CompilerParams(
                vmem_limit_bytes=(40 if rows <= 1024 else 56) * 1024 * 1024
            ),
            cost_estimate=pl.CostEstimate(
                flops=parts * units, bytes_accessed=moved, transcendentals=exps
            ),
        )

    hid = shaped(rows, count * width)
    lat = shaped(rows, latent)
    col = shaped(count, latent, width)
    forward = call(
        forward_kernel,
        [whole, gate_spec, col_proj, col_proj, row_proj],
        [hidden, hidden, hidden, whole],
        [hid, hid, hid, lat],
        [joined, total],
        3,
        3 * weight_bytes + 3 * hidden_bytes + 2 * latent_bytes,
        rows * width * count,
    )
    backward = call(
        backward_kernel,
        [whole, hidden, hidden, col_proj, col_proj, row_proj],
        [hidden2, whole],
        [shaped(rows, 2 * count * width), lat],
        [joined, total],
        3,
        3 * weight_bytes + 4 * hidden_bytes + 2 * latent_bytes,
    )
    down_grads = call(
        down_grad_kernel,
        [hidden, whole],
        row_proj,
        shaped(count * width, latent),
        [],
        1,
        weight_bytes + hidden_bytes + latent_bytes,
    )
    input_grads = call(
        input_grad_kernel,
        [whole, hidden2],
        [col_proj, col_proj],
        [col, col],
        [],
        2,
        2 * weight_bytes + 2 * hidden_bytes + latent_bytes,
    )

    def gate_blocks(gate_columns):
        return gate_columns.reshape(rows, count // pair, pair).transpose(1, 0, 2)

    return forward, backward, down_grads, input_grads, gate_blocks


def local(tokens, down_weight, up_weight, gate_proj, up_proj, down_proj, routes, gates, cotangent):
    n_expert = lax.axis_size("expert")
    n_group = lax.axis_size("group")
    own = lax.axis_index("expert")
    t = lax.axis_index("tensor")
    tok_rows = tokens.shape[0]
    half_rows = tok_rows // 2
    quarter_d = tokens.shape[1] // 4
    exp_local, latent, width = gate_proj.shape
    shard = down_weight.shape[1]

    nh = n_expert // 4
    h, q = own // 4, own % 4
    cols = latent // nh
    shared = n_group % 2 == 0
    g = lax.axis_index("group") % 2

    def to_peer(v, r):
        return lax.ppermute(v, "expert", [(e, e ^ r) for e in range(n_expert)])

    def t_swap(v):
        return lax.ppermute(v, "tensor", [(0, 1), (1, 0)])

    def g_swap(v):
        return lax.ppermute(v, "group", [(i, i ^ 1) for i in range(n_group)])

    def up(v):
        return lax.ppermute(v, "expert", [(e, (e + 4) % n_expert) for e in range(n_expert)])

    def down(v):
        return lax.ppermute(v, "expert", [((e + 4) % n_expert, e) for e in range(n_expert)])

    def add(*terms):
        return sum(v.astype(f32) for v in terms).astype(bf16)

    def after(v, *done):
        return lax.optimization_barrier((v, *done))[0]

    def turn(blocks):
        result = []
        for k in range(nh):
            block = blocks[-k % nh]
            for i in range(1, nh):
                block = jnp.where(h == i, blocks[(i - k) % nh], block)
            result.append(block)
        return result

    def by_quarter(parts):
        low = [jnp.where(q % 2 == 0, parts[i], parts[i ^ 1]) for i in range(4)]
        return [jnp.where(q < 2, low[i], low[i ^ 2]) for i in range(4)]

    def flip(v, index, axis):
        first, second = jnp.split(v, 2, axis=axis)
        return jnp.where(index == 0, v, jnp.concatenate([second, first], axis=axis))

    def exchange(block_for):
        return [block_for(0)] + [to_peer(block_for(r), r) for r in (1, 2, 3)]

    def together(*values):
        return lax.optimization_barrier(values)

    def gather_h(v):
        parts = [v]
        for _ in range(nh - 1):
            parts.append(up(parts[-1]))
        return parts

    def square_rows(v):
        parts = exchange(
            lambda r: lax.dynamic_slice_in_dim(v, (q ^ r) * quarter_d, quarter_d, 1)
        )
        return jnp.concatenate(parts, axis=0)

    def square_weight(v):
        size = quarter_d // 2 if shared else quarter_d
        first = g * size if shared else 0
        parts = exchange(
            lambda r: lax.dynamic_slice_in_dim(v, (q ^ r) * quarter_d + first, size, 0)
        )
        return jnp.concatenate(by_quarter(parts), axis=1), parts[3]

    def all_features(v):
        return flip(jnp.concatenate([v, g_swap(v)], axis=0), g, 0) if shared else v

    def project(rows, weights):
        blocks = []
        for weight in weights:
            part = dot(rows, weight).astype(bf16).reshape(4, 2, half_rows, cols)
            mine = lax.dynamic_index_in_dim(part, t, 1, keepdims=False)
            other = lax.dynamic_index_in_dim(part, 1 - t, 1, keepdims=False)
            part = add(mine, t_swap(other))
            blocks.append(add(*exchange(lambda r: part[r])))
        return jnp.concatenate(turn(blocks), axis=1)

    def all_rows(part):
        return jnp.stack([part, t_swap(part)]).reshape(-1, latent)

    def sum_tensor(part):
        part = part.reshape(2, 4, nh, half_rows, latent)
        return add(part[0], t_swap(part[1]))

    def sum_squares(part):
        if nh == 2:
            return part, up(part)
        total = part[nh - 1]
        for k in range(nh - 2, -1, -1):
            total = add(down(total), part[k])
        return part, jnp.stack(gather_h(total))

    def join_squares(part, theirs):
        rows = [add(part[0], theirs[1]), add(part[1], theirs[0])] if nh == 2 else list(theirs)
        split = [turn(jnp.split(v, nh, axis=1)) for v in rows]
        return jnp.concatenate(split[0] + [v[0] for v in split[1:]], axis=1)

    def square_blocks(part):
        part = flip(jnp.stack([part, t_swap(part)], axis=1), t, 1)
        return jnp.split(part.reshape(4 * tok_rows, -1), 2 * nh - 1, axis=1)

    def products(blocks, rows, weights):
        grad = sum(dot(v, block, TN) for v, block in zip(rows, blocks[:1] + blocks[nh:]))
        whole = sum(dot(block, weight, NT) for block, weight in zip(blocks, weights))
        return grad.astype(bf16), whole.astype(bf16)

    def send_products(grad, whole):
        whole = whole.reshape(4, tok_rows, quarter_d)
        grads = exchange(lambda r: lax.dynamic_slice_in_dim(grad, (q ^ r) * shard, shard, 1))
        return grads, exchange(lambda r: whole[r])

    def join_products(grads, wholes):
        grad = jnp.concatenate(by_quarter(grads), axis=0).astype(f32)
        return jnp.concatenate(by_quarter(wholes), axis=1), grad

    local_ids = own * exp_local + jnp.arange(exp_local, dtype=jnp.int32)
    hit = routes[:, :, None] == local_ids[None, None, :]
    gate_all = jnp.sum(jnp.where(hit, gates[:, :, None], 0), axis=1).astype(f32) * gate_unit
    gate_all = gate_all.reshape(nh, 4, 2, half_rows, exp_local)
    gate_all = jnp.stack(turn(list(gate_all)))
    gate_all = jnp.stack(by_quarter([gate_all[:, i] for i in range(4)]))
    gate_all = flip(gate_all, t, 2)
    gate_columns = gate_all.transpose(2, 0, 1, 3, 4).reshape(-1, exp_local)

    group_rows = n_expert * tok_rows
    forward, backward, down_grads, input_grads, gate_blocks = expert_calls(
        group_rows, latent, exp_local, width
    )
    down_rows = down_proj.reshape(exp_local * width, latent)

    down_block, down_last = square_weight(down_weight)
    up_block, up_last = square_weight(up_weight)
    token_rows = square_rows(after(tokens, down_last, up_last))
    cot_rows = square_rows(after(cotangent, down_last, up_last))
    down_parts = gather_h(down_block)
    up_parts = gather_h(after(up_block, down_parts[-1]))
    down_parts = [all_features(v) for v in down_parts]
    up_parts = [all_features(v) for v in up_parts]

    part_x = jnp.stack(gather_h(project(token_rows, down_parts)))
    part_x = jnp.stack(exchange(lambda r: part_x))
    part_y = jnp.stack(gather_h(project(cot_rows, up_parts)))
    latent_in = all_rows(after(part_x, part_y))
    token_parts = gather_h(after(token_rows, part_x))

    hs, cp, cu, out_part = forward(
        latent_in, gate_blocks(gate_columns), gate_proj, up_proj, down_rows
    )
    part_y = exchange(lambda r: part_y)
    *part_y, token_parts[-1], out_part = together(*part_y, token_parts[-1], out_part)
    latent_grad = all_rows(jnp.stack(part_y))
    cot_parts = gather_h(after(cot_rows, token_parts[-1]))
    out_part = sum_tensor(out_part)
    down_proj_grad = down_grads(hs, latent_grad)
    out_part = after(out_part, down_proj_grad)
    dpu, in_part = backward(
        after(latent_grad, out_part), cp, cu, gate_proj, up_proj, down_rows
    )
    out_part = exchange(lambda r: out_part[r])
    *out_part, cot_parts[-1], in_part = together(*out_part, cot_parts[-1], in_part)
    out_part = add(*out_part)
    in_part = sum_tensor(after(in_part, out_part))
    gate_proj_grad, up_proj_grad = input_grads(latent_in, after(dpu, in_part))
    in_part = exchange(lambda r: in_part[r])
    *in_part, out_theirs, gate_proj_grad = together(
        *in_part, sum_squares(out_part)[1], gate_proj_grad
    )
    out_part = join_squares(out_part, out_theirs)
    in_part, in_theirs = sum_squares(add(*in_part))
    out_part = exchange(lambda r: out_part)
    *out_part, in_theirs = together(*out_part, in_theirs)
    out_part = jnp.stack(out_part)
    in_part = join_squares(in_part, in_theirs)
    in_part = jnp.stack(exchange(lambda r: in_part))
    out_sent = send_products(*products(square_blocks(out_part), cot_parts, up_parts))
    in_products = products(square_blocks(in_part), token_parts, down_parts)
    received = together(*out_sent[0], *out_sent[1], *in_products)
    out, up_grad = join_products(received[:4], received[4:8])
    tokens_grad, down_grad = join_products(*send_products(*in_products))
    down_proj_grad = down_proj_grad.reshape(down_proj.shape)
    return (out, tokens_grad, gate_proj_grad, up_proj_grad, down_proj_grad, down_grad, up_grad)


def solution(mesh):
    in_specs = (
        P(("group", "expert"), "tensor"),
        P("tensor", "expert"),
        P("tensor", "expert"),
        P("expert", None, "tensor"),
        P("expert", None, "tensor"),
        P("expert", "tensor", None),
        P("group", None),
        P("group", None),
        P(("group", "expert"), "tensor"),
    )
    out_specs = (
        P(("group", "expert"), "tensor"),
        P(("group", "expert"), "tensor"),
        P(("group", "expert"), None, "tensor"),
        P(("group", "expert"), None, "tensor"),
        P(("group", "expert"), "tensor", None),
        P(("group", "tensor"), "expert"),
        P(("group", "tensor"), "expert"),
    )
    return jax.shard_map(local, mesh=mesh, in_specs=in_specs, out_specs=out_specs, check_vma=False)
```

```python
import jax
import jax.numpy as jnp
from jax import lax
from jax.experimental import pallas as pl
from jax.experimental.pallas import tpu as pltpu
from jax.sharding import PartitionSpec as P

gate_unit = 2.0 ** (-15)
bf16 = jnp.bfloat16
f32 = jnp.float32

NN = (((1,), (0,)), ((), ()))
NT = (((1,), (1,)), ((), ()))
TN = (((0,), (0,)), ((), ()))


def dot(a, b, dims=NN):
    return lax.dot_general(a, b, dims, preferred_element_type=f32)


def join_projections(wg_ref, wu_ref, wgu):
    pair, _, width = wg_ref.shape
    for j in range(pair):
        wgu[:, 2 * j * width : (2 * j + 1) * width] = wg_ref[j]
        wgu[:, (2 * j + 1) * width : (2 * j + 2) * width] = wu_ref[j]


def forward_kernel(
    x_ref, g_ref, wg_ref, wu_ref, wd_ref, hs_ref, cp_ref, cu_ref, lo_ref, wgu, lo_acc
):
    step = pl.program_id(0)
    pair, _, width = wg_ref.shape
    block = 256
    join_projections(wg_ref, wu_ref, wgu)

    @pl.when(step == 0)
    def _():
        lo_acc[...] = jnp.zeros_like(lo_acc)

    for i in range(x_ref.shape[0] // block):
        rows = slice(i * block, (i + 1) * block)
        x = x_ref[rows, :]
        for j in range(pair):
            cols = slice(j * width, (j + 1) * width)
            both = dot(x, wgu[:, 2 * j * width : (2 * j + 2) * width])
            gate_pre, up_pre = both[:, :width], both[:, width:]
            gate = g_ref[0, rows, j : j + 1]
            sig = jax.nn.sigmoid(gate_pre)
            act = gate_pre * sig * gate
            hs_ref[rows, cols] = (act * up_pre).astype(bf16)
            cu_ref[rows, cols] = act.astype(bf16)
            slope = up_pre * (sig * (1.0 + gate_pre * (1.0 - sig)))
            cp_ref[rows, cols] = (slope * gate).astype(bf16)
        lo_acc[rows, :] += dot(hs_ref[rows, :], wd_ref[...])

    @pl.when(step == pl.num_programs(0) - 1)
    def _():
        lo_ref[...] = lo_acc[...].astype(bf16)


def backward_kernel(
    y_ref, cp_ref, cu_ref, wg_ref, wu_ref, wd_ref, dpu_ref, lig_ref, wgu, lig_acc
):
    step = pl.program_id(0)
    pair, _, width = wg_ref.shape
    block = 256
    join_projections(wg_ref, wu_ref, wgu)

    @pl.when(step == 0)
    def _():
        lig_acc[...] = jnp.zeros_like(lig_acc)

    for i in range(y_ref.shape[0] // block):
        rows = slice(i * block, (i + 1) * block)
        hidden_grad = dot(y_ref[rows, :], wd_ref[...], NT)
        for j in range(pair):
            cols = slice(j * width, (j + 1) * width)
            hg = hidden_grad[:, cols]
            dp = hg * cp_ref[rows, cols].astype(f32)
            du = hg * cu_ref[rows, cols].astype(f32)
            dpu_ref[rows, 2 * j * width : (2 * j + 1) * width] = dp.astype(bf16)
            dpu_ref[rows, (2 * j + 1) * width : (2 * j + 2) * width] = du.astype(bf16)
        lig_acc[rows, :] += dot(dpu_ref[rows, :], wgu[...], NT)

    @pl.when(step == pl.num_programs(0) - 1)
    def _():
        lig_ref[...] = lig_acc[...].astype(bf16)


def down_grad_kernel(hs_ref, y_ref, dwd_ref):
    dwd_ref[...] = dot(hs_ref[...], y_ref[...], TN).astype(bf16)


def input_grad_kernel(x_ref, dpu_ref, dwg_ref, dwu_ref):
    pair, latent, width = dwg_ref.shape
    block = 256

    for i in range(latent // block):
        cols = slice(i * block, (i + 1) * block)
        grads = dot(x_ref[:, cols], dpu_ref[...], TN)
        for j in range(pair):
            dwg_ref[j, cols, :] = grads[:, 2 * j * width : (2 * j + 1) * width].astype(bf16)
            dwu_ref[j, cols, :] = grads[:, (2 * j + 1) * width : (2 * j + 2) * width].astype(bf16)


def shaped(*shape):
    return jax.ShapeDtypeStruct(shape, bf16)


def expert_calls(rows, latent, count, width):
    pair = 2 if rows <= 1024 and count % 2 == 0 else 1
    whole = pl.BlockSpec((rows, latent), lambda i: (0, 0))
    col_proj = pl.BlockSpec((pair, latent, width), lambda i: (i, 0, 0))
    row_proj = pl.BlockSpec((pair * width, latent), lambda i: (i, 0))
    hidden = pl.BlockSpec((rows, pair * width), lambda i: (0, i))
    hidden2 = pl.BlockSpec((rows, 2 * pair * width), lambda i: (0, i))
    gate_spec = pl.BlockSpec((1, rows, pair), lambda i: (i, 0, 0))
    joined = pltpu.VMEM((latent, 2 * pair * width), bf16)
    total = pltpu.VMEM((rows, latent), f32)
    units = 2 * rows * latent * width * count
    weight_bytes = 2 * latent * width * count
    hidden_bytes = 2 * rows * width * count
    latent_bytes = 2 * rows * latent

    def call(kernel, ins, outs, out_shape, scratch, parts, moved, exps=0):
        return pl.pallas_call(
            kernel,
            grid=(count // pair,),
            in_specs=ins,
            out_specs=outs,
            out_shape=out_shape,
            scratch_shapes=scratch,
            compiler_params=pltpu.CompilerParams(
                vmem_limit_bytes=(40 if rows <= 1024 else 56) * 1024 * 1024
            ),
            cost_estimate=pl.CostEstimate(
                flops=parts * units, bytes_accessed=moved, transcendentals=exps
            ),
        )

    hid = shaped(rows, count * width)
    lat = shaped(rows, latent)
    col = shaped(count, latent, width)
    forward = call(
        forward_kernel,
        [whole, gate_spec, col_proj, col_proj, row_proj],
        [hidden, hidden, hidden, whole],
        [hid, hid, hid, lat],
        [joined, total],
        3,
        3 * weight_bytes + 3 * hidden_bytes + 2 * latent_bytes,
        rows * width * count,
    )
    backward = call(
        backward_kernel,
        [whole, hidden, hidden, col_proj, col_proj, row_proj],
        [hidden2, whole],
        [shaped(rows, 2 * count * width), lat],
        [joined, total],
        3,
        3 * weight_bytes + 4 * hidden_bytes + 2 * latent_bytes,
    )
    down_grads = call(
        down_grad_kernel,
        [hidden, whole],
        row_proj,
        shaped(count * width, latent),
        [],
        1,
        weight_bytes + hidden_bytes + latent_bytes,
    )
    input_grads = call(
        input_grad_kernel,
        [whole, hidden2],
        [col_proj, col_proj],
        [col, col],
        [],
        2,
        2 * weight_bytes + 2 * hidden_bytes + latent_bytes,
    )

    def gate_blocks(gate_columns):
        return gate_columns.reshape(rows, count // pair, pair).transpose(1, 0, 2)

    return forward, backward, down_grads, input_grads, gate_blocks


def local(tokens, down_weight, up_weight, gate_proj, up_proj, down_proj, routes, gates, cotangent):
    n_expert = lax.axis_size("expert")
    n_group = lax.axis_size("group")
    own = lax.axis_index("expert")
    t = lax.axis_index("tensor")
    tok_rows = tokens.shape[0]
    half_rows = tok_rows // 2
    quarter_d = tokens.shape[1] // 4
    exp_local, latent, width = gate_proj.shape
    shard = down_weight.shape[1]

    nh = n_expert // 4
    h, q = own // 4, own % 4
    cols = latent // nh
    shared = n_group % 2 == 0
    g = lax.axis_index("group") % 2

    def to_peer(v, r):
        return lax.ppermute(v, "expert", [(e, e ^ r) for e in range(n_expert)])

    def t_swap(v):
        return lax.ppermute(v, "tensor", [(0, 1), (1, 0)])

    def g_swap(v):
        return lax.ppermute(v, "group", [(i, i ^ 1) for i in range(n_group)])

    def up(v):
        return lax.ppermute(v, "expert", [(e, (e + 4) % n_expert) for e in range(n_expert)])

    def down(v):
        return lax.ppermute(v, "expert", [((e + 4) % n_expert, e) for e in range(n_expert)])

    def add(*terms):
        return sum(v.astype(f32) for v in terms).astype(bf16)

    def after(v, *done):
        return lax.optimization_barrier((v, *done))[0]

    def turn(blocks):
        result = []
        for k in range(nh):
            block = blocks[-k % nh]
            for i in range(1, nh):
                block = jnp.where(h == i, blocks[(i - k) % nh], block)
            result.append(block)
        return result

    def by_quarter(parts):
        low = [jnp.where(q % 2 == 0, parts[i], parts[i ^ 1]) for i in range(4)]
        return [jnp.where(q < 2, low[i], low[i ^ 2]) for i in range(4)]

    def flip(v, index, axis):
        first, second = jnp.split(v, 2, axis=axis)
        return jnp.where(index == 0, v, jnp.concatenate([second, first], axis=axis))

    def exchange(block_for):
        return [block_for(0)] + [to_peer(block_for(r), r) for r in (1, 2, 3)]

    def together(*values):
        return lax.optimization_barrier(values)

    def gather_h(v):
        parts = [v]
        for _ in range(nh - 1):
            parts.append(up(parts[-1]))
        return parts

    def square_rows(v):
        return exchange(
            lambda r: lax.dynamic_slice_in_dim(v, (q ^ r) * quarter_d, quarter_d, 1)
        )

    def first_rows(v):
        size = 2 * quarter_d
        mine = lax.dynamic_slice_in_dim(v, q // 2 * size, size, 1)
        other = lax.dynamic_slice_in_dim(v, (1 - q // 2) * size, size, 1)
        return jnp.concatenate([mine, to_peer(other, 2)], axis=0)

    def second_rows(v):
        mine = lax.dynamic_slice_in_dim(v, q % 2 * quarter_d, quarter_d, 1)
        other = lax.dynamic_slice_in_dim(v, (1 - q % 2) * quarter_d, quarter_d, 1)
        return mine, to_peer(other, 1)

    def square_weight(v):
        size = quarter_d // 2 if shared else quarter_d
        first = g * size if shared else 0
        parts = exchange(
            lambda r: lax.dynamic_slice_in_dim(v, (q ^ r) * quarter_d + first, size, 0)
        )
        return parts

    def join_quarters(parts):
        return jnp.concatenate(by_quarter(parts), axis=1)

    def swap_features(v):
        return g_swap(v) if shared else v

    def all_features(v, theirs):
        return flip(jnp.concatenate([v, theirs], axis=0), g, 0) if shared else v

    def project(rows, weights):
        parts = [dot(rows, weight).astype(bf16) for weight in weights]
        part = jnp.concatenate(parts, axis=1).reshape(4, 2, half_rows, latent)
        mine = lax.dynamic_index_in_dim(part, t, 1, keepdims=False)
        return mine, lax.dynamic_index_in_dim(part, 1 - t, 1, keepdims=False)

    def own_latent(parts):
        return jnp.concatenate(turn(jnp.split(add(*parts), nh, axis=1)), axis=1)

    def sum_tensor(part):
        part = part.reshape(2, 4, nh, half_rows, latent)
        return add(part[0], t_swap(part[1]))

    def sum_squares(part):
        if nh == 2:
            return part, up(part)
        total = part[nh - 1]
        for k in range(nh - 2, -1, -1):
            total = add(down(total), part[k])
        return part, jnp.stack(gather_h(total))

    def join_squares(part, theirs):
        rows = [add(part[0], theirs[1]), add(part[1], theirs[0])] if nh == 2 else list(theirs)
        split = [turn(jnp.split(v, nh, axis=1)) for v in rows]
        return jnp.concatenate(split[0] + [v[0] for v in split[1:]], axis=1)

    def square_blocks(part):
        part = flip(jnp.stack([part, t_swap(part)], axis=1), t, 1)
        return jnp.split(part.reshape(4 * tok_rows, -1), 2 * nh - 1, axis=1)

    def products(blocks, rows, weights):
        grad = sum(dot(v, block, TN) for v, block in zip(rows, blocks[:1] + blocks[nh:]))
        whole = sum(dot(block, weight, NT) for block, weight in zip(blocks, weights))
        return grad.astype(bf16), whole.astype(bf16)

    def send_products(grad, whole):
        whole = whole.reshape(4, tok_rows, quarter_d)
        grads = exchange(lambda r: lax.dynamic_slice_in_dim(grad, (q ^ r) * shard, shard, 1))
        return grads, exchange(lambda r: whole[r])

    def join_products(grads, wholes):
        grad = jnp.concatenate(by_quarter(grads), axis=0).astype(f32)
        return jnp.concatenate(by_quarter(wholes), axis=1), grad

    local_ids = own * exp_local + jnp.arange(exp_local, dtype=jnp.int32)
    hit = routes[:, :, None] == local_ids[None, None, :]
    gate_all = jnp.sum(jnp.where(hit, gates[:, :, None], 0), axis=1).astype(f32) * gate_unit
    gate_all = gate_all.reshape(nh, 4, 2, half_rows, exp_local)
    gate_all = jnp.stack(turn(list(gate_all)))
    gate_all = jnp.stack(by_quarter([gate_all[:, i] for i in range(4)]))
    gate_all = flip(gate_all, t, 2)
    gate_columns = gate_all.transpose(2, 0, 1, 3, 4).reshape(-1, exp_local)

    group_rows = n_expert * tok_rows
    forward, backward, down_grads, input_grads, gate_blocks = expert_calls(
        group_rows, latent, exp_local, width
    )
    down_rows = down_proj.reshape(exp_local * width, latent)

    def rows_with(part, theirs):
        return jnp.stack([part, theirs]).reshape(-1, latent)

    down_parts = gather_h(join_quarters(square_weight(down_weight)))
    up_block = square_weight(up_weight)
    theirs = [swap_features(down_parts[0])]
    *up_block, down_parts[-1], theirs[0] = together(*up_block, down_parts[-1], theirs[0])
    up_parts = gather_h(join_quarters(up_block))
    token_rows = square_rows(after(tokens, down_parts[-1]))
    theirs += [swap_features(v) for v in down_parts[1:]]
    *token_rows, theirs[-1], up_parts[-1] = together(*token_rows, theirs[-1], up_parts[-1])
    cot_rows = first_rows(after(cotangent, token_rows[-1]))
    token_rows = jnp.concatenate(token_rows, axis=0)
    down_parts = [all_features(v, w) for v, w in zip(down_parts, theirs)]

    mine, other = project(token_rows, down_parts)
    theirs = [swap_features(v) for v in up_parts]
    part_x = add(mine, t_swap(other))
    cot_rows = after(cot_rows, part_x)
    part_x = exchange(lambda r: part_x[r])
    mine, other = second_rows(cot_rows)
    *part_x, other, theirs[-1] = together(*part_x, other, theirs[-1])
    cot_rows = [v[i * tok_rows : (i + 1) * tok_rows] for i in (0, 1) for v in (mine, other)]
    cot_rows = jnp.concatenate(cot_rows, axis=0)
    part_x = gather_h(own_latent(part_x))
    up_parts = [all_features(v, w) for v, w in zip(up_parts, theirs)]
    mine, other = project(cot_rows, up_parts)
    *part_x, other = together(*part_x, t_swap(other))
    part_y = add(mine, other)
    part_x = jnp.stack(part_x)
    part_x = exchange(lambda r: part_x)
    part_y = exchange(lambda r: part_y[r])
    *part_x, part_y[1], part_y[2], part_y[3] = together(*part_x, *part_y[1:])
    part_x = jnp.stack(part_x)
    part_y = gather_h(own_latent(part_y))
    *part_y, other = together(*part_y, t_swap(part_x))
    part_y = jnp.stack(part_y)
    latent_in = rows_with(part_x, other)
    token_parts = gather_h(after(token_rows, other))

    hs, cp, cu, out_part = forward(
        latent_in, gate_blocks(gate_columns), gate_proj, up_proj, down_rows
    )
    part_y = exchange(lambda r: part_y)
    *part_y, token_parts[-1], out_part = together(*part_y, token_parts[-1], out_part)
    part_y = jnp.stack(part_y)
    latent_grad = rows_with(part_y, t_swap(part_y))
    cot_parts = gather_h(after(cot_rows, token_parts[-1]))
    out_part = sum_tensor(out_part)
    down_proj_grad = down_grads(hs, latent_grad)
    out_part = after(out_part, down_proj_grad)
    dpu, in_part = backward(
        after(latent_grad, out_part), cp, cu, gate_proj, up_proj, down_rows
    )
    out_part = exchange(lambda r: out_part[r])
    *out_part, cot_parts[-1], in_part = together(*out_part, cot_parts[-1], in_part)
    out_part = add(*out_part)
    in_part = sum_tensor(after(in_part, out_part))
    gate_proj_grad, up_proj_grad = input_grads(latent_in, after(dpu, in_part))
    in_part = exchange(lambda r: in_part[r])
    *in_part, out_theirs, gate_proj_grad = together(
        *in_part, sum_squares(out_part)[1], gate_proj_grad
    )
    out_part = join_squares(out_part, out_theirs)
    in_part, in_theirs = sum_squares(add(*in_part))
    out_part = exchange(lambda r: out_part)
    *out_part, in_theirs = together(*out_part, in_theirs)
    out_part = jnp.stack(out_part)
    in_part = join_squares(in_part, in_theirs)
    in_part = jnp.stack(exchange(lambda r: in_part))
    out_sent = send_products(*products(square_blocks(out_part), cot_parts, up_parts))
    in_products = products(square_blocks(in_part), token_parts, down_parts)
    received = together(*out_sent[0], *out_sent[1], *in_products)
    out, up_grad = join_products(received[:4], received[4:8])
    tokens_grad, down_grad = join_products(*send_products(*in_products))
    down_proj_grad = down_proj_grad.reshape(down_proj.shape)
    return (out, tokens_grad, gate_proj_grad, up_proj_grad, down_proj_grad, down_grad, up_grad)


def solution(mesh):
    in_specs = (
        P(("group", "expert"), "tensor"),
        P("tensor", "expert"),
        P("tensor", "expert"),
        P("expert", None, "tensor"),
        P("expert", None, "tensor"),
        P("expert", "tensor", None),
        P("group", None),
        P("group", None),
        P(("group", "expert"), "tensor"),
    )
    out_specs = (
        P(("group", "expert"), "tensor"),
        P(("group", "expert"), "tensor"),
        P(("group", "expert"), None, "tensor"),
        P(("group", "expert"), None, "tensor"),
        P(("group", "expert"), "tensor", None),
        P(("group", "tensor"), "expert"),
        P(("group", "tensor"), "expert"),
    )
    return jax.shard_map(local, mesh=mesh, in_specs=in_specs, out_specs=out_specs, check_vma=False)
```

```python
import jax
import jax.numpy as jnp
from jax import lax
from jax.experimental import pallas as pl
from jax.experimental.pallas import tpu as pltpu
from jax.sharding import PartitionSpec as P

gate_unit = 2.0 ** (-15)
bf16 = jnp.bfloat16
f32 = jnp.float32

NN = (((1,), (0,)), ((), ()))
NT = (((1,), (1,)), ((), ()))
TN = (((0,), (0,)), ((), ()))


def dot(a, b, dims=NN):
    return lax.dot_general(a, b, dims, preferred_element_type=f32)


def join_projections(wg_ref, wu_ref, wgu):
    pair, _, width = wg_ref.shape
    for j in range(pair):
        wgu[:, 2 * j * width : (2 * j + 1) * width] = wg_ref[j]
        wgu[:, (2 * j + 1) * width : (2 * j + 2) * width] = wu_ref[j]


def forward_kernel(
    x_ref, g_ref, wg_ref, wu_ref, wd_ref, hs_ref, cp_ref, cu_ref, lo_ref, wgu, lo_acc
):
    step = pl.program_id(0)
    pair, _, width = wg_ref.shape
    block = 256
    join_projections(wg_ref, wu_ref, wgu)

    @pl.when(step == 0)
    def _():
        lo_acc[...] = jnp.zeros_like(lo_acc)

    for i in range(x_ref.shape[0] // block):
        rows = slice(i * block, (i + 1) * block)
        x = x_ref[rows, :]
        for j in range(pair):
            cols = slice(j * width, (j + 1) * width)
            both = dot(x, wgu[:, 2 * j * width : (2 * j + 2) * width])
            gate_pre, up_pre = both[:, :width], both[:, width:]
            gate = g_ref[0, rows, j : j + 1]
            sig = jax.nn.sigmoid(gate_pre)
            act = gate_pre * sig * gate
            hs_ref[rows, cols] = (act * up_pre).astype(bf16)
            cu_ref[rows, cols] = act.astype(bf16)
            slope = up_pre * (sig * (1.0 + gate_pre * (1.0 - sig)))
            cp_ref[rows, cols] = (slope * gate).astype(bf16)
        lo_acc[rows, :] += dot(hs_ref[rows, :], wd_ref[...])

    @pl.when(step == pl.num_programs(0) - 1)
    def _():
        lo_ref[...] = lo_acc[...].astype(bf16)


def backward_kernel(
    y_ref, cp_ref, cu_ref, wg_ref, wu_ref, wd_ref, dpu_ref, lig_ref, wgu, lig_acc
):
    step = pl.program_id(0)
    pair, _, width = wg_ref.shape
    block = 256
    join_projections(wg_ref, wu_ref, wgu)

    @pl.when(step == 0)
    def _():
        lig_acc[...] = jnp.zeros_like(lig_acc)

    for i in range(y_ref.shape[0] // block):
        rows = slice(i * block, (i + 1) * block)
        hidden_grad = dot(y_ref[rows, :], wd_ref[...], NT)
        for j in range(pair):
            cols = slice(j * width, (j + 1) * width)
            hg = hidden_grad[:, cols]
            dp = hg * cp_ref[rows, cols].astype(f32)
            du = hg * cu_ref[rows, cols].astype(f32)
            dpu_ref[rows, 2 * j * width : (2 * j + 1) * width] = dp.astype(bf16)
            dpu_ref[rows, (2 * j + 1) * width : (2 * j + 2) * width] = du.astype(bf16)
        lig_acc[rows, :] += dot(dpu_ref[rows, :], wgu[...], NT)

    @pl.when(step == pl.num_programs(0) - 1)
    def _():
        lig_ref[...] = lig_acc[...].astype(bf16)


def down_grad_kernel(hs_ref, y_ref, dwd_ref):
    dwd_ref[...] = dot(hs_ref[...], y_ref[...], TN).astype(bf16)


def input_grad_kernel(x_ref, dpu_ref, dwg_ref, dwu_ref):
    pair, latent, width = dwg_ref.shape
    block = 256

    for i in range(latent // block):
        cols = slice(i * block, (i + 1) * block)
        grads = dot(x_ref[:, cols], dpu_ref[...], TN)
        for j in range(pair):
            dwg_ref[j, cols, :] = grads[:, 2 * j * width : (2 * j + 1) * width].astype(bf16)
            dwu_ref[j, cols, :] = grads[:, (2 * j + 1) * width : (2 * j + 2) * width].astype(bf16)


def shaped(*shape):
    return jax.ShapeDtypeStruct(shape, bf16)


def expert_calls(rows, latent, count, width):
    pair = 2 if rows <= 1024 and count % 2 == 0 else 1
    whole = pl.BlockSpec((rows, latent), lambda i: (0, 0))
    col_proj = pl.BlockSpec((pair, latent, width), lambda i: (i, 0, 0))
    row_proj = pl.BlockSpec((pair * width, latent), lambda i: (i, 0))
    hidden = pl.BlockSpec((rows, pair * width), lambda i: (0, i))
    hidden2 = pl.BlockSpec((rows, 2 * pair * width), lambda i: (0, i))
    gate_spec = pl.BlockSpec((1, rows, pair), lambda i: (i, 0, 0))
    joined = pltpu.VMEM((latent, 2 * pair * width), bf16)
    total = pltpu.VMEM((rows, latent), f32)
    units = 2 * rows * latent * width * count
    weight_bytes = 2 * latent * width * count
    hidden_bytes = 2 * rows * width * count
    latent_bytes = 2 * rows * latent

    def call(kernel, ins, outs, out_shape, scratch, parts, moved, exps=0):
        return pl.pallas_call(
            kernel,
            grid=(count // pair,),
            in_specs=ins,
            out_specs=outs,
            out_shape=out_shape,
            scratch_shapes=scratch,
            compiler_params=pltpu.CompilerParams(
                vmem_limit_bytes=(40 if rows <= 1024 else 56) * 1024 * 1024
            ),
            cost_estimate=pl.CostEstimate(
                flops=parts * units, bytes_accessed=moved, transcendentals=exps
            ),
        )

    hid = shaped(rows, count * width)
    lat = shaped(rows, latent)
    col = shaped(count, latent, width)
    forward = call(
        forward_kernel,
        [whole, gate_spec, col_proj, col_proj, row_proj],
        [hidden, hidden, hidden, whole],
        [hid, hid, hid, lat],
        [joined, total],
        3,
        3 * weight_bytes + 3 * hidden_bytes + 2 * latent_bytes,
        rows * width * count,
    )
    backward = call(
        backward_kernel,
        [whole, hidden, hidden, col_proj, col_proj, row_proj],
        [hidden2, whole],
        [shaped(rows, 2 * count * width), lat],
        [joined, total],
        3,
        3 * weight_bytes + 4 * hidden_bytes + 2 * latent_bytes,
    )
    down_grads = call(
        down_grad_kernel,
        [hidden, whole],
        row_proj,
        shaped(count * width, latent),
        [],
        1,
        weight_bytes + hidden_bytes + latent_bytes,
    )
    input_grads = call(
        input_grad_kernel,
        [whole, hidden2],
        [col_proj, col_proj],
        [col, col],
        [],
        2,
        2 * weight_bytes + 2 * hidden_bytes + latent_bytes,
    )

    def gate_blocks(gate_columns):
        return gate_columns.reshape(rows, count // pair, pair).transpose(1, 0, 2)

    return forward, backward, down_grads, input_grads, gate_blocks


def local(tokens, down_weight, up_weight, gate_proj, up_proj, down_proj, routes, gates, cotangent):
    n_expert = lax.axis_size("expert")
    n_group = lax.axis_size("group")
    own = lax.axis_index("expert")
    t = lax.axis_index("tensor")
    tok_rows = tokens.shape[0]
    half_rows = tok_rows // 2
    quarter_d = tokens.shape[1] // 4
    exp_local, latent, width = gate_proj.shape
    shard = down_weight.shape[1]

    nh = n_expert // 4
    h, q = own // 4, own % 4
    cols = latent // nh
    shared = n_group % 2 == 0
    g = lax.axis_index("group") % 2

    def to_peer(v, r):
        return lax.ppermute(v, "expert", [(e, e ^ r) for e in range(n_expert)])

    def t_swap(v):
        return lax.ppermute(v, "tensor", [(0, 1), (1, 0)])

    def g_swap(v):
        return lax.ppermute(v, "group", [(i, i ^ 1) for i in range(n_group)])

    def up(v):
        return lax.ppermute(v, "expert", [(e, (e + 4) % n_expert) for e in range(n_expert)])

    def down(v):
        return lax.ppermute(v, "expert", [((e + 4) % n_expert, e) for e in range(n_expert)])

    def add(*terms):
        return sum(v.astype(f32) for v in terms).astype(bf16)

    def after(v, *done):
        return lax.optimization_barrier((v, *done))[0]

    def turn(blocks):
        result = []
        for k in range(nh):
            block = blocks[-k % nh]
            for i in range(1, nh):
                block = jnp.where(h == i, blocks[(i - k) % nh], block)
            result.append(block)
        return result

    def by_quarter(parts):
        low = [jnp.where(q % 2 == 0, parts[i], parts[i ^ 1]) for i in range(4)]
        return [jnp.where(q < 2, low[i], low[i ^ 2]) for i in range(4)]

    def flip(v, index, axis):
        first, second = jnp.split(v, 2, axis=axis)
        return jnp.where(index == 0, v, jnp.concatenate([second, first], axis=axis))

    def exchange(block_for):
        return [block_for(0)] + [to_peer(block_for(r), r) for r in (1, 2, 3)]

    def together(*values):
        return lax.optimization_barrier(values)

    def gather_h(v):
        parts = [v]
        for _ in range(nh - 1):
            parts.append(up(parts[-1]))
        return parts

    def square_rows(v):
        return exchange(
            lambda r: lax.dynamic_slice_in_dim(v, (q ^ r) * quarter_d, quarter_d, 1)
        )

    def first_rows(v):
        size = 2 * quarter_d
        mine = lax.dynamic_slice_in_dim(v, q // 2 * size, size, 1)
        other = lax.dynamic_slice_in_dim(v, (1 - q // 2) * size, size, 1)
        return jnp.concatenate([mine, to_peer(other, 2)], axis=0)

    def second_rows(v):
        mine = lax.dynamic_slice_in_dim(v, q % 2 * quarter_d, quarter_d, 1)
        other = lax.dynamic_slice_in_dim(v, (1 - q % 2) * quarter_d, quarter_d, 1)
        return mine, to_peer(other, 1)

    def square_weight(v):
        size = quarter_d // 2 if shared else quarter_d
        first = g * size if shared else 0
        parts = exchange(
            lambda r: lax.dynamic_slice_in_dim(v, (q ^ r) * quarter_d + first, size, 0)
        )
        return parts

    def join_quarters(parts):
        return jnp.concatenate(by_quarter(parts), axis=1)

    def first_weight(v):
        size = quarter_d // 2 if shared else quarter_d
        first = g * size if shared else 0

        def half(i):
            starts = [(2 * i + j) * quarter_d + first for j in (0, 1)]
            return jnp.stack([lax.dynamic_slice_in_dim(v, at, size, 0) for at in starts])

        return half(q // 2), to_peer(half(1 - q // 2), 2)

    def second_weight(mine, theirs):
        both = jnp.concatenate([mine, theirs], axis=2)
        other = lax.dynamic_index_in_dim(both, 1 - q % 2, 0, keepdims=False)
        return lax.dynamic_index_in_dim(both, q % 2, 0, keepdims=False), to_peer(other, 1)

    def join_steps(mine, theirs):
        return join_quarters([v[:, i * shard : (i + 1) * shard] for i in (0, 1) for v in (mine, theirs)])

    def swap_features(v):
        return g_swap(v) if shared else v

    def all_features(v, theirs):
        return flip(jnp.concatenate([v, theirs], axis=0), g, 0) if shared else v

    def project(rows, weights):
        parts = [dot(rows, weight).astype(bf16) for weight in weights]
        part = jnp.concatenate(parts, axis=1).reshape(4, 2, half_rows, latent)
        mine = lax.dynamic_index_in_dim(part, t, 1, keepdims=False)
        return mine, lax.dynamic_index_in_dim(part, 1 - t, 1, keepdims=False)

    def own_latent(parts):
        return jnp.concatenate(turn(jnp.split(add(*parts), nh, axis=1)), axis=1)

    def sum_tensor(part):
        part = part.reshape(2, nh, 4, half_rows, latent)
        return add(part[0], t_swap(part[1]))

    def for_peer(part):
        return lambda r: lax.dynamic_index_in_dim(part, q ^ r, 1, keepdims=False)

    def sum_squares(part):
        if nh == 2:
            return part, up(part)
        pieces = turn(list(part))
        total = pieces[nh - 1]
        for k in range(nh - 2, -1, -1):
            total = add(down(total), pieces[k])
        return part, jnp.stack(turn(gather_h(total)))

    def join_squares(part, theirs):
        rows = turn(list(add(part, theirs) if nh == 2 else theirs))
        split = [turn(jnp.split(v, nh, axis=1)) for v in rows]
        return jnp.concatenate(split[0] + [v[0] for v in split[1:]], axis=1)

    def square_blocks(part):
        part = flip(jnp.stack([part, t_swap(part)], axis=1), t, 1)
        return jnp.split(part.reshape(4 * tok_rows, -1), 2 * nh - 1, axis=1)

    def products(blocks, rows, weights):
        grad = sum(dot(v, block, TN) for v, block in zip(rows, blocks[:1] + blocks[nh:]))
        whole = sum(dot(block, weight, NT) for block, weight in zip(blocks, weights))
        return grad.astype(bf16), whole.astype(bf16)

    def send_products(grad, whole):
        whole = whole.reshape(4, tok_rows, quarter_d)
        grads = exchange(lambda r: lax.dynamic_slice_in_dim(grad, (q ^ r) * shard, shard, 1))
        return grads, exchange(lambda r: whole[r])

    def join_products(grads, wholes):
        grad = jnp.concatenate(by_quarter(grads), axis=0).astype(f32)
        return jnp.concatenate(by_quarter(wholes), axis=1), grad

    local_ids = own * exp_local + jnp.arange(exp_local, dtype=jnp.int32)
    hit = routes[:, :, None] == local_ids[None, None, :]
    gate_all = jnp.sum(jnp.where(hit, gates[:, :, None], 0), axis=1).astype(f32) * gate_unit
    gate_all = gate_all.reshape(n_expert, 2, half_rows, exp_local)
    gate_all = jnp.stack([gate_all[:, 0], gate_all[:, 1]])
    gate_columns = flip(gate_all, t, 0).reshape(-1, exp_local)

    group_rows = n_expert * tok_rows
    forward, backward, down_grads, input_grads, gate_blocks = expert_calls(
        group_rows, latent, exp_local, width
    )
    down_rows = down_proj.reshape(exp_local * width, latent)

    def gather_latent(part):
        return lax.all_gather(part, "expert").reshape(n_expert * half_rows, latent)

    def join_rows(mine, theirs):
        return [v[i * tok_rows : (i + 1) * tok_rows] for i in (0, 1) for v in (mine, theirs)]

    down_block = square_weight(down_weight)
    token_rows = first_rows(tokens)
    up_mine, up_theirs = first_weight(up_weight)
    up_mine, up_theirs = second_weight(up_mine, after(up_theirs, *down_block[1:]))
    down_parts = gather_h(join_quarters(down_block))
    theirs = [swap_features(down_parts[0])]
    token_rows, up_theirs, down_parts[-1], theirs[0] = together(
        token_rows, up_theirs, down_parts[-1], theirs[0]
    )
    up_parts = gather_h(join_steps(up_mine, up_theirs))
    theirs += [swap_features(v) for v in down_parts[1:]]
    mine, other = second_rows(token_rows)
    cot_rows = first_rows(after(cotangent, token_rows))
    other, cot_rows, theirs[-1] = together(other, cot_rows, theirs[-1])
    token_rows = jnp.concatenate(join_rows(mine, other), axis=0)
    down_parts = [all_features(v, w) for v, w in zip(down_parts, theirs)]

    cot_mine, cot_theirs = second_rows(cot_rows)
    mine, other = project(token_rows, down_parts)
    other, up_parts[-1] = together(t_swap(other), up_parts[-1])
    theirs = [swap_features(v) for v in up_parts]
    part_x = add(mine, other)
    part_x = exchange(lambda r: part_x[r])
    *part_x, cot_theirs, theirs[-1] = together(*part_x, cot_theirs, theirs[-1])
    part_x = gather_latent(own_latent(part_x))
    cot_rows = jnp.concatenate(join_rows(cot_mine, cot_theirs), axis=0)
    up_parts = [all_features(v, w) for v, w in zip(up_parts, theirs)]
    mine, other = project(cot_rows, up_parts)
    part_y = add(mine, t_swap(other))
    part_y = gather_latent(own_latent(exchange(lambda r: part_y[r])))
    other = t_swap(part_x)
    latent_in = jnp.concatenate([part_x, other], axis=0)
    token_parts = gather_h(after(token_rows, other))

    hs, cp, cu, out_part = forward(
        latent_in, gate_blocks(gate_columns), gate_proj, up_proj, down_rows
    )
    part_y, token_parts[-1], out_part = together(part_y, token_parts[-1], out_part)
    latent_grad = jnp.concatenate([part_y, t_swap(part_y)], axis=0)
    cot_parts = gather_h(after(cot_rows, token_parts[-1]))
    out_part = sum_tensor(out_part)
    down_proj_grad = down_grads(hs, latent_grad)
    out_part = after(out_part, down_proj_grad)
    dpu, in_part = backward(
        after(latent_grad, out_part), cp, cu, gate_proj, up_proj, down_rows
    )
    out_part = exchange(for_peer(out_part))
    *out_part, cot_parts[-1], in_part = together(*out_part, cot_parts[-1], in_part)
    out_part = add(*out_part)
    in_part = sum_tensor(after(in_part, out_part))
    gate_proj_grad, up_proj_grad = input_grads(latent_in, after(dpu, in_part))
    in_part = exchange(for_peer(in_part))
    *in_part, out_theirs, gate_proj_grad = together(
        *in_part, sum_squares(out_part)[1], gate_proj_grad
    )
    out_part = join_squares(out_part, out_theirs)
    in_part, in_theirs = sum_squares(add(*in_part))
    out_part = exchange(lambda r: out_part)
    *out_part, in_theirs = together(*out_part, in_theirs)
    out_part = jnp.stack(out_part)
    in_part = join_squares(in_part, in_theirs)
    in_part = jnp.stack(exchange(lambda r: in_part))
    out_sent = send_products(*products(square_blocks(out_part), cot_parts, up_parts))
    in_products = products(square_blocks(in_part), token_parts, down_parts)
    received = together(*out_sent[0], *out_sent[1], *in_products)
    out, up_grad = join_products(received[:4], received[4:8])
    tokens_grad, down_grad = join_products(*send_products(*in_products))
    down_proj_grad = down_proj_grad.reshape(down_proj.shape)
    return (out, tokens_grad, gate_proj_grad, up_proj_grad, down_proj_grad, down_grad, up_grad)


def solution(mesh):
    in_specs = (
        P(("group", "expert"), "tensor"),
        P("tensor", "expert"),
        P("tensor", "expert"),
        P("expert", None, "tensor"),
        P("expert", None, "tensor"),
        P("expert", "tensor", None),
        P("group", None),
        P("group", None),
        P(("group", "expert"), "tensor"),
    )
    out_specs = (
        P(("group", "expert"), "tensor"),
        P(("group", "expert"), "tensor"),
        P(("group", "expert"), None, "tensor"),
        P(("group", "expert"), None, "tensor"),
        P(("group", "expert"), "tensor", None),
        P(("group", "tensor"), "expert"),
        P(("group", "tensor"), "expert"),
    )
    return jax.shard_map(local, mesh=mesh, in_specs=in_specs, out_specs=out_specs, check_vma=False)
```

```python
import jax
import jax.numpy as jnp
from jax import lax
from jax.experimental import pallas as pl
from jax.experimental.pallas import tpu as pltpu
from jax.sharding import PartitionSpec as P

gate_unit = 2.0 ** (-15)
bf16 = jnp.bfloat16
f32 = jnp.float32

NN = (((1,), (0,)), ((), ()))
NT = (((1,), (1,)), ((), ()))
TN = (((0,), (0,)), ((), ()))


def dot(a, b, dims=NN):
    return lax.dot_general(a, b, dims, preferred_element_type=f32)


def join_projections(wg_ref, wu_ref, wgu):
    pair, _, width = wg_ref.shape
    for j in range(pair):
        wgu[:, 2 * j * width : (2 * j + 1) * width] = wg_ref[j]
        wgu[:, (2 * j + 1) * width : (2 * j + 2) * width] = wu_ref[j]


def forward_kernel(
    x_ref, g_ref, wg_ref, wu_ref, wd_ref, hs_ref, cp_ref, cu_ref, lo_ref, wgu, lo_acc
):
    step = pl.program_id(0)
    pair, _, width = wg_ref.shape
    block = 256
    join_projections(wg_ref, wu_ref, wgu)

    @pl.when(step == 0)
    def _():
        lo_acc[...] = jnp.zeros_like(lo_acc)

    for i in range(x_ref.shape[0] // block):
        rows = slice(i * block, (i + 1) * block)
        x = x_ref[rows, :]
        for j in range(pair):
            cols = slice(j * width, (j + 1) * width)
            both = dot(x, wgu[:, 2 * j * width : (2 * j + 2) * width])
            gate_pre, up_pre = both[:, :width], both[:, width:]
            gate = g_ref[0, rows, j : j + 1]
            sig = jax.nn.sigmoid(gate_pre)
            act = gate_pre * sig * gate
            hs_ref[rows, cols] = (act * up_pre).astype(bf16)
            cu_ref[rows, cols] = act.astype(bf16)
            slope = up_pre * (sig * (1.0 + gate_pre * (1.0 - sig)))
            cp_ref[rows, cols] = (slope * gate).astype(bf16)
        lo_acc[rows, :] += dot(hs_ref[rows, :], wd_ref[...])

    @pl.when(step == pl.num_programs(0) - 1)
    def _():
        lo_ref[...] = lo_acc[...].astype(bf16)


def backward_kernel(
    y_ref, cp_ref, cu_ref, wg_ref, wu_ref, wd_ref, dpu_ref, lig_ref, wgu, lig_acc
):
    step = pl.program_id(0)
    pair, _, width = wg_ref.shape
    block = 256
    join_projections(wg_ref, wu_ref, wgu)

    @pl.when(step == 0)
    def _():
        lig_acc[...] = jnp.zeros_like(lig_acc)

    for i in range(y_ref.shape[0] // block):
        rows = slice(i * block, (i + 1) * block)
        hidden_grad = dot(y_ref[rows, :], wd_ref[...], NT)
        for j in range(pair):
            cols = slice(j * width, (j + 1) * width)
            hg = hidden_grad[:, cols]
            dp = hg * cp_ref[rows, cols].astype(f32)
            du = hg * cu_ref[rows, cols].astype(f32)
            dpu_ref[rows, 2 * j * width : (2 * j + 1) * width] = dp.astype(bf16)
            dpu_ref[rows, (2 * j + 1) * width : (2 * j + 2) * width] = du.astype(bf16)
        lig_acc[rows, :] += dot(dpu_ref[rows, :], wgu[...], NT)

    @pl.when(step == pl.num_programs(0) - 1)
    def _():
        lig_ref[...] = lig_acc[...].astype(bf16)


def down_grad_kernel(hs_ref, y_ref, dwd_ref):
    dwd_ref[...] = dot(hs_ref[...], y_ref[...], TN).astype(bf16)


def input_grad_kernel(x_ref, dpu_ref, dwg_ref, dwu_ref):
    pair, latent, width = dwg_ref.shape
    block = 256

    for i in range(latent // block):
        cols = slice(i * block, (i + 1) * block)
        grads = dot(x_ref[:, cols], dpu_ref[...], TN)
        for j in range(pair):
            dwg_ref[j, cols, :] = grads[:, 2 * j * width : (2 * j + 1) * width].astype(bf16)
            dwu_ref[j, cols, :] = grads[:, (2 * j + 1) * width : (2 * j + 2) * width].astype(bf16)


def shaped(*shape):
    return jax.ShapeDtypeStruct(shape, bf16)


def expert_calls(rows, latent, count, width):
    pair = 2 if rows <= 1024 and count % 2 == 0 else 1
    whole = pl.BlockSpec((rows, latent), lambda i: (0, 0))
    col_proj = pl.BlockSpec((pair, latent, width), lambda i: (i, 0, 0))
    row_proj = pl.BlockSpec((pair * width, latent), lambda i: (i, 0))
    hidden = pl.BlockSpec((rows, pair * width), lambda i: (0, i))
    hidden2 = pl.BlockSpec((rows, 2 * pair * width), lambda i: (0, i))
    gate_spec = pl.BlockSpec((1, rows, pair), lambda i: (i, 0, 0))
    joined = pltpu.VMEM((latent, 2 * pair * width), bf16)
    total = pltpu.VMEM((rows, latent), f32)
    units = 2 * rows * latent * width * count
    weight_bytes = 2 * latent * width * count
    hidden_bytes = 2 * rows * width * count
    latent_bytes = 2 * rows * latent

    def call(kernel, ins, outs, out_shape, scratch, parts, moved, exps=0):
        return pl.pallas_call(
            kernel,
            grid=(count // pair,),
            in_specs=ins,
            out_specs=outs,
            out_shape=out_shape,
            scratch_shapes=scratch,
            compiler_params=pltpu.CompilerParams(
                vmem_limit_bytes=(40 if rows <= 1024 else 56) * 1024 * 1024
            ),
            cost_estimate=pl.CostEstimate(
                flops=parts * units, bytes_accessed=moved, transcendentals=exps
            ),
        )

    hid = shaped(rows, count * width)
    lat = shaped(rows, latent)
    col = shaped(count, latent, width)
    forward = call(
        forward_kernel,
        [whole, gate_spec, col_proj, col_proj, row_proj],
        [hidden, hidden, hidden, whole],
        [hid, hid, hid, lat],
        [joined, total],
        3,
        3 * weight_bytes + 3 * hidden_bytes + 2 * latent_bytes,
        rows * width * count,
    )
    backward = call(
        backward_kernel,
        [whole, hidden, hidden, col_proj, col_proj, row_proj],
        [hidden2, whole],
        [shaped(rows, 2 * count * width), lat],
        [joined, total],
        3,
        3 * weight_bytes + 4 * hidden_bytes + 2 * latent_bytes,
    )
    down_grads = call(
        down_grad_kernel,
        [hidden, whole],
        row_proj,
        shaped(count * width, latent),
        [],
        1,
        weight_bytes + hidden_bytes + latent_bytes,
    )
    input_grads = call(
        input_grad_kernel,
        [whole, hidden2],
        [col_proj, col_proj],
        [col, col],
        [],
        2,
        2 * weight_bytes + 2 * hidden_bytes + latent_bytes,
    )

    def gate_blocks(gate_columns):
        return gate_columns.reshape(rows, count // pair, pair).transpose(1, 0, 2)

    return forward, backward, down_grads, input_grads, gate_blocks


def local(tokens, down_weight, up_weight, gate_proj, up_proj, down_proj, routes, gates, cotangent):
    n_expert = lax.axis_size("expert")
    n_group = lax.axis_size("group")
    own = lax.axis_index("expert")
    t = lax.axis_index("tensor")
    tok_rows = tokens.shape[0]
    half_rows = tok_rows // 2
    quarter_d = tokens.shape[1] // 4
    exp_local, latent, width = gate_proj.shape
    shard = down_weight.shape[1]

    nh = n_expert // 4
    h, q = own // 4, own % 4
    cols = latent // nh
    shared = n_group % 2 == 0
    g = lax.axis_index("group") % 2

    def to_peer(v, r):
        return lax.ppermute(v, "expert", [(e, e ^ r) for e in range(n_expert)])

    def t_swap(v):
        return lax.ppermute(v, "tensor", [(0, 1), (1, 0)])

    def g_swap(v):
        return lax.ppermute(v, "group", [(i, i ^ 1) for i in range(n_group)])

    def up(v):
        return lax.ppermute(v, "expert", [(e, (e + 4) % n_expert) for e in range(n_expert)])

    def down(v):
        return lax.ppermute(v, "expert", [((e + 4) % n_expert, e) for e in range(n_expert)])

    def add(*terms):
        return sum(v.astype(f32) for v in terms).astype(bf16)

    def after(v, *done):
        return lax.optimization_barrier((v, *done))[0]

    def turn(blocks):
        result = []
        for k in range(nh):
            block = blocks[-k % nh]
            for i in range(1, nh):
                block = jnp.where(h == i, blocks[(i - k) % nh], block)
            result.append(block)
        return result

    def by_quarter(parts):
        low = [jnp.where(q % 2 == 0, parts[i], parts[i ^ 1]) for i in range(4)]
        return [jnp.where(q < 2, low[i], low[i ^ 2]) for i in range(4)]

    def flip(v, index, axis):
        first, second = jnp.split(v, 2, axis=axis)
        return jnp.where(index == 0, v, jnp.concatenate([second, first], axis=axis))

    def exchange(block_for):
        return [block_for(0)] + [to_peer(block_for(r), r) for r in (1, 2, 3)]

    def together(*values):
        return lax.optimization_barrier(values)

    def gather_h(v):
        parts = [v]
        for _ in range(nh - 1):
            parts.append(up(parts[-1]))
        return parts

    def square_rows(v):
        return exchange(
            lambda r: lax.dynamic_slice_in_dim(v, (q ^ r) * quarter_d, quarter_d, 1)
        )

    def first_rows(v):
        size = 2 * quarter_d
        mine = lax.dynamic_slice_in_dim(v, q // 2 * size, size, 1)
        other = lax.dynamic_slice_in_dim(v, (1 - q // 2) * size, size, 1)
        return jnp.concatenate([mine, to_peer(other, 2)], axis=0)

    def second_rows(v):
        mine = lax.dynamic_slice_in_dim(v, q % 2 * quarter_d, quarter_d, 1)
        other = lax.dynamic_slice_in_dim(v, (1 - q % 2) * quarter_d, quarter_d, 1)
        return mine, to_peer(other, 1)

    def square_weight(v):
        size = quarter_d // 2 if shared else quarter_d
        first = g * size if shared else 0
        parts = exchange(
            lambda r: lax.dynamic_slice_in_dim(v, (q ^ r) * quarter_d + first, size, 0)
        )
        return parts

    def join_quarters(parts):
        return jnp.concatenate(by_quarter(parts), axis=1)

    def first_weight(v):
        pairs = v.reshape(2, 2, quarter_d, shard)
        mine = lax.dynamic_index_in_dim(pairs, q // 2, 0, keepdims=False)
        other = lax.dynamic_index_in_dim(pairs, 1 - q // 2, 0, keepdims=False)
        return mine, to_peer(other, 2)

    def second_weight(mine, theirs):
        both = jnp.concatenate([mine, theirs], axis=2)
        other = lax.dynamic_index_in_dim(both, 1 - q % 2, 0, keepdims=False)
        return lax.dynamic_index_in_dim(both, q % 2, 0, keepdims=False), to_peer(other, 1)

    def join_steps(mine, theirs):
        return join_quarters([v[:, i * shard : (i + 1) * shard] for i in (0, 1) for v in (mine, theirs)])

    def own_half(v):
        size = quarter_d // 2
        return lax.dynamic_slice_in_dim(v, g * size, size, 0) if shared else v

    def join_rows(mine, theirs):
        return [v[i * tok_rows : (i + 1) * tok_rows] for i in (0, 1) for v in (mine, theirs)]

    def swap_features(v):
        return g_swap(v) if shared else v

    def all_features(v, theirs):
        return flip(jnp.concatenate([v, theirs], axis=0), g, 0) if shared else v

    def project(rows, weights):
        parts = [dot(rows, weight).astype(bf16) for weight in weights]
        part = jnp.concatenate(parts, axis=1).reshape(4, 2, half_rows, latent)
        mine = lax.dynamic_index_in_dim(part, t, 1, keepdims=False)
        return mine, lax.dynamic_index_in_dim(part, 1 - t, 1, keepdims=False)

    def own_latent(parts):
        return jnp.concatenate(turn(jnp.split(add(*parts), nh, axis=1)), axis=1)

    def sum_tensor(part):
        part = part.reshape(2, 4, nh, half_rows, latent)
        return add(part[0], t_swap(part[1]))

    def sum_squares(part):
        if nh == 2:
            return part, up(part)
        total = part[nh - 1]
        for k in range(nh - 2, -1, -1):
            total = add(down(total), part[k])
        return part, jnp.stack(gather_h(total))

    def join_squares(part, theirs):
        rows = [add(part[0], theirs[1]), add(part[1], theirs[0])] if nh == 2 else list(theirs)
        split = [turn(jnp.split(v, nh, axis=1)) for v in rows]
        return jnp.concatenate(split[0] + [v[0] for v in split[1:]], axis=1)

    def square_blocks(part):
        part = flip(jnp.stack([part, t_swap(part)], axis=1), t, 1)
        return jnp.split(part.reshape(4 * tok_rows, -1), 2 * nh - 1, axis=1)

    def products(blocks, rows, weights):
        grad = sum(dot(v, block, TN) for v, block in zip(rows, blocks[:1] + blocks[nh:]))
        whole = sum(dot(block, weight, NT) for block, weight in zip(blocks, weights))
        return grad.astype(bf16), whole.astype(bf16)

    def send_products(grad, whole):
        whole = whole.reshape(4, tok_rows, quarter_d)
        grads = exchange(lambda r: lax.dynamic_slice_in_dim(grad, (q ^ r) * shard, shard, 1))
        return grads, exchange(lambda r: whole[r])

    def join_products(grads, wholes):
        grad = jnp.concatenate(by_quarter(grads), axis=0).astype(f32)
        return jnp.concatenate(by_quarter(wholes), axis=1), grad

    local_ids = own * exp_local + jnp.arange(exp_local, dtype=jnp.int32)
    hit = routes[:, :, None] == local_ids[None, None, :]
    gate_all = jnp.sum(jnp.where(hit, gates[:, :, None], 0), axis=1).astype(f32) * gate_unit
    gate_all = gate_all.reshape(nh, 4, 2, half_rows, exp_local)
    gate_all = jnp.stack(turn(list(gate_all)))
    gate_all = jnp.stack(by_quarter([gate_all[:, i] for i in range(4)]))
    gate_all = flip(gate_all, t, 2)
    gate_columns = gate_all.transpose(2, 0, 1, 3, 4).reshape(-1, exp_local)

    group_rows = n_expert * tok_rows
    forward, backward, down_grads, input_grads, gate_blocks = expert_calls(
        group_rows, latent, exp_local, width
    )
    down_rows = down_proj.reshape(exp_local * width, latent)

    def rows_with(part, theirs):
        return jnp.stack([part, theirs]).reshape(-1, latent)

    down_block = square_weight(down_weight)
    token_rows = first_rows(tokens)
    up_mine, up_theirs = first_weight(up_weight)
    up_mine, up_theirs = second_weight(up_mine, after(up_theirs, *down_block[1:]))
    down_parts = gather_h(join_quarters(down_block))
    theirs = [swap_features(down_parts[0])]
    token_rows, up_theirs, down_parts[-1], theirs[0] = together(
        token_rows, up_theirs, down_parts[-1], theirs[0]
    )
    theirs += [swap_features(v) for v in down_parts[1:]]
    mine, other = second_rows(token_rows)
    cot_rows = first_rows(after(cotangent, token_rows))
    other, cot_rows, theirs[-1] = together(other, cot_rows, theirs[-1])
    token_rows = jnp.concatenate(join_rows(mine, other), axis=0)
    down_parts = [all_features(v, w) for v, w in zip(down_parts, theirs)]

    up_block = join_steps(up_mine, up_theirs)
    up_parts = gather_h(own_half(up_block))
    cot_mine, cot_theirs = second_rows(cot_rows)
    mine, other = project(token_rows, down_parts)
    part_x = add(mine, t_swap(other))
    part_x = exchange(lambda r: part_x[r])
    *part_x, cot_theirs, up_parts[-1] = together(*part_x, cot_theirs, up_parts[-1])
    cot_rows = jnp.concatenate(join_rows(cot_mine, cot_theirs), axis=0)
    part_x = gather_h(own_latent(part_x))
    theirs = [swap_features(v) for v in up_parts[1:]]
    *part_x, theirs[-1] = together(*part_x, theirs[-1])
    part_x = jnp.stack(part_x)
    up_parts = [up_block] + [all_features(v, w) for v, w in zip(up_parts[1:], theirs)]
    part_x = exchange(lambda r: part_x)
    mine, other = project(cot_rows, up_parts)
    *part_x, other = together(*part_x, t_swap(other))
    part_x = jnp.stack(part_x)
    part_y = add(mine, other)
    part_y = exchange(lambda r: part_y[r])
    *part_y, other = together(*part_y, t_swap(part_x))
    latent_in = rows_with(part_x, other)
    part_y = jnp.stack(gather_h(own_latent(part_y)))
    latent_in = after(latent_in, part_y)
    token_parts = gather_h(after(token_rows, part_y))

    hs, cp, cu, out_part = forward(
        latent_in, gate_blocks(gate_columns), gate_proj, up_proj, down_rows
    )
    part_y = exchange(lambda r: part_y)
    *part_y, token_parts[-1], out_part = together(*part_y, token_parts[-1], out_part)
    part_y = jnp.stack(part_y)
    latent_grad = rows_with(part_y, t_swap(part_y))
    cot_parts = gather_h(after(cot_rows, token_parts[-1]))
    out_part = sum_tensor(out_part)
    down_proj_grad = down_grads(hs, latent_grad)
    out_part = after(out_part, down_proj_grad)
    dpu, in_part = backward(
        after(latent_grad, out_part), cp, cu, gate_proj, up_proj, down_rows
    )
    out_part = exchange(lambda r: out_part[r])
    *out_part, cot_parts[-1], in_part = together(*out_part, cot_parts[-1], in_part)
    out_part = add(*out_part)
    in_part = sum_tensor(after(in_part, out_part))
    gate_proj_grad, up_proj_grad = input_grads(latent_in, after(dpu, in_part))
    in_part = exchange(lambda r: in_part[r])
    *in_part, out_theirs, gate_proj_grad = together(
        *in_part, sum_squares(out_part)[1], gate_proj_grad
    )
    out_part = join_squares(out_part, out_theirs)
    in_part, in_theirs = sum_squares(add(*in_part))
    out_part = exchange(lambda r: out_part)
    *out_part, in_theirs = together(*out_part, in_theirs)
    out_part = jnp.stack(out_part)
    in_part = join_squares(in_part, in_theirs)
    in_part = jnp.stack(exchange(lambda r: in_part))
    out_sent = send_products(*products(square_blocks(out_part), cot_parts, up_parts))
    in_products = products(square_blocks(in_part), token_parts, down_parts)
    received = together(*out_sent[0], *out_sent[1], *in_products)
    out, up_grad = join_products(received[:4], received[4:8])
    tokens_grad, down_grad = join_products(*send_products(*in_products))
    down_proj_grad = down_proj_grad.reshape(down_proj.shape)
    return (out, tokens_grad, gate_proj_grad, up_proj_grad, down_proj_grad, down_grad, up_grad)


def solution(mesh):
    in_specs = (
        P(("group", "expert"), "tensor"),
        P("tensor", "expert"),
        P("tensor", "expert"),
        P("expert", None, "tensor"),
        P("expert", None, "tensor"),
        P("expert", "tensor", None),
        P("group", None),
        P("group", None),
        P(("group", "expert"), "tensor"),
    )
    out_specs = (
        P(("group", "expert"), "tensor"),
        P(("group", "expert"), "tensor"),
        P(("group", "expert"), None, "tensor"),
        P(("group", "expert"), None, "tensor"),
        P(("group", "expert"), "tensor", None),
        P(("group", "tensor"), "expert"),
        P(("group", "tensor"), "expert"),
    )
    return jax.shard_map(local, mesh=mesh, in_specs=in_specs, out_specs=out_specs, check_vma=False)
```

```python
import jax
import jax.numpy as jnp
from jax import lax
from jax.experimental import pallas as pl
from jax.experimental.pallas import tpu as pltpu
from jax.sharding import PartitionSpec as P

gate_unit = 2.0 ** (-15)
bf16 = jnp.bfloat16
f32 = jnp.float32

NN = (((1,), (0,)), ((), ()))
NT = (((1,), (1,)), ((), ()))
TN = (((0,), (0,)), ((), ()))


def dot(a, b, dims=NN):
    return lax.dot_general(a, b, dims, preferred_element_type=f32)


def join_projections(wg_ref, wu_ref, wgu):
    pair, _, width = wg_ref.shape
    for j in range(pair):
        wgu[:, 2 * j * width : (2 * j + 1) * width] = wg_ref[j]
        wgu[:, (2 * j + 1) * width : (2 * j + 2) * width] = wu_ref[j]


def forward_kernel(
    x_ref, g_ref, wg_ref, wu_ref, wd_ref, hs_ref, cp_ref, cu_ref, lo_ref, wgu, lo_acc
):
    step = pl.program_id(0)
    pair, _, width = wg_ref.shape
    block = 256
    join_projections(wg_ref, wu_ref, wgu)

    @pl.when(step == 0)
    def _():
        lo_acc[...] = jnp.zeros_like(lo_acc)

    for i in range(x_ref.shape[0] // block):
        rows = slice(i * block, (i + 1) * block)
        x = x_ref[rows, :]
        for j in range(pair):
            cols = slice(j * width, (j + 1) * width)
            both = dot(x, wgu[:, 2 * j * width : (2 * j + 2) * width])
            gate_pre, up_pre = both[:, :width], both[:, width:]
            gate = g_ref[0, rows, j : j + 1]
            sig = jax.nn.sigmoid(gate_pre)
            act = gate_pre * sig * gate
            hs_ref[rows, cols] = (act * up_pre).astype(bf16)
            cu_ref[rows, cols] = act.astype(bf16)
            slope = up_pre * (sig * (1.0 + gate_pre * (1.0 - sig)))
            cp_ref[rows, cols] = (slope * gate).astype(bf16)
        lo_acc[rows, :] += dot(hs_ref[rows, :], wd_ref[...])

    @pl.when(step == pl.num_programs(0) - 1)
    def _():
        lo_ref[...] = lo_acc[...].astype(bf16)


def backward_kernel(
    y_ref, cp_ref, cu_ref, wg_ref, wu_ref, wd_ref, dpu_ref, lig_ref, wgu, lig_acc
):
    step = pl.program_id(0)
    pair, _, width = wg_ref.shape
    block = 256
    join_projections(wg_ref, wu_ref, wgu)

    @pl.when(step == 0)
    def _():
        lig_acc[...] = jnp.zeros_like(lig_acc)

    for i in range(y_ref.shape[0] // block):
        rows = slice(i * block, (i + 1) * block)
        hidden_grad = dot(y_ref[rows, :], wd_ref[...], NT)
        for j in range(pair):
            cols = slice(j * width, (j + 1) * width)
            hg = hidden_grad[:, cols]
            dp = hg * cp_ref[rows, cols].astype(f32)
            du = hg * cu_ref[rows, cols].astype(f32)
            dpu_ref[rows, 2 * j * width : (2 * j + 1) * width] = dp.astype(bf16)
            dpu_ref[rows, (2 * j + 1) * width : (2 * j + 2) * width] = du.astype(bf16)
        lig_acc[rows, :] += dot(dpu_ref[rows, :], wgu[...], NT)

    @pl.when(step == pl.num_programs(0) - 1)
    def _():
        lig_ref[...] = lig_acc[...].astype(bf16)


def down_grad_kernel(hs_ref, hs2_ref, y_ref, y2_ref, dwd_ref):
    total = dot(hs_ref[...], y_ref[...], TN) + dot(hs2_ref[...], y2_ref[...], TN)
    dwd_ref[...] = total.astype(bf16)


def input_grad_kernel(x_ref, x2_ref, dpu_ref, dpu2_ref, dwg_ref, dwu_ref):
    pair, latent, width = dwg_ref.shape
    block = 256

    for i in range(latent // block):
        cols = slice(i * block, (i + 1) * block)
        grads = dot(x_ref[:, cols], dpu_ref[...], TN) + dot(x2_ref[:, cols], dpu2_ref[...], TN)
        for j in range(pair):
            dwg_ref[j, cols, :] = grads[:, 2 * j * width : (2 * j + 1) * width].astype(bf16)
            dwu_ref[j, cols, :] = grads[:, (2 * j + 1) * width : (2 * j + 2) * width].astype(bf16)


def shaped(*shape):
    return jax.ShapeDtypeStruct(shape, bf16)


def expert_calls(rows, latent, count, width):
    pair = 2 if rows <= 1024 and count % 2 == 0 else 1
    whole = pl.BlockSpec((rows, latent), lambda i: (0, 0))
    col_proj = pl.BlockSpec((pair, latent, width), lambda i: (i, 0, 0))
    row_proj = pl.BlockSpec((pair * width, latent), lambda i: (i, 0))
    hidden = pl.BlockSpec((rows, pair * width), lambda i: (0, i))
    hidden2 = pl.BlockSpec((rows, 2 * pair * width), lambda i: (0, i))
    gate_spec = pl.BlockSpec((1, rows, pair), lambda i: (i, 0, 0))
    joined = pltpu.VMEM((latent, 2 * pair * width), bf16)
    total = pltpu.VMEM((rows, latent), f32)
    units = 2 * rows * latent * width * count
    weight_bytes = 2 * latent * width * count
    hidden_bytes = 2 * rows * width * count
    latent_bytes = 2 * rows * latent

    def call(kernel, ins, outs, out_shape, scratch, parts, moved, exps=0):
        return pl.pallas_call(
            kernel,
            grid=(count // pair,),
            in_specs=ins,
            out_specs=outs,
            out_shape=out_shape,
            scratch_shapes=scratch,
            compiler_params=pltpu.CompilerParams(
                vmem_limit_bytes=(40 if rows <= 1024 else 56) * 1024 * 1024
            ),
            cost_estimate=pl.CostEstimate(
                flops=parts * units, bytes_accessed=moved, transcendentals=exps
            ),
        )

    hid = shaped(rows, count * width)
    lat = shaped(rows, latent)
    col = shaped(count, latent, width)
    forward = call(
        forward_kernel,
        [whole, gate_spec, col_proj, col_proj, row_proj],
        [hidden, hidden, hidden, whole],
        [hid, hid, hid, lat],
        [joined, total],
        3,
        3 * weight_bytes + 3 * hidden_bytes + 2 * latent_bytes,
        rows * width * count,
    )
    backward = call(
        backward_kernel,
        [whole, hidden, hidden, col_proj, col_proj, row_proj],
        [hidden2, whole],
        [shaped(rows, 2 * count * width), lat],
        [joined, total],
        3,
        3 * weight_bytes + 4 * hidden_bytes + 2 * latent_bytes,
    )
    down_grads = call(
        down_grad_kernel,
        [hidden, hidden, whole, whole],
        row_proj,
        shaped(count * width, latent),
        [],
        2,
        weight_bytes + 2 * hidden_bytes + 2 * latent_bytes,
    )
    input_grads = call(
        input_grad_kernel,
        [whole, whole, hidden2, hidden2],
        [col_proj, col_proj],
        [col, col],
        [],
        4,
        2 * weight_bytes + 4 * hidden_bytes + 2 * latent_bytes,
    )

    def gate_blocks(gate_columns):
        return gate_columns.reshape(2, rows, count // pair, pair).transpose(0, 2, 1, 3)

    return forward, backward, down_grads, input_grads, gate_blocks


def local(tokens, down_weight, up_weight, gate_proj, up_proj, down_proj, routes, gates, cotangent):
    n_expert = lax.axis_size("expert")
    n_group = lax.axis_size("group")
    own = lax.axis_index("expert")
    t = lax.axis_index("tensor")
    tok_rows = tokens.shape[0]
    half_rows = tok_rows // 2
    quarter_d = tokens.shape[1] // 4
    exp_local, latent, width = gate_proj.shape
    shard = down_weight.shape[1]

    nh = n_expert // 4
    h, q = own // 4, own % 4
    cols = latent // nh
    shared = n_group % 2 == 0
    g = lax.axis_index("group") % 2

    def to_peer(v, r):
        return lax.ppermute(v, "expert", [(e, e ^ r) for e in range(n_expert)])

    def t_swap(v):
        return lax.ppermute(v, "tensor", [(0, 1), (1, 0)])

    def g_swap(v):
        return lax.ppermute(v, "group", [(i, i ^ 1) for i in range(n_group)])

    def up(v):
        return lax.ppermute(v, "expert", [(e, (e + 4) % n_expert) for e in range(n_expert)])

    def down(v):
        return lax.ppermute(v, "expert", [((e + 4) % n_expert, e) for e in range(n_expert)])

    def add(*terms):
        return sum(v.astype(f32) for v in terms).astype(bf16)

    def after(v, *done):
        return lax.optimization_barrier((v, *done))[0]

    def turn(blocks):
        result = []
        for k in range(nh):
            block = blocks[-k % nh]
            for i in range(1, nh):
                block = jnp.where(h == i, blocks[(i - k) % nh], block)
            result.append(block)
        return result

    def by_quarter(parts):
        low = [jnp.where(q % 2 == 0, parts[i], parts[i ^ 1]) for i in range(4)]
        return [jnp.where(q < 2, low[i], low[i ^ 2]) for i in range(4)]

    def flip(v, index, axis):
        first, second = jnp.split(v, 2, axis=axis)
        return jnp.where(index == 0, v, jnp.concatenate([second, first], axis=axis))

    def exchange(block_for):
        return [block_for(0)] + [to_peer(block_for(r), r) for r in (1, 2, 3)]

    def together(*values):
        return lax.optimization_barrier(values)

    def gather_h(v):
        parts = [v]
        for _ in range(nh - 1):
            parts.append(up(parts[-1]))
        return parts

    def square_rows(v):
        return exchange(
            lambda r: lax.dynamic_slice_in_dim(v, (q ^ r) * quarter_d, quarter_d, 1)
        )

    def first_rows(v):
        size = 2 * quarter_d
        mine = lax.dynamic_slice_in_dim(v, q // 2 * size, size, 1)
        other = lax.dynamic_slice_in_dim(v, (1 - q // 2) * size, size, 1)
        return jnp.concatenate([mine, to_peer(other, 2)], axis=0)

    def second_rows(v):
        mine = lax.dynamic_slice_in_dim(v, q % 2 * quarter_d, quarter_d, 1)
        other = lax.dynamic_slice_in_dim(v, (1 - q % 2) * quarter_d, quarter_d, 1)
        return mine, to_peer(other, 1)

    def square_weight(v):
        size = quarter_d // 2 if shared else quarter_d
        first = g * size if shared else 0
        parts = exchange(
            lambda r: lax.dynamic_slice_in_dim(v, (q ^ r) * quarter_d + first, size, 0)
        )
        return parts

    def join_quarters(parts):
        return jnp.concatenate(by_quarter(parts), axis=1)

    def first_weight(v):
        pairs = v.reshape(2, 2, quarter_d, shard)
        mine = lax.dynamic_index_in_dim(pairs, q // 2, 0, keepdims=False)
        other = lax.dynamic_index_in_dim(pairs, 1 - q // 2, 0, keepdims=False)
        return mine, to_peer(other, 2)

    def second_weight(mine, theirs):
        both = jnp.concatenate([mine, theirs], axis=2)
        other = lax.dynamic_index_in_dim(both, 1 - q % 2, 0, keepdims=False)
        return lax.dynamic_index_in_dim(both, q % 2, 0, keepdims=False), to_peer(other, 1)

    def join_steps(mine, theirs):
        return join_quarters([v[:, i * shard : (i + 1) * shard] for i in (0, 1) for v in (mine, theirs)])

    def own_half(v):
        size = quarter_d // 2
        return lax.dynamic_slice_in_dim(v, g * size, size, 0) if shared else v

    def join_rows(mine, theirs):
        return [v[i * tok_rows : (i + 1) * tok_rows] for i in (0, 1) for v in (mine, theirs)]

    def swap_features(v):
        return g_swap(v) if shared else v

    def all_features(v, theirs):
        return flip(jnp.concatenate([v, theirs], axis=0), g, 0) if shared else v

    def project(rows, weights):
        parts = [dot(rows, weight).astype(bf16) for weight in weights]
        part = jnp.concatenate(parts, axis=1).reshape(4, 2, half_rows, latent)
        mine = lax.dynamic_index_in_dim(part, t, 1, keepdims=False)
        return mine, lax.dynamic_index_in_dim(part, 1 - t, 1, keepdims=False)

    def own_latent(parts):
        return jnp.concatenate(turn(jnp.split(add(*parts), nh, axis=1)), axis=1)

    def sum_squares(part):
        if nh == 2:
            return part, up(part)
        total = part[nh - 1]
        for k in range(nh - 2, -1, -1):
            total = add(down(total), part[k])
        return part, jnp.stack(gather_h(total))

    def join_squares(part, theirs):
        rows = [add(part[0], theirs[1]), add(part[1], theirs[0])] if nh == 2 else list(theirs)
        split = [turn(jnp.split(v, nh, axis=1)) for v in rows]
        return jnp.concatenate(split[0] + [v[0] for v in split[1:]], axis=1)

    def square_blocks(part):
        part = flip(jnp.stack([part, t_swap(part)], axis=1), t, 1)
        return jnp.split(part.reshape(4 * tok_rows, -1), 2 * nh - 1, axis=1)

    def products(blocks, rows, weights):
        grad = sum(dot(v, block, TN) for v, block in zip(rows, blocks[:1] + blocks[nh:]))
        whole = sum(dot(block, weight, NT) for block, weight in zip(blocks, weights))
        return grad.astype(bf16), whole.astype(bf16)

    def send_products(grad, whole):
        whole = whole.reshape(4, tok_rows, quarter_d)
        grads = exchange(lambda r: lax.dynamic_slice_in_dim(grad, (q ^ r) * shard, shard, 1))
        return grads, exchange(lambda r: whole[r])

    def join_products(grads, wholes):
        grad = jnp.concatenate(by_quarter(grads), axis=0).astype(f32)
        return jnp.concatenate(by_quarter(wholes), axis=1), grad

    local_ids = own * exp_local + jnp.arange(exp_local, dtype=jnp.int32)
    hit = routes[:, :, None] == local_ids[None, None, :]
    gate_all = jnp.sum(jnp.where(hit, gates[:, :, None], 0), axis=1).astype(f32) * gate_unit
    gate_all = gate_all.reshape(nh, 4, 2, half_rows, exp_local)
    gate_all = jnp.stack(turn(list(gate_all)))
    gate_all = jnp.stack(by_quarter([gate_all[:, i] for i in range(4)]))
    gate_all = flip(gate_all, t, 2)
    gate_columns = gate_all.transpose(2, 0, 1, 3, 4).reshape(-1, exp_local)

    side_rows = n_expert * half_rows
    forward, backward, down_grads, input_grads, gate_blocks = expert_calls(
        side_rows, latent, exp_local, width
    )
    down_rows = down_proj.reshape(exp_local * width, latent)

    down_block = square_weight(down_weight)
    token_rows = first_rows(tokens)
    up_mine, up_theirs = first_weight(up_weight)
    up_mine, up_theirs = second_weight(up_mine, after(up_theirs, *down_block[1:]))
    down_parts = gather_h(join_quarters(down_block))
    theirs = [swap_features(down_parts[0])]
    token_rows, up_theirs, down_parts[-1], theirs[0] = together(
        token_rows, up_theirs, down_parts[-1], theirs[0]
    )
    theirs += [swap_features(v) for v in down_parts[1:]]
    mine, other = second_rows(token_rows)
    cot_rows = first_rows(after(cotangent, token_rows))
    up_block = join_steps(up_mine, up_theirs)
    up_parts = gather_h(own_half(up_block))
    other, cot_rows, theirs[-1], up_parts[-1] = together(
        other, cot_rows, theirs[-1], up_parts[-1]
    )
    token_rows = jnp.concatenate(join_rows(mine, other), axis=0)
    down_parts = [all_features(v, w) for v, w in zip(down_parts, theirs)]

    cot_mine, cot_theirs = second_rows(cot_rows)
    theirs = [swap_features(v) for v in up_parts[1:]]
    mine, other = project(token_rows, down_parts)
    part_x = add(mine, t_swap(other))
    part_x = exchange(lambda r: part_x[r])
    *part_x, cot_theirs, theirs[-1] = together(*part_x, cot_theirs, theirs[-1])
    cot_rows = jnp.concatenate(join_rows(cot_mine, cot_theirs), axis=0)
    up_parts = [up_block] + [all_features(v, w) for v, w in zip(up_parts[1:], theirs)]
    part_x = gather_h(own_latent(part_x))
    mine, other = project(cot_rows, up_parts)
    *part_x, other = together(*part_x, t_swap(other))
    part_x = jnp.stack(part_x)
    part_y = add(mine, other)
    part_x = exchange(lambda r: part_x)
    part_y = exchange(lambda r: part_y[r])
    *part_x, part_y[1], part_y[2], part_y[3] = together(*part_x, *part_y[1:])
    x_own = jnp.stack(part_x).reshape(-1, latent)

    gate_own, gate_other = gate_blocks(gate_columns)
    hs, cp, cu, out_own = forward(x_own, gate_own, gate_proj, up_proj, down_rows)
    part_y = gather_h(own_latent(part_y))
    x_other, part_y[-1], out_own = together(t_swap(x_own), part_y[-1], out_own)
    part_y = jnp.stack(part_y)
    token_parts = gather_h(after(token_rows, x_own))
    hs2, cp2, cu2, out_other = forward(
        after(x_other, out_own), gate_other, gate_proj, up_proj, down_rows
    )
    part_y = exchange(lambda r: part_y)
    *part_y, token_parts[-1], out_other = together(*part_y, token_parts[-1], out_other)
    y_own = jnp.stack(part_y).reshape(-1, latent)
    cot_parts = gather_h(after(cot_rows, y_own))
    dpu, in_own = backward(y_own, cp, cu, gate_proj, up_proj, down_rows)
    y_other, out_other, in_own = together(t_swap(y_own), t_swap(out_other), in_own)
    out_part = add(out_own, out_other).reshape(4, nh, half_rows, latent)
    out_part = exchange(lambda r: out_part[r])
    down_proj_grad = down_grads(hs, hs2, after(y_own, in_own), y_other)
    dpu2, in_other = backward(
        after(y_other, down_proj_grad), cp2, cu2, gate_proj, up_proj, down_rows
    )
    *out_part, cot_parts[-1], in_other = together(*out_part, cot_parts[-1], in_other)
    in_part = add(in_own, t_swap(in_other)).reshape(4, nh, half_rows, latent)
    out_part = add(*out_part)
    gate_proj_grad, up_proj_grad = input_grads(
        x_own, x_other, dpu, after(dpu2, in_part)
    )
    in_part = exchange(lambda r: in_part[r])
    *in_part, out_theirs, gate_proj_grad = together(
        *in_part, sum_squares(out_part)[1], gate_proj_grad
    )
    out_part = join_squares(out_part, out_theirs)
    in_part, in_theirs = sum_squares(add(*in_part))
    out_part = exchange(lambda r: out_part)
    *out_part, in_theirs = together(*out_part, in_theirs)
    out_part = jnp.stack(out_part)
    in_part = join_squares(in_part, in_theirs)
    in_part = jnp.stack(exchange(lambda r: in_part))
    out_sent = send_products(*products(square_blocks(out_part), cot_parts, up_parts))
    in_products = products(square_blocks(in_part), token_parts, down_parts)
    received = together(*out_sent[0], *out_sent[1], *in_products)
    out, up_grad = join_products(received[:4], received[4:8])
    tokens_grad, down_grad = join_products(*send_products(*in_products))
    down_proj_grad = down_proj_grad.reshape(down_proj.shape)
    return (out, tokens_grad, gate_proj_grad, up_proj_grad, down_proj_grad, down_grad, up_grad)


def solution(mesh):
    in_specs = (
        P(("group", "expert"), "tensor"),
        P("tensor", "expert"),
        P("tensor", "expert"),
        P("expert", None, "tensor"),
        P("expert", None, "tensor"),
        P("expert", "tensor", None),
        P("group", None),
        P("group", None),
        P(("group", "expert"), "tensor"),
    )
    out_specs = (
        P(("group", "expert"), "tensor"),
        P(("group", "expert"), "tensor"),
        P(("group", "expert"), None, "tensor"),
        P(("group", "expert"), None, "tensor"),
        P(("group", "expert"), "tensor", None),
        P(("group", "tensor"), "expert"),
        P(("group", "tensor"), "expert"),
    )
    return jax.shard_map(local, mesh=mesh, in_specs=in_specs, out_specs=out_specs, check_vma=False)
```

```python
import jax
import jax.numpy as jnp
from jax import lax
from jax.experimental import pallas as pl
from jax.experimental.pallas import tpu as pltpu
from jax.sharding import PartitionSpec as P

gate_unit = 2.0 ** (-15)
bf16 = jnp.bfloat16
f32 = jnp.float32

NN = (((1,), (0,)), ((), ()))
NT = (((1,), (1,)), ((), ()))
TN = (((0,), (0,)), ((), ()))


def dot(a, b, dims=NN):
    return lax.dot_general(a, b, dims, preferred_element_type=f32)


def join_projections(wg_ref, wu_ref, wgu):
    pair, _, width = wg_ref.shape
    for j in range(pair):
        wgu[:, 2 * j * width : (2 * j + 1) * width] = wg_ref[j]
        wgu[:, (2 * j + 1) * width : (2 * j + 2) * width] = wu_ref[j]


def forward_kernel(
    x_ref, g_ref, wg_ref, wu_ref, wd_ref, hs_ref, cp_ref, cu_ref, lo_ref, wgu, lo_acc
):
    step = pl.program_id(0)
    pair, _, width = wg_ref.shape
    block = 256
    join_projections(wg_ref, wu_ref, wgu)

    @pl.when(step == 0)
    def _():
        lo_acc[...] = jnp.zeros_like(lo_acc)

    for i in range(x_ref.shape[0] // block):
        rows = slice(i * block, (i + 1) * block)
        x = x_ref[rows, :]
        for j in range(pair):
            cols = slice(j * width, (j + 1) * width)
            both = dot(x, wgu[:, 2 * j * width : (2 * j + 2) * width])
            gate_pre, up_pre = both[:, :width], both[:, width:]
            gate = g_ref[0, rows, j : j + 1]
            sig = jax.nn.sigmoid(gate_pre)
            act = gate_pre * sig * gate
            hs_ref[rows, cols] = (act * up_pre).astype(bf16)
            cu_ref[rows, cols] = act.astype(bf16)
            slope = up_pre * (sig * (1.0 + gate_pre * (1.0 - sig)))
            cp_ref[rows, cols] = (slope * gate).astype(bf16)
        lo_acc[rows, :] += dot(hs_ref[rows, :], wd_ref[...])

    @pl.when(step == pl.num_programs(0) - 1)
    def _():
        lo_ref[...] = lo_acc[...].astype(bf16)


def backward_kernel(
    y_ref, cp_ref, cu_ref, wg_ref, wu_ref, wd_ref, dpu_ref, lig_ref, wgu, lig_acc
):
    step = pl.program_id(0)
    pair, _, width = wg_ref.shape
    block = 256
    join_projections(wg_ref, wu_ref, wgu)

    @pl.when(step == 0)
    def _():
        lig_acc[...] = jnp.zeros_like(lig_acc)

    for i in range(y_ref.shape[0] // block):
        rows = slice(i * block, (i + 1) * block)
        hidden_grad = dot(y_ref[rows, :], wd_ref[...], NT)
        for j in range(pair):
            cols = slice(j * width, (j + 1) * width)
            hg = hidden_grad[:, cols]
            dp = hg * cp_ref[rows, cols].astype(f32)
            du = hg * cu_ref[rows, cols].astype(f32)
            dpu_ref[rows, 2 * j * width : (2 * j + 1) * width] = dp.astype(bf16)
            dpu_ref[rows, (2 * j + 1) * width : (2 * j + 2) * width] = du.astype(bf16)
        lig_acc[rows, :] += dot(dpu_ref[rows, :], wgu[...], NT)

    @pl.when(step == pl.num_programs(0) - 1)
    def _():
        lig_ref[...] = lig_acc[...].astype(bf16)


def down_grad_kernel(hs_ref, y_ref, dwd_ref):
    dwd_ref[...] = dot(hs_ref[...], y_ref[...], TN).astype(bf16)


def input_grad_kernel(x_ref, dpu_ref, dwg_ref, dwu_ref):
    pair, latent, width = dwg_ref.shape
    block = 256

    for i in range(latent // block):
        cols = slice(i * block, (i + 1) * block)
        grads = dot(x_ref[:, cols], dpu_ref[...], TN)
        for j in range(pair):
            dwg_ref[j, cols, :] = grads[:, 2 * j * width : (2 * j + 1) * width].astype(bf16)
            dwu_ref[j, cols, :] = grads[:, (2 * j + 1) * width : (2 * j + 2) * width].astype(bf16)


def shaped(*shape):
    return jax.ShapeDtypeStruct(shape, bf16)


def expert_calls(rows, latent, count, width):
    pair = 2 if rows <= 1024 and count % 2 == 0 else 1
    whole = pl.BlockSpec((rows, latent), lambda i: (0, 0))
    col_proj = pl.BlockSpec((pair, latent, width), lambda i: (i, 0, 0))
    row_proj = pl.BlockSpec((pair * width, latent), lambda i: (i, 0))
    hidden = pl.BlockSpec((rows, pair * width), lambda i: (0, i))
    hidden2 = pl.BlockSpec((rows, 2 * pair * width), lambda i: (0, i))
    gate_spec = pl.BlockSpec((1, rows, pair), lambda i: (i, 0, 0))
    joined = pltpu.VMEM((latent, 2 * pair * width), bf16)
    total = pltpu.VMEM((rows, latent), f32)
    units = 2 * rows * latent * width * count
    weight_bytes = 2 * latent * width * count
    hidden_bytes = 2 * rows * width * count
    latent_bytes = 2 * rows * latent

    def call(kernel, ins, outs, out_shape, scratch, parts, moved, exps=0):
        return pl.pallas_call(
            kernel,
            grid=(count // pair,),
            in_specs=ins,
            out_specs=outs,
            out_shape=out_shape,
            scratch_shapes=scratch,
            compiler_params=pltpu.CompilerParams(
                vmem_limit_bytes=(40 if rows <= 1024 else 56) * 1024 * 1024
            ),
            cost_estimate=pl.CostEstimate(
                flops=parts * units, bytes_accessed=moved, transcendentals=exps
            ),
        )

    hid = shaped(rows, count * width)
    lat = shaped(rows, latent)
    col = shaped(count, latent, width)
    forward = call(
        forward_kernel,
        [whole, gate_spec, col_proj, col_proj, row_proj],
        [hidden, hidden, hidden, whole],
        [hid, hid, hid, lat],
        [joined, total],
        3,
        3 * weight_bytes + 3 * hidden_bytes + 2 * latent_bytes,
        rows * width * count,
    )
    backward = call(
        backward_kernel,
        [whole, hidden, hidden, col_proj, col_proj, row_proj],
        [hidden2, whole],
        [shaped(rows, 2 * count * width), lat],
        [joined, total],
        3,
        3 * weight_bytes + 4 * hidden_bytes + 2 * latent_bytes,
    )
    down_grads = call(
        down_grad_kernel,
        [hidden, whole],
        row_proj,
        shaped(count * width, latent),
        [],
        1,
        weight_bytes + hidden_bytes + latent_bytes,
    )
    input_grads = call(
        input_grad_kernel,
        [whole, hidden2],
        [col_proj, col_proj],
        [col, col],
        [],
        2,
        2 * weight_bytes + 2 * hidden_bytes + latent_bytes,
    )

    def gate_blocks(gate_columns):
        return gate_columns.reshape(rows, count // pair, pair).transpose(1, 0, 2)

    return forward, backward, down_grads, input_grads, gate_blocks


def local(tokens, down_weight, up_weight, gate_proj, up_proj, down_proj, routes, gates, cotangent):
    n_expert = lax.axis_size("expert")
    n_group = lax.axis_size("group")
    own = lax.axis_index("expert")
    t = lax.axis_index("tensor")
    tok_rows = tokens.shape[0]
    half_rows = tok_rows // 2
    quarter_d = tokens.shape[1] // 4
    exp_local, latent, width = gate_proj.shape
    shard = down_weight.shape[1]

    nh = n_expert // 4
    h, q = own // 4, own % 4
    cols = latent // nh
    shared = n_group % 2 == 0
    g = lax.axis_index("group") % 2

    def to_peer(v, r):
        return lax.ppermute(v, "expert", [(e, e ^ r) for e in range(n_expert)])

    def t_swap(v):
        return lax.ppermute(v, "tensor", [(0, 1), (1, 0)])

    def g_swap(v):
        return lax.ppermute(v, "group", [(i, i ^ 1) for i in range(n_group)])

    def up(v):
        return lax.ppermute(v, "expert", [(e, (e + 4) % n_expert) for e in range(n_expert)])

    def down(v):
        return lax.ppermute(v, "expert", [((e + 4) % n_expert, e) for e in range(n_expert)])

    def add(*terms):
        return sum(v.astype(f32) for v in terms).astype(bf16)

    def after(v, *done):
        return lax.optimization_barrier((v, *done))[0]

    def turn(blocks):
        result = []
        for k in range(nh):
            block = blocks[-k % nh]
            for i in range(1, nh):
                block = jnp.where(h == i, blocks[(i - k) % nh], block)
            result.append(block)
        return result

    def by_quarter(parts):
        low = [jnp.where(q % 2 == 0, parts[i], parts[i ^ 1]) for i in range(4)]
        return [jnp.where(q < 2, low[i], low[i ^ 2]) for i in range(4)]

    def flip(v, index, axis):
        first, second = jnp.split(v, 2, axis=axis)
        return jnp.where(index == 0, v, jnp.concatenate([second, first], axis=axis))

    def exchange(block_for):
        return [block_for(0)] + [to_peer(block_for(r), r) for r in (1, 2, 3)]

    def together(*values):
        return lax.optimization_barrier(values)

    def gather_h(v):
        parts = [v]
        for _ in range(nh - 1):
            parts.append(up(parts[-1]))
        return parts

    def to_square(v, k, r):
        perm = [(e, (e // 4 + k) % nh * 4 + (e % 4 ^ r)) for e in range(n_expert)]
        return lax.ppermute(v, "expert", perm)

    def pair_rows(v):
        def quarters(i):
            parts = [(2 * j + i) * quarter_d for j in (0, 1)]
            parts = [lax.dynamic_slice_in_dim(v, at, quarter_d, 1) for at in parts]
            return jnp.concatenate(parts, axis=1)

        return quarters(q % 2), to_peer(quarters(1 - q % 2), 1)

    def spread_rows(mine, theirs):
        v = jnp.concatenate([mine, theirs], axis=0)
        mine = lax.dynamic_slice_in_dim(v, q // 2 * quarter_d, quarter_d, 1)
        other = lax.dynamic_slice_in_dim(v, (1 - q // 2) * quarter_d, quarter_d, 1)
        far = [(to_square(mine, k, 0), to_square(other, k, 2)) for k in range(1, nh)]
        return (mine, other), far

    def join_pairs(parts):
        return [jnp.concatenate(v, axis=0) for v in parts]

    def square_weight(v):
        size = quarter_d // 2 if shared else quarter_d
        first = g * size if shared else 0
        parts = exchange(
            lambda r: lax.dynamic_slice_in_dim(v, (q ^ r) * quarter_d + first, size, 0)
        )
        return parts

    def join_quarters(parts):
        return jnp.concatenate(by_quarter(parts), axis=1)

    def swap_features(v):
        return g_swap(v) if shared else v

    def all_features(v, theirs):
        return flip(jnp.concatenate([v, theirs], axis=0), g, 0) if shared else v

    def project(rows, weight):
        parts = [dot(v, weight).astype(bf16).reshape(4, 2, half_rows, cols) for v in rows]
        part = jnp.stack(parts, axis=1)
        mine = lax.dynamic_index_in_dim(part, t, 2, keepdims=False)
        return mine, lax.dynamic_index_in_dim(part, 1 - t, 2, keepdims=False)

    def own_latent(pieces):
        rows = []
        for k in range(nh):
            blocks = turn([pieces[j][(k - j) % nh] for j in range(nh)])
            rows.append(jnp.concatenate(blocks, axis=1))
        return jnp.stack(rows)

    def sum_tensor(part):
        part = part.reshape(2, 4, nh, half_rows, latent)
        return add(part[0], t_swap(part[1]))

    def sum_squares(part):
        if nh == 2:
            return part, up(part)
        total = part[nh - 1]
        for k in range(nh - 2, -1, -1):
            total = add(down(total), part[k])
        return part, jnp.stack(gather_h(total))

    def join_squares(part, theirs):
        rows = [add(part[0], theirs[1]), add(part[1], theirs[0])] if nh == 2 else list(theirs)
        split = [turn(jnp.split(v, nh, axis=1)) for v in rows]
        return jnp.concatenate(split[0] + [v[0] for v in split[1:]], axis=1)

    def square_blocks(part):
        part = flip(jnp.stack([part, t_swap(part)], axis=1), t, 1)
        return jnp.split(part.reshape(4 * tok_rows, -1), 2 * nh - 1, axis=1)

    def products(blocks, rows, weights):
        grad = sum(dot(v, block, TN) for v, block in zip(rows, blocks[:1] + blocks[nh:]))
        whole = sum(dot(block, weight, NT) for block, weight in zip(blocks, weights))
        return grad.astype(bf16), whole.astype(bf16)

    def send_products(grad, whole):
        whole = whole.reshape(4, tok_rows, quarter_d)
        grads = exchange(lambda r: lax.dynamic_slice_in_dim(grad, (q ^ r) * shard, shard, 1))
        return grads, exchange(lambda r: whole[r])

    def join_products(grads, wholes):
        grad = jnp.concatenate(by_quarter(grads), axis=0).astype(f32)
        return jnp.concatenate(by_quarter(wholes), axis=1), grad

    local_ids = own * exp_local + jnp.arange(exp_local, dtype=jnp.int32)
    hit = routes[:, :, None] == local_ids[None, None, :]
    gate_all = jnp.sum(jnp.where(hit, gates[:, :, None], 0), axis=1).astype(f32) * gate_unit
    gate_all = gate_all.reshape(nh, 4, 2, half_rows, exp_local)
    gate_all = jnp.stack(turn(list(gate_all)))
    gate_all = jnp.stack(by_quarter([gate_all[:, i] for i in range(4)]))
    gate_all = flip(gate_all, t, 2)
    gate_columns = gate_all.transpose(2, 0, 1, 3, 4).reshape(-1, exp_local)

    group_rows = n_expert * tok_rows
    forward, backward, down_grads, input_grads, gate_blocks = expert_calls(
        group_rows, latent, exp_local, width
    )
    down_rows = down_proj.reshape(exp_local * width, latent)

    def rows_with(part, theirs):
        return jnp.stack([part, theirs]).reshape(-1, latent)

    tok_mine, tok_theirs = pair_rows(tokens)
    down_half = square_weight(down_weight)
    cot_mine, cot_theirs = pair_rows(after(cotangent, tok_theirs, *down_half[1:]))
    up_half = square_weight(after(up_weight, tok_theirs, *down_half[1:]))
    tok_near, tok_far = spread_rows(tok_mine, tok_theirs)
    *up_half, cot_theirs, near, far, far2 = together(
        *up_half, cot_theirs, to_peer(tok_near[1], 2), *tok_far[-1]
    )
    token_parts = join_pairs([(tok_near[0], near), *tok_far[:-1], (far, far2)])
    cot_near, cot_far = spread_rows(cot_mine, cot_theirs)
    down_half, up_half = join_quarters(down_half), join_quarters(up_half)
    down_own = all_features(down_half, swap_features(down_half))

    mine, other = project(token_parts, down_own)
    part_x = add(mine, t_swap(other))
    part_x = exchange(lambda r: part_x[r])
    sum_x = add(*part_x)
    near = to_peer(after(cot_near[1], sum_x), 2)
    up_own = all_features(up_half, swap_features(after(up_half, sum_x)))
    part_x = gather_h(sum_x)
    part_x[-1], *far = together(part_x[-1], *cot_far[-1])
    cot_parts = join_pairs([(cot_near[0], near), *cot_far[:-1], far])
    part_x = own_latent(part_x)
    part_x = jnp.stack(exchange(lambda r: part_x))
    mine, other = project(cot_parts, up_own)
    part_y = add(mine, t_swap(other))
    part_y = own_latent(gather_h(add(*exchange(lambda r: part_y[r]))))
    part_x = after(part_x, part_y)
    latent_in = rows_with(part_x, t_swap(part_x))
    up_far = gather_h(after(up_half, part_x))[1:]

    hs, cp, cu, out_part = forward(
        latent_in, gate_blocks(gate_columns), gate_proj, up_proj, down_rows
    )
    part_y = exchange(lambda r: part_y)
    *part_y, up_far[-1], out_part = together(*part_y, up_far[-1], out_part)
    part_y = jnp.stack(part_y)
    latent_grad = rows_with(part_y, t_swap(part_y))
    up_theirs = [swap_features(v) for v in up_far]
    down_far = gather_h(after(down_half, up_far[-1]))[1:]
    out_part = sum_tensor(out_part)
    down_proj_grad = down_grads(hs, latent_grad)
    out_part = after(out_part, down_proj_grad)
    dpu, in_part = backward(
        after(latent_grad, out_part), cp, cu, gate_proj, up_proj, down_rows
    )
    out_part = exchange(lambda r: out_part[r])
    *out_part, up_theirs[-1], down_far[-1], in_part = together(
        *out_part, up_theirs[-1], down_far[-1], in_part
    )
    up_parts = [up_own] + [all_features(v, w) for v, w in zip(up_far, up_theirs)]
    down_theirs = [swap_features(v) for v in down_far]
    out_part = add(*out_part)
    in_part = sum_tensor(after(in_part, out_part))
    gate_proj_grad, up_proj_grad = input_grads(latent_in, after(dpu, in_part))
    in_part = exchange(lambda r: in_part[r])
    *in_part, out_theirs, down_theirs[-1], gate_proj_grad = together(
        *in_part, sum_squares(out_part)[1], down_theirs[-1], gate_proj_grad
    )
    down_parts = [down_own] + [all_features(v, w) for v, w in zip(down_far, down_theirs)]
    out_part = join_squares(out_part, out_theirs)
    in_part, in_theirs = sum_squares(add(*in_part))
    out_part = exchange(lambda r: out_part)
    *out_part, in_theirs = together(*out_part, in_theirs)
    out_part = jnp.stack(out_part)
    in_part = join_squares(in_part, in_theirs)
    in_part = jnp.stack(exchange(lambda r: in_part))
    out_sent = send_products(*products(square_blocks(out_part), cot_parts, up_parts))
    in_products = products(square_blocks(in_part), token_parts, down_parts)
    received = together(*out_sent[0], *out_sent[1], *in_products)
    out, up_grad = join_products(received[:4], received[4:8])
    tokens_grad, down_grad = join_products(*send_products(*in_products))
    down_proj_grad = down_proj_grad.reshape(down_proj.shape)
    return (out, tokens_grad, gate_proj_grad, up_proj_grad, down_proj_grad, down_grad, up_grad)


def solution(mesh):
    in_specs = (
        P(("group", "expert"), "tensor"),
        P("tensor", "expert"),
        P("tensor", "expert"),
        P("expert", None, "tensor"),
        P("expert", None, "tensor"),
        P("expert", "tensor", None),
        P("group", None),
        P("group", None),
        P(("group", "expert"), "tensor"),
    )
    out_specs = (
        P(("group", "expert"), "tensor"),
        P(("group", "expert"), "tensor"),
        P(("group", "expert"), None, "tensor"),
        P(("group", "expert"), None, "tensor"),
        P(("group", "expert"), "tensor", None),
        P(("group", "tensor"), "expert"),
        P(("group", "tensor"), "expert"),
    )
    return jax.shard_map(local, mesh=mesh, in_specs=in_specs, out_specs=out_specs, check_vma=False)
```

```python
import jax
import jax.numpy as jnp
from jax import lax
from jax.experimental import pallas as pl
from jax.experimental.pallas import tpu as pltpu
from jax.sharding import PartitionSpec as P

gate_unit = 2.0 ** (-15)
bf16 = jnp.bfloat16
f32 = jnp.float32

NN = (((1,), (0,)), ((), ()))
NT = (((1,), (1,)), ((), ()))
TN = (((0,), (0,)), ((), ()))


def dot(a, b, dims=NN):
    return lax.dot_general(a, b, dims, preferred_element_type=f32)


def join_projections(wg_ref, wu_ref, wgu):
    pair, _, width = wg_ref.shape
    for j in range(pair):
        wgu[:, 2 * j * width : (2 * j + 1) * width] = wg_ref[j]
        wgu[:, (2 * j + 1) * width : (2 * j + 2) * width] = wu_ref[j]


def forward_kernel(
    x_ref, g_ref, wg_ref, wu_ref, wd_ref, hs_ref, cp_ref, cu_ref, lo_ref, wgu, lo_acc
):
    step = pl.program_id(0)
    pair, _, width = wg_ref.shape
    block = 256
    join_projections(wg_ref, wu_ref, wgu)

    @pl.when(step == 0)
    def _():
        lo_acc[...] = jnp.zeros_like(lo_acc)

    for i in range(x_ref.shape[0] // block):
        rows = slice(i * block, (i + 1) * block)
        x = x_ref[rows, :]
        for j in range(pair):
            cols = slice(j * width, (j + 1) * width)
            both = dot(x, wgu[:, 2 * j * width : (2 * j + 2) * width])
            gate_pre, up_pre = both[:, :width], both[:, width:]
            gate = g_ref[0, rows, j : j + 1]
            sig = jax.nn.sigmoid(gate_pre)
            act = gate_pre * sig * gate
            hs_ref[rows, cols] = (act * up_pre).astype(bf16)
            cu_ref[rows, cols] = act.astype(bf16)
            slope = up_pre * (sig * (1.0 + gate_pre * (1.0 - sig)))
            cp_ref[rows, cols] = (slope * gate).astype(bf16)
        lo_acc[rows, :] += dot(hs_ref[rows, :], wd_ref[...])

    @pl.when(step == pl.num_programs(0) - 1)
    def _():
        lo_ref[...] = lo_acc[...].astype(bf16)


def backward_kernel(
    y_ref, cp_ref, cu_ref, wg_ref, wu_ref, wd_ref, dpu_ref, lig_ref, wgu, lig_acc
):
    step = pl.program_id(0)
    pair, _, width = wg_ref.shape
    block = 256
    join_projections(wg_ref, wu_ref, wgu)

    @pl.when(step == 0)
    def _():
        lig_acc[...] = jnp.zeros_like(lig_acc)

    for i in range(y_ref.shape[0] // block):
        rows = slice(i * block, (i + 1) * block)
        hidden_grad = dot(y_ref[rows, :], wd_ref[...], NT)
        for j in range(pair):
            cols = slice(j * width, (j + 1) * width)
            hg = hidden_grad[:, cols]
            dp = hg * cp_ref[rows, cols].astype(f32)
            du = hg * cu_ref[rows, cols].astype(f32)
            dpu_ref[rows, 2 * j * width : (2 * j + 1) * width] = dp.astype(bf16)
            dpu_ref[rows, (2 * j + 1) * width : (2 * j + 2) * width] = du.astype(bf16)
        lig_acc[rows, :] += dot(dpu_ref[rows, :], wgu[...], NT)

    @pl.when(step == pl.num_programs(0) - 1)
    def _():
        lig_ref[...] = lig_acc[...].astype(bf16)


def down_grad_kernel(hs_ref, y_ref, dwd_ref):
    dwd_ref[...] = dot(hs_ref[...], y_ref[...], TN).astype(bf16)


def input_grad_kernel(x_ref, dpu_ref, dwg_ref, dwu_ref):
    pair, latent, width = dwg_ref.shape
    block = 256

    for i in range(latent // block):
        cols = slice(i * block, (i + 1) * block)
        grads = dot(x_ref[:, cols], dpu_ref[...], TN)
        for j in range(pair):
            dwg_ref[j, cols, :] = grads[:, 2 * j * width : (2 * j + 1) * width].astype(bf16)
            dwu_ref[j, cols, :] = grads[:, (2 * j + 1) * width : (2 * j + 2) * width].astype(bf16)


def shaped(*shape):
    return jax.ShapeDtypeStruct(shape, bf16)


def expert_calls(rows, latent, count, width):
    pair = 2 if rows <= 1024 and count % 2 == 0 else 1
    whole = pl.BlockSpec((rows, latent), lambda i: (0, 0))
    col_proj = pl.BlockSpec((pair, latent, width), lambda i: (i, 0, 0))
    row_proj = pl.BlockSpec((pair * width, latent), lambda i: (i, 0))
    hidden = pl.BlockSpec((rows, pair * width), lambda i: (0, i))
    hidden2 = pl.BlockSpec((rows, 2 * pair * width), lambda i: (0, i))
    gate_spec = pl.BlockSpec((1, rows, pair), lambda i: (i, 0, 0))
    joined = pltpu.VMEM((latent, 2 * pair * width), bf16)
    total = pltpu.VMEM((rows, latent), f32)
    units = 2 * rows * latent * width * count
    weight_bytes = 2 * latent * width * count
    hidden_bytes = 2 * rows * width * count
    latent_bytes = 2 * rows * latent

    def call(kernel, ins, outs, out_shape, scratch, parts, moved, exps=0):
        return pl.pallas_call(
            kernel,
            grid=(count // pair,),
            in_specs=ins,
            out_specs=outs,
            out_shape=out_shape,
            scratch_shapes=scratch,
            compiler_params=pltpu.CompilerParams(
                vmem_limit_bytes=(40 if rows <= 1024 else 56) * 1024 * 1024
            ),
            cost_estimate=pl.CostEstimate(
                flops=parts * units, bytes_accessed=moved, transcendentals=exps
            ),
        )

    hid = shaped(rows, count * width)
    lat = shaped(rows, latent)
    col = shaped(count, latent, width)
    forward = call(
        forward_kernel,
        [whole, gate_spec, col_proj, col_proj, row_proj],
        [hidden, hidden, hidden, whole],
        [hid, hid, hid, lat],
        [joined, total],
        3,
        3 * weight_bytes + 3 * hidden_bytes + 2 * latent_bytes,
        rows * width * count,
    )
    backward = call(
        backward_kernel,
        [whole, hidden, hidden, col_proj, col_proj, row_proj],
        [hidden2, whole],
        [shaped(rows, 2 * count * width), lat],
        [joined, total],
        3,
        3 * weight_bytes + 4 * hidden_bytes + 2 * latent_bytes,
    )
    down_grads = call(
        down_grad_kernel,
        [hidden, whole],
        row_proj,
        shaped(count * width, latent),
        [],
        1,
        weight_bytes + hidden_bytes + latent_bytes,
    )
    input_grads = call(
        input_grad_kernel,
        [whole, hidden2],
        [col_proj, col_proj],
        [col, col],
        [],
        2,
        2 * weight_bytes + 2 * hidden_bytes + latent_bytes,
    )

    def gate_blocks(gate_columns):
        return gate_columns.reshape(rows, count // pair, pair).transpose(1, 0, 2)

    return forward, backward, down_grads, input_grads, gate_blocks


def local(tokens, down_weight, up_weight, gate_proj, up_proj, down_proj, routes, gates, cotangent):
    n_expert = lax.axis_size("expert")
    n_group = lax.axis_size("group")
    own = lax.axis_index("expert")
    t = lax.axis_index("tensor")
    tok_rows = tokens.shape[0]
    half_rows = tok_rows // 2
    quarter_d = tokens.shape[1] // 4
    exp_local, latent, width = gate_proj.shape
    shard = down_weight.shape[1]

    nh = n_expert // 4
    h, q = own // 4, own % 4
    cols = latent // nh
    shared = n_group % 2 == 0
    g = lax.axis_index("group") % 2

    def to_peer(v, r):
        return lax.ppermute(v, "expert", [(e, e ^ r) for e in range(n_expert)])

    def t_swap(v):
        return lax.ppermute(v, "tensor", [(0, 1), (1, 0)])

    def g_swap(v):
        return lax.ppermute(v, "group", [(i, i ^ 1) for i in range(n_group)])

    def up(v):
        return lax.ppermute(v, "expert", [(e, (e + 4) % n_expert) for e in range(n_expert)])

    def down(v):
        return lax.ppermute(v, "expert", [((e + 4) % n_expert, e) for e in range(n_expert)])

    def add(*terms):
        return sum(v.astype(f32) for v in terms).astype(bf16)

    def after(v, *done):
        return lax.optimization_barrier((v, *done))[0]

    def turn(blocks):
        result = []
        for k in range(nh):
            block = blocks[-k % nh]
            for i in range(1, nh):
                block = jnp.where(h == i, blocks[(i - k) % nh], block)
            result.append(block)
        return result

    def by_quarter(parts):
        low = [jnp.where(q % 2 == 0, parts[i], parts[i ^ 1]) for i in range(4)]
        return [jnp.where(q < 2, low[i], low[i ^ 2]) for i in range(4)]

    def flip(v, index, axis):
        first, second = jnp.split(v, 2, axis=axis)
        return jnp.where(index == 0, v, jnp.concatenate([second, first], axis=axis))

    def exchange(block_for):
        return [block_for(0)] + [to_peer(block_for(r), r) for r in (1, 2, 3)]

    def together(*values):
        return lax.optimization_barrier(values)

    def gather_h(v):
        parts = [v]
        for _ in range(nh - 1):
            parts.append(up(parts[-1]))
        return parts

    def to_square(v, k, r):
        perm = [(e, (e // 4 + k) % nh * 4 + (e % 4 ^ r)) for e in range(n_expert)]
        return lax.ppermute(v, "expert", perm)

    def pair_rows(v):
        def quarters(i):
            parts = [(2 * j + i) * quarter_d for j in (0, 1)]
            parts = [lax.dynamic_slice_in_dim(v, at, quarter_d, 1) for at in parts]
            return jnp.concatenate(parts, axis=1)

        return quarters(q % 2), to_peer(quarters(1 - q % 2), 1)

    def by_half(mine, theirs):
        v = jnp.concatenate([mine, theirs], axis=0)
        mine = lax.dynamic_slice_in_dim(v, q // 2 * quarter_d, quarter_d, 1)
        return mine, lax.dynamic_slice_in_dim(v, (1 - q // 2) * quarter_d, quarter_d, 1)

    def far_rows(mine, other):
        return [(to_square(mine, k, 0), to_square(other, k, 2)) for k in range(1, nh)]

    def join_pairs(parts):
        return [jnp.concatenate(v, axis=0) for v in parts]

    def square_weight(v):
        size = quarter_d // 2 if shared else quarter_d
        first = g * size if shared else 0
        parts = exchange(
            lambda r: lax.dynamic_slice_in_dim(v, (q ^ r) * quarter_d + first, size, 0)
        )
        return parts

    def join_quarters(parts):
        return jnp.concatenate(by_quarter(parts), axis=1)

    def first_weight(v):
        size = quarter_d // 2 if shared else quarter_d
        first = g * size if shared else 0

        def half(i):
            starts = [(2 * i + j) * quarter_d + first for j in (0, 1)]
            return jnp.stack([lax.dynamic_slice_in_dim(v, at, size, 0) for at in starts])

        return half(q // 2), to_peer(half(1 - q // 2), 2)

    def second_weight(mine, theirs):
        both = jnp.concatenate([mine, theirs], axis=2)
        other = lax.dynamic_index_in_dim(both, 1 - q % 2, 0, keepdims=False)
        return lax.dynamic_index_in_dim(both, q % 2, 0, keepdims=False), to_peer(other, 1)

    def join_steps(mine, theirs):
        return join_quarters([v[:, i * shard : (i + 1) * shard] for i in (0, 1) for v in (mine, theirs)])

    def swap_features(v):
        return g_swap(v) if shared else v

    def all_features(v, theirs):
        return flip(jnp.concatenate([v, theirs], axis=0), g, 0) if shared else v

    def project(rows, weight):
        parts = [dot(v, weight).astype(bf16).reshape(4, 2, half_rows, cols) for v in rows]
        part = jnp.stack(parts, axis=1)
        mine = lax.dynamic_index_in_dim(part, t, 2, keepdims=False)
        return mine, lax.dynamic_index_in_dim(part, 1 - t, 2, keepdims=False)

    def project_square(rows, weights):
        parts = [dot(rows, weight).astype(bf16) for weight in weights]
        part = jnp.concatenate(parts, axis=1).reshape(4, 2, half_rows, latent)
        mine = lax.dynamic_index_in_dim(part, t, 1, keepdims=False)
        return mine, lax.dynamic_index_in_dim(part, 1 - t, 1, keepdims=False)

    def own_latent(pieces):
        rows = []
        for k in range(nh):
            blocks = turn([pieces[j][(k - j) % nh] for j in range(nh)])
            rows.append(jnp.concatenate(blocks, axis=1))
        return jnp.stack(rows)

    def sum_tensor(part):
        part = part.reshape(2, 4, nh, half_rows, latent)
        return add(part[0], t_swap(part[1]))

    def sum_squares(part):
        if nh == 2:
            return part, up(part)
        total = part[nh - 1]
        for k in range(nh - 2, -1, -1):
            total = add(down(total), part[k])
        return part, jnp.stack(gather_h(total))

    def join_squares(part, theirs):
        rows = [add(part[0], theirs[1]), add(part[1], theirs[0])] if nh == 2 else list(theirs)
        split = [turn(jnp.split(v, nh, axis=1)) for v in rows]
        return jnp.concatenate(split[0] + [v[0] for v in split[1:]], axis=1)

    def square_blocks(part):
        part = flip(jnp.stack([part, t_swap(part)], axis=1), t, 1)
        return jnp.split(part.reshape(4 * tok_rows, -1), 2 * nh - 1, axis=1)

    def products(blocks, rows, weights):
        grad = sum(dot(v, block, TN) for v, block in zip(rows, blocks[:1] + blocks[nh:]))
        whole = sum(dot(block, weight, NT) for block, weight in zip(blocks, weights))
        return grad.astype(bf16), whole.astype(bf16)

    def send_products(grad, whole):
        whole = whole.reshape(4, tok_rows, quarter_d)
        grads = exchange(lambda r: lax.dynamic_slice_in_dim(grad, (q ^ r) * shard, shard, 1))
        return grads, exchange(lambda r: whole[r])

    def join_products(grads, wholes):
        grad = jnp.concatenate(by_quarter(grads), axis=0).astype(f32)
        return jnp.concatenate(by_quarter(wholes), axis=1), grad

    local_ids = own * exp_local + jnp.arange(exp_local, dtype=jnp.int32)
    hit = routes[:, :, None] == local_ids[None, None, :]
    gate_all = jnp.sum(jnp.where(hit, gates[:, :, None], 0), axis=1).astype(f32) * gate_unit
    gate_all = gate_all.reshape(nh, 4, 2, half_rows, exp_local)
    gate_all = jnp.stack(turn(list(gate_all)))
    gate_all = jnp.stack(by_quarter([gate_all[:, i] for i in range(4)]))
    gate_all = flip(gate_all, t, 2)
    gate_columns = gate_all.transpose(2, 0, 1, 3, 4).reshape(-1, exp_local)

    group_rows = n_expert * tok_rows
    forward, backward, down_grads, input_grads, gate_blocks = expert_calls(
        group_rows, latent, exp_local, width
    )
    down_rows = down_proj.reshape(exp_local * width, latent)

    def rows_with(part, theirs):
        return jnp.stack([part, theirs]).reshape(-1, latent)

    tok_mine, tok_theirs = pair_rows(tokens)
    down_half = join_quarters(square_weight(down_weight))
    down_theirs = swap_features(down_half)
    first = (tok_theirs, down_theirs)
    up_mine, up_theirs = first_weight(after(up_weight, *first))
    cot_mine, cot_theirs = pair_rows(after(cotangent, *first))
    tok_mine, other = by_half(tok_mine, tok_theirs)
    tok_far = far_rows(tok_mine, other)
    up_mine, up_theirs = second_weight(up_mine, up_theirs)
    cot_mine, cot_other = by_half(cot_mine, cot_theirs)
    near, far, far2, down_theirs, up_theirs, cot_other = together(
        to_peer(other, 2), *tok_far[-1], down_theirs, up_theirs, to_peer(cot_other, 2)
    )
    token_parts = join_pairs([(tok_mine, near), *tok_far[:-1], (far, far2)])
    cot_rows = jnp.concatenate([cot_mine, cot_other], axis=0)
    down_own = all_features(down_half, down_theirs)
    up_halves = gather_h(join_steps(up_mine, up_theirs))

    mine, other = project(token_parts, down_own)
    part_x = add(mine, t_swap(other))
    part_x = exchange(lambda r: part_x[r])
    *part_x, up_halves[-1] = together(*part_x, up_halves[-1])
    part_x = gather_h(add(*part_x))
    up_theirs = [swap_features(v) for v in up_halves]
    part_x[-1], up_theirs[-1] = together(part_x[-1], up_theirs[-1])
    up_parts = [all_features(v, w) for v, w in zip(up_halves, up_theirs)]
    part_x = own_latent(part_x)
    part_x = jnp.stack(exchange(lambda r: part_x))
    mine, other = project_square(cot_rows, up_parts)
    part_y = add(mine, t_swap(other))
    part_y = add(*exchange(lambda r: part_y[r]))
    part_y = jnp.concatenate(turn(jnp.split(part_y, nh, axis=1)), axis=1)
    part_y = jnp.stack(gather_h(part_y))
    part_x = after(part_x, part_y)
    latent_in = rows_with(part_x, t_swap(part_x))
    down_far = gather_h(after(down_half, part_x))[1:]
    cot_first = gather_h(after(cot_rows[: 2 * tok_rows], part_x))

    hs, cp, cu, out_part = forward(
        latent_in, gate_blocks(gate_columns), gate_proj, up_proj, down_rows
    )
    part_y = exchange(lambda r: part_y)
    *part_y, down_far[-1], cot_first[-1], out_part = together(
        *part_y, down_far[-1], cot_first[-1], out_part
    )
    part_y = jnp.stack(part_y)
    latent_grad = rows_with(part_y, t_swap(part_y))
    down_theirs = [swap_features(v) for v in down_far]
    cot_second = gather_h(after(cot_rows[2 * tok_rows :], cot_first[-1]))
    out_part = sum_tensor(out_part)
    down_proj_grad = down_grads(hs, latent_grad)
    out_part = after(out_part, down_proj_grad)
    dpu, in_part = backward(
        after(latent_grad, out_part), cp, cu, gate_proj, up_proj, down_rows
    )
    out_part = exchange(lambda r: out_part[r])
    *out_part, down_theirs[-1], cot_second[-1], in_part = together(
        *out_part, down_theirs[-1], cot_second[-1], in_part
    )
    down_parts = [down_own] + [all_features(v, w) for v, w in zip(down_far, down_theirs)]
    cot_parts = join_pairs(zip(cot_first, cot_second))
    out_part = add(*out_part)
    in_part = sum_tensor(after(in_part, out_part))
    gate_proj_grad, up_proj_grad = input_grads(latent_in, after(dpu, in_part))
    in_part = exchange(lambda r: in_part[r])
    *in_part, out_theirs, gate_proj_grad = together(
        *in_part, sum_squares(out_part)[1], gate_proj_grad
    )
    out_part = join_squares(out_part, out_theirs)
    in_part, in_theirs = sum_squares(add(*in_part))
    out_part = exchange(lambda r: out_part)
    *out_part, in_theirs = together(*out_part, in_theirs)
    out_part = jnp.stack(out_part)
    in_part = join_squares(in_part, in_theirs)
    in_part = jnp.stack(exchange(lambda r: in_part))
    out_sent = send_products(*products(square_blocks(out_part), cot_parts, up_parts))
    in_products = products(square_blocks(in_part), token_parts, down_parts)
    received = together(*out_sent[0], *out_sent[1], *in_products)
    out, up_grad = join_products(received[:4], received[4:8])
    tokens_grad, down_grad = join_products(*send_products(*in_products))
    down_proj_grad = down_proj_grad.reshape(down_proj.shape)
    return (out, tokens_grad, gate_proj_grad, up_proj_grad, down_proj_grad, down_grad, up_grad)


def solution(mesh):
    in_specs = (
        P(("group", "expert"), "tensor"),
        P("tensor", "expert"),
        P("tensor", "expert"),
        P("expert", None, "tensor"),
        P("expert", None, "tensor"),
        P("expert", "tensor", None),
        P("group", None),
        P("group", None),
        P(("group", "expert"), "tensor"),
    )
    out_specs = (
        P(("group", "expert"), "tensor"),
        P(("group", "expert"), "tensor"),
        P(("group", "expert"), None, "tensor"),
        P(("group", "expert"), None, "tensor"),
        P(("group", "expert"), "tensor", None),
        P(("group", "tensor"), "expert"),
        P(("group", "tensor"), "expert"),
    )
    return jax.shard_map(local, mesh=mesh, in_specs=in_specs, out_specs=out_specs, check_vma=False)
```

```python
import jax
import jax.numpy as jnp
from jax import lax
from jax.experimental import pallas as pl
from jax.experimental.pallas import tpu as pltpu
from jax.sharding import PartitionSpec as P

gate_unit = 2.0 ** (-15)
bf16 = jnp.bfloat16
f32 = jnp.float32

NN = (((1,), (0,)), ((), ()))
NT = (((1,), (1,)), ((), ()))
TN = (((0,), (0,)), ((), ()))


def dot(a, b, dims=NN):
    return lax.dot_general(a, b, dims, preferred_element_type=f32)


def join_projections(wg_ref, wu_ref, wgu):
    pair, _, width = wg_ref.shape
    for j in range(pair):
        wgu[:, 2 * j * width : (2 * j + 1) * width] = wg_ref[j]
        wgu[:, (2 * j + 1) * width : (2 * j + 2) * width] = wu_ref[j]


def forward_kernel(
    x_ref, g_ref, wg_ref, wu_ref, wd_ref, hs_ref, cp_ref, cu_ref, lo_ref, wgu, lo_acc
):
    step = pl.program_id(0)
    pair, _, width = wg_ref.shape
    block = 256
    join_projections(wg_ref, wu_ref, wgu)

    @pl.when(step == 0)
    def _():
        lo_acc[...] = jnp.zeros_like(lo_acc)

    for i in range(x_ref.shape[0] // block):
        rows = slice(i * block, (i + 1) * block)
        x = x_ref[rows, :]
        for j in range(pair):
            cols = slice(j * width, (j + 1) * width)
            both = dot(x, wgu[:, 2 * j * width : (2 * j + 2) * width])
            gate_pre, up_pre = both[:, :width], both[:, width:]
            gate = g_ref[0, rows, j : j + 1]
            sig = jax.nn.sigmoid(gate_pre)
            act = gate_pre * sig * gate
            hs_ref[rows, cols] = (act * up_pre).astype(bf16)
            cu_ref[rows, cols] = act.astype(bf16)
            slope = up_pre * (sig * (1.0 + gate_pre * (1.0 - sig)))
            cp_ref[rows, cols] = (slope * gate).astype(bf16)
        lo_acc[rows, :] += dot(hs_ref[rows, :], wd_ref[...])

    @pl.when(step == pl.num_programs(0) - 1)
    def _():
        lo_ref[...] = lo_acc[...].astype(bf16)


def backward_kernel(
    y_ref, cp_ref, cu_ref, wg_ref, wu_ref, wd_ref, dpu_ref, lig_ref, wgu, lig_acc
):
    step = pl.program_id(0)
    pair, _, width = wg_ref.shape
    block = 256
    join_projections(wg_ref, wu_ref, wgu)

    @pl.when(step == 0)
    def _():
        lig_acc[...] = jnp.zeros_like(lig_acc)

    for i in range(y_ref.shape[0] // block):
        rows = slice(i * block, (i + 1) * block)
        hidden_grad = dot(y_ref[rows, :], wd_ref[...], NT)
        for j in range(pair):
            cols = slice(j * width, (j + 1) * width)
            hg = hidden_grad[:, cols]
            dp = hg * cp_ref[rows, cols].astype(f32)
            du = hg * cu_ref[rows, cols].astype(f32)
            dpu_ref[rows, 2 * j * width : (2 * j + 1) * width] = dp.astype(bf16)
            dpu_ref[rows, (2 * j + 1) * width : (2 * j + 2) * width] = du.astype(bf16)
        lig_acc[rows, :] += dot(dpu_ref[rows, :], wgu[...], NT)

    @pl.when(step == pl.num_programs(0) - 1)
    def _():
        lig_ref[...] = lig_acc[...].astype(bf16)


def down_grad_kernel(hs_ref, y_ref, dwd_ref):
    dwd_ref[...] = dot(hs_ref[...], y_ref[...], TN).astype(bf16)


def input_grad_kernel(x_ref, dpu_ref, dwg_ref, dwu_ref):
    pair, latent, width = dwg_ref.shape
    block = 256

    for i in range(latent // block):
        cols = slice(i * block, (i + 1) * block)
        grads = dot(x_ref[:, cols], dpu_ref[...], TN)
        for j in range(pair):
            dwg_ref[j, cols, :] = grads[:, 2 * j * width : (2 * j + 1) * width].astype(bf16)
            dwu_ref[j, cols, :] = grads[:, (2 * j + 1) * width : (2 * j + 2) * width].astype(bf16)


def shaped(*shape):
    return jax.ShapeDtypeStruct(shape, bf16)


def expert_calls(rows, latent, count, width):
    pair = 2 if rows <= 1024 and count % 2 == 0 else 1
    whole = pl.BlockSpec((rows, latent), lambda i: (0, 0))
    col_proj = pl.BlockSpec((pair, latent, width), lambda i: (i, 0, 0))
    row_proj = pl.BlockSpec((pair * width, latent), lambda i: (i, 0))
    hidden = pl.BlockSpec((rows, pair * width), lambda i: (0, i))
    hidden2 = pl.BlockSpec((rows, 2 * pair * width), lambda i: (0, i))
    gate_spec = pl.BlockSpec((1, rows, pair), lambda i: (i, 0, 0))
    joined = pltpu.VMEM((latent, 2 * pair * width), bf16)
    total = pltpu.VMEM((rows, latent), f32)
    units = 2 * rows * latent * width * count
    weight_bytes = 2 * latent * width * count
    hidden_bytes = 2 * rows * width * count
    latent_bytes = 2 * rows * latent

    def call(kernel, ins, outs, out_shape, scratch, parts, moved, exps=0):
        return pl.pallas_call(
            kernel,
            grid=(count // pair,),
            in_specs=ins,
            out_specs=outs,
            out_shape=out_shape,
            scratch_shapes=scratch,
            compiler_params=pltpu.CompilerParams(
                vmem_limit_bytes=(40 if rows <= 1024 else 56) * 1024 * 1024
            ),
            cost_estimate=pl.CostEstimate(
                flops=parts * units, bytes_accessed=moved, transcendentals=exps
            ),
        )

    hid = shaped(rows, count * width)
    lat = shaped(rows, latent)
    col = shaped(count, latent, width)
    forward = call(
        forward_kernel,
        [whole, gate_spec, col_proj, col_proj, row_proj],
        [hidden, hidden, hidden, whole],
        [hid, hid, hid, lat],
        [joined, total],
        3,
        3 * weight_bytes + 3 * hidden_bytes + 2 * latent_bytes,
        rows * width * count,
    )
    backward = call(
        backward_kernel,
        [whole, hidden, hidden, col_proj, col_proj, row_proj],
        [hidden2, whole],
        [shaped(rows, 2 * count * width), lat],
        [joined, total],
        3,
        3 * weight_bytes + 4 * hidden_bytes + 2 * latent_bytes,
    )
    down_grads = call(
        down_grad_kernel,
        [hidden, whole],
        row_proj,
        shaped(count * width, latent),
        [],
        1,
        weight_bytes + hidden_bytes + latent_bytes,
    )
    input_grads = call(
        input_grad_kernel,
        [whole, hidden2],
        [col_proj, col_proj],
        [col, col],
        [],
        2,
        2 * weight_bytes + 2 * hidden_bytes + latent_bytes,
    )

    def gate_blocks(gate_columns):
        return gate_columns.reshape(rows, count // pair, pair).transpose(1, 0, 2)

    return forward, backward, down_grads, input_grads, gate_blocks


def local(tokens, down_weight, up_weight, gate_proj, up_proj, down_proj, routes, gates, cotangent):
    n_expert = lax.axis_size("expert")
    n_group = lax.axis_size("group")
    own = lax.axis_index("expert")
    t = lax.axis_index("tensor")
    tok_rows = tokens.shape[0]
    half_rows = tok_rows // 2
    quarter_d = tokens.shape[1] // 4
    exp_local, latent, width = gate_proj.shape
    shard = down_weight.shape[1]

    nh = n_expert // 4
    h, q = own // 4, own % 4
    cols = latent // nh
    shared = n_group % 2 == 0
    g = lax.axis_index("group") % 2

    def to_peer(v, r):
        return lax.ppermute(v, "expert", [(e, e ^ r) for e in range(n_expert)])

    def t_swap(v):
        return lax.ppermute(v, "tensor", [(0, 1), (1, 0)])

    def g_swap(v):
        return lax.ppermute(v, "group", [(i, i ^ 1) for i in range(n_group)])

    def up(v):
        return lax.ppermute(v, "expert", [(e, (e + 4) % n_expert) for e in range(n_expert)])

    def down(v):
        return lax.ppermute(v, "expert", [((e + 4) % n_expert, e) for e in range(n_expert)])

    def add(*terms):
        return sum(v.astype(f32) for v in terms).astype(bf16)

    def after(v, *done):
        return lax.optimization_barrier((v, *done))[0]

    def turn(blocks):
        result = []
        for k in range(nh):
            block = blocks[-k % nh]
            for i in range(1, nh):
                block = jnp.where(h == i, blocks[(i - k) % nh], block)
            result.append(block)
        return result

    def by_quarter(parts):
        low = [jnp.where(q % 2 == 0, parts[i], parts[i ^ 1]) for i in range(4)]
        return [jnp.where(q < 2, low[i], low[i ^ 2]) for i in range(4)]

    def flip(v, index, axis):
        first, second = jnp.split(v, 2, axis=axis)
        return jnp.where(index == 0, v, jnp.concatenate([second, first], axis=axis))

    def exchange(block_for):
        return [block_for(0)] + [to_peer(block_for(r), r) for r in (1, 2, 3)]

    def together(*values):
        return lax.optimization_barrier(values)

    def gather_h(v):
        parts = [v]
        for _ in range(nh - 1):
            parts.append(up(parts[-1]))
        return parts

    def to_square(v, k, r):
        perm = [(e, (e // 4 + k) % nh * 4 + (e % 4 ^ r)) for e in range(n_expert)]
        return lax.ppermute(v, "expert", perm)

    def pair_rows(v):
        def quarters(i):
            parts = [(2 * j + i) * quarter_d for j in (0, 1)]
            parts = [lax.dynamic_slice_in_dim(v, at, quarter_d, 1) for at in parts]
            return jnp.concatenate(parts, axis=1)

        return quarters(q % 2), to_peer(quarters(1 - q % 2), 1)

    def by_half(v):
        mine = lax.dynamic_slice_in_dim(v, q // 2 * quarter_d, quarter_d, 1)
        return mine, lax.dynamic_slice_in_dim(v, (1 - q // 2) * quarter_d, quarter_d, 1)

    def far_rows(mine, other):
        return [(to_square(mine, k, 0), to_square(other, k, 2)) for k in range(1, nh)]

    def join_pairs(parts):
        return [jnp.concatenate(v, axis=0) for v in parts]

    def square_weight(v):
        size = quarter_d // 2 if shared else quarter_d
        first = g * size if shared else 0
        parts = exchange(
            lambda r: lax.dynamic_slice_in_dim(v, (q ^ r) * quarter_d + first, size, 0)
        )
        return parts

    def join_quarters(parts):
        return jnp.concatenate(by_quarter(parts), axis=1)

    def first_weight(v):
        size = quarter_d // 2 if shared else quarter_d
        first = g * size if shared else 0

        def half(i):
            starts = [(2 * i + j) * quarter_d + first for j in (0, 1)]
            return jnp.stack([lax.dynamic_slice_in_dim(v, at, size, 0) for at in starts])

        return half(q // 2), to_peer(half(1 - q // 2), 2)

    def second_weight(mine, theirs):
        both = jnp.concatenate([mine, theirs], axis=2)
        other = lax.dynamic_index_in_dim(both, 1 - q % 2, 0, keepdims=False)
        return lax.dynamic_index_in_dim(both, q % 2, 0, keepdims=False), to_peer(other, 1)

    def join_steps(mine, theirs):
        return join_quarters([v[:, i * shard : (i + 1) * shard] for i in (0, 1) for v in (mine, theirs)])

    def swap_features(v):
        return g_swap(v) if shared else v

    def all_features(v, theirs):
        return flip(jnp.concatenate([v, theirs], axis=0), g, 0) if shared else v

    def project(rows, weight):
        parts = [dot(v, weight).astype(bf16).reshape(4, 2, half_rows, cols) for v in rows]
        part = jnp.stack(parts, axis=1)
        mine = lax.dynamic_index_in_dim(part, t, 2, keepdims=False)
        return mine, lax.dynamic_index_in_dim(part, 1 - t, 2, keepdims=False)

    def project_square(rows, weights):
        parts = [dot(rows, weight).astype(bf16) for weight in weights]
        part = jnp.concatenate(parts, axis=1).reshape(4, 2, half_rows, latent)
        mine = lax.dynamic_index_in_dim(part, t, 1, keepdims=False)
        return mine, lax.dynamic_index_in_dim(part, 1 - t, 1, keepdims=False)

    def own_latent(pieces):
        rows = []
        for k in range(nh):
            blocks = turn([pieces[j][(k - j) % nh] for j in range(nh)])
            rows.append(jnp.concatenate(blocks, axis=1))
        return jnp.stack(rows)

    def sum_tensor(part):
        part = part.reshape(2, 4, nh, half_rows, latent)
        return add(part[0], t_swap(part[1]))

    def sum_squares(part):
        if nh == 2:
            return part, up(part)
        total = part[nh - 1]
        for k in range(nh - 2, -1, -1):
            total = add(down(total), part[k])
        return part, jnp.stack(gather_h(total))

    def join_squares(part, theirs):
        rows = [add(part[0], theirs[1]), add(part[1], theirs[0])] if nh == 2 else list(theirs)
        split = [turn(jnp.split(v, nh, axis=1)) for v in rows]
        return jnp.concatenate(split[0] + [v[0] for v in split[1:]], axis=1)

    def square_blocks(part):
        part = flip(jnp.stack([part, t_swap(part)], axis=1), t, 1)
        return jnp.split(part.reshape(4 * tok_rows, -1), 2 * nh - 1, axis=1)

    def products(blocks, rows, weights):
        grad = sum(dot(v, block, TN) for v, block in zip(rows, blocks[:1] + blocks[nh:]))
        whole = sum(dot(block, weight, NT) for block, weight in zip(blocks, weights))
        return grad.astype(bf16), whole.astype(bf16)

    def send_products(grad, whole):
        whole = whole.reshape(4, tok_rows, quarter_d)
        grads = exchange(lambda r: lax.dynamic_slice_in_dim(grad, (q ^ r) * shard, shard, 1))
        return grads, exchange(lambda r: whole[r])

    def join_products(grads, wholes):
        grad = jnp.concatenate(by_quarter(grads), axis=0).astype(f32)
        return jnp.concatenate(by_quarter(wholes), axis=1), grad

    local_ids = own * exp_local + jnp.arange(exp_local, dtype=jnp.int32)
    hit = routes[:, :, None] == local_ids[None, None, :]
    gate_all = jnp.sum(jnp.where(hit, gates[:, :, None], 0), axis=1).astype(f32) * gate_unit
    gate_all = gate_all.reshape(nh, 4, 2, half_rows, exp_local)
    gate_all = jnp.stack(turn(list(gate_all)))
    gate_all = jnp.stack(by_quarter([gate_all[:, i] for i in range(4)]))
    gate_all = flip(gate_all, t, 2)
    gate_columns = gate_all.transpose(2, 0, 1, 3, 4).reshape(-1, exp_local)

    group_rows = n_expert * tok_rows
    forward, backward, down_grads, input_grads, gate_blocks = expert_calls(
        group_rows, latent, exp_local, width
    )
    down_rows = down_proj.reshape(exp_local * width, latent)

    def rows_with(part, theirs):
        return jnp.stack([part, theirs]).reshape(-1, latent)

    tok_mine, tok_theirs = pair_rows(tokens)
    mine, other = by_half(tok_mine)
    far = far_rows(mine, other)
    down_half = square_weight(down_weight)
    first = (tok_theirs, *down_half[1:])
    up_mine, up_theirs = first_weight(after(up_weight, *first))
    cot_mine, cot_theirs = pair_rows(after(cotangent, *first))
    mine2, other2 = by_half(tok_theirs)
    near = to_peer(jnp.concatenate([other, other2], axis=0), 2)
    far2 = far_rows(after(mine2, *far[-1]), after(other2, *far[-1]))
    down_half = join_quarters(down_half)
    down_theirs = swap_features(down_half)
    up_mine, up_theirs = second_weight(up_mine, up_theirs)
    cot_mine, cot_other = by_half(jnp.concatenate([cot_mine, cot_theirs], axis=0))
    near, *far2[-1], down_theirs, up_theirs, cot_other = together(
        near, *far2[-1], down_theirs, up_theirs, to_peer(cot_other, 2)
    )
    token_parts = [(mine, mine2, near)] + [
        (a[0], b[0], a[1], b[1]) for a, b in zip(far, far2)
    ]
    token_parts = join_pairs(token_parts)
    cot_rows = jnp.concatenate([cot_mine, cot_other], axis=0)
    down_own = all_features(down_half, down_theirs)
    up_halves = gather_h(join_steps(up_mine, up_theirs))

    mine, other = project(token_parts, down_own)
    part_x = add(mine, t_swap(other))
    part_x = exchange(lambda r: part_x[r])
    *part_x, up_halves[-1] = together(*part_x, up_halves[-1])
    part_x = gather_h(add(*part_x))
    up_theirs = [swap_features(v) for v in up_halves]
    part_x[-1], up_theirs[-1] = together(part_x[-1], up_theirs[-1])
    up_parts = [all_features(v, w) for v, w in zip(up_halves, up_theirs)]
    part_x = own_latent(part_x)
    part_x = jnp.stack(exchange(lambda r: part_x))
    mine, other = project_square(cot_rows, up_parts)
    part_y = add(mine, t_swap(other))
    part_y = add(*exchange(lambda r: part_y[r]))
    part_y = jnp.concatenate(turn(jnp.split(part_y, nh, axis=1)), axis=1)
    part_y = jnp.stack(gather_h(part_y))
    part_x = after(part_x, part_y)
    latent_in = rows_with(part_x, t_swap(part_x))
    cot_first = gather_h(after(cot_rows[: 2 * tok_rows], part_x))

    hs, cp, cu, out_part = forward(
        latent_in, gate_blocks(gate_columns), gate_proj, up_proj, down_rows
    )
    part_y = exchange(lambda r: part_y)
    *part_y, cot_first[-1], out_part = together(*part_y, cot_first[-1], out_part)
    part_y = jnp.stack(part_y)
    latent_grad = rows_with(part_y, t_swap(part_y))
    down_far = gather_h(after(down_half, cot_first[-1]))[1:]
    cot_second = gather_h(after(cot_rows[2 * tok_rows :], cot_first[-1]))
    out_part = sum_tensor(out_part)
    down_proj_grad = down_grads(hs, latent_grad)
    out_part = after(out_part, down_proj_grad)
    dpu, in_part = backward(
        after(latent_grad, out_part), cp, cu, gate_proj, up_proj, down_rows
    )
    out_part = exchange(lambda r: out_part[r])
    *out_part, down_far[-1], cot_second[-1], in_part = together(
        *out_part, down_far[-1], cot_second[-1], in_part
    )
    down_theirs = [swap_features(v) for v in down_far]
    cot_parts = join_pairs(zip(cot_first, cot_second))
    out_part = add(*out_part)
    in_part = sum_tensor(after(in_part, out_part))
    gate_proj_grad, up_proj_grad = input_grads(latent_in, after(dpu, in_part))
    in_part = exchange(lambda r: in_part[r])
    *in_part, out_theirs, down_theirs[-1], gate_proj_grad = together(
        *in_part, sum_squares(out_part)[1], down_theirs[-1], gate_proj_grad
    )
    down_parts = [down_own] + [all_features(v, w) for v, w in zip(down_far, down_theirs)]
    out_part = join_squares(out_part, out_theirs)
    in_part, in_theirs = sum_squares(add(*in_part))
    out_part = exchange(lambda r: out_part)
    *out_part, in_theirs = together(*out_part, in_theirs)
    out_part = jnp.stack(out_part)
    in_part = join_squares(in_part, in_theirs)
    in_part = exchange(lambda r: in_part)
    out_products = products(square_blocks(out_part), cot_parts, up_parts)
    in_part = jnp.stack(together(*in_part, *out_products)[:4])
    out_sent = send_products(*out_products)
    in_products = products(square_blocks(in_part), token_parts, down_parts)
    received = together(*out_sent[0], *out_sent[1], *in_products)
    out, up_grad = join_products(received[:4], received[4:8])
    tokens_grad, down_grad = join_products(*send_products(*in_products))
    down_proj_grad = down_proj_grad.reshape(down_proj.shape)
    return (out, tokens_grad, gate_proj_grad, up_proj_grad, down_proj_grad, down_grad, up_grad)


def solution(mesh):
    in_specs = (
        P(("group", "expert"), "tensor"),
        P("tensor", "expert"),
        P("tensor", "expert"),
        P("expert", None, "tensor"),
        P("expert", None, "tensor"),
        P("expert", "tensor", None),
        P("group", None),
        P("group", None),
        P(("group", "expert"), "tensor"),
    )
    out_specs = (
        P(("group", "expert"), "tensor"),
        P(("group", "expert"), "tensor"),
        P(("group", "expert"), None, "tensor"),
        P(("group", "expert"), None, "tensor"),
        P(("group", "expert"), "tensor", None),
        P(("group", "tensor"), "expert"),
        P(("group", "tensor"), "expert"),
    )
    return jax.shard_map(local, mesh=mesh, in_specs=in_specs, out_specs=out_specs, check_vma=False)
```

```python
import jax
import jax.numpy as jnp
from jax import lax
from jax.experimental import pallas as pl
from jax.experimental.pallas import tpu as pltpu
from jax.sharding import PartitionSpec as P

gate_unit = 2.0 ** (-15)
bf16 = jnp.bfloat16
f32 = jnp.float32

NN = (((1,), (0,)), ((), ()))
NT = (((1,), (1,)), ((), ()))
TN = (((0,), (0,)), ((), ()))


def dot(a, b, dims=NN):
    return lax.dot_general(a, b, dims, preferred_element_type=f32)


def join_projections(wg_ref, wu_ref, wgu):
    pair, _, width = wg_ref.shape
    for j in range(pair):
        wgu[:, 2 * j * width : (2 * j + 1) * width] = wg_ref[j]
        wgu[:, (2 * j + 1) * width : (2 * j + 2) * width] = wu_ref[j]


def forward_kernel(
    x_ref, g_ref, wg_ref, wu_ref, wd_ref, hs_ref, cp_ref, cu_ref, lo_ref, wgu, lo_acc
):
    step = pl.program_id(0)
    pair, _, width = wg_ref.shape
    block = 512
    join_projections(wg_ref, wu_ref, wgu)

    @pl.when(step == 0)
    def _():
        lo_acc[...] = jnp.zeros_like(lo_acc)

    for i in range(x_ref.shape[0] // block):
        rows = slice(i * block, (i + 1) * block)
        x = x_ref[rows, :]
        for j in range(pair):
            cols = slice(j * width, (j + 1) * width)
            both = dot(x, wgu[:, 2 * j * width : (2 * j + 2) * width])
            gate_pre, up_pre = both[:, :width], both[:, width:]
            gate = g_ref[0, rows, j : j + 1]
            sig = jax.nn.sigmoid(gate_pre)
            act = gate_pre * sig * gate
            hs_ref[rows, cols] = (act * up_pre).astype(bf16)
            cu_ref[rows, cols] = act.astype(bf16)
            slope = up_pre * (sig * (1.0 + gate_pre * (1.0 - sig)))
            cp_ref[rows, cols] = (slope * gate).astype(bf16)
        lo_acc[rows, :] += dot(hs_ref[rows, :], wd_ref[...])

    @pl.when(step == pl.num_programs(0) - 1)
    def _():
        lo_ref[...] = lo_acc[...].astype(bf16)


def backward_kernel(
    y_ref, cp_ref, cu_ref, wg_ref, wu_ref, wd_ref, dpu_ref, lig_ref, wgu, lig_acc
):
    step = pl.program_id(0)
    pair, _, width = wg_ref.shape
    block = 512
    join_projections(wg_ref, wu_ref, wgu)

    @pl.when(step == 0)
    def _():
        lig_acc[...] = jnp.zeros_like(lig_acc)

    for i in range(y_ref.shape[0] // block):
        rows = slice(i * block, (i + 1) * block)
        hidden_grad = dot(y_ref[rows, :], wd_ref[...], NT)
        for j in range(pair):
            cols = slice(j * width, (j + 1) * width)
            hg = hidden_grad[:, cols]
            dp = hg * cp_ref[rows, cols].astype(f32)
            du = hg * cu_ref[rows, cols].astype(f32)
            dpu_ref[rows, 2 * j * width : (2 * j + 1) * width] = dp.astype(bf16)
            dpu_ref[rows, (2 * j + 1) * width : (2 * j + 2) * width] = du.astype(bf16)
        lig_acc[rows, :] += dot(dpu_ref[rows, :], wgu[...], NT)

    @pl.when(step == pl.num_programs(0) - 1)
    def _():
        lig_ref[...] = lig_acc[...].astype(bf16)


def down_grad_kernel(hs_ref, y_ref, dwd_ref):
    dwd_ref[...] = dot(hs_ref[...], y_ref[...], TN).astype(bf16)


def input_grad_kernel(x_ref, dpu_ref, dwg_ref, dwu_ref):
    pair, latent, width = dwg_ref.shape
    block = 256

    for i in range(latent // block):
        cols = slice(i * block, (i + 1) * block)
        grads = dot(x_ref[:, cols], dpu_ref[...], TN)
        for j in range(pair):
            dwg_ref[j, cols, :] = grads[:, 2 * j * width : (2 * j + 1) * width].astype(bf16)
            dwu_ref[j, cols, :] = grads[:, (2 * j + 1) * width : (2 * j + 2) * width].astype(bf16)


def shaped(*shape):
    return jax.ShapeDtypeStruct(shape, bf16)


def expert_calls(rows, latent, count, width):
    pair = 2 if rows <= 1024 and count % 2 == 0 else 1
    whole = pl.BlockSpec((rows, latent), lambda i: (0, 0))
    col_proj = pl.BlockSpec((pair, latent, width), lambda i: (i, 0, 0))
    row_proj = pl.BlockSpec((pair * width, latent), lambda i: (i, 0))
    hidden = pl.BlockSpec((rows, pair * width), lambda i: (0, i))
    hidden2 = pl.BlockSpec((rows, 2 * pair * width), lambda i: (0, i))
    gate_spec = pl.BlockSpec((1, rows, pair), lambda i: (i, 0, 0))
    joined = pltpu.VMEM((latent, 2 * pair * width), bf16)
    total = pltpu.VMEM((rows, latent), f32)
    units = 2 * rows * latent * width * count
    weight_bytes = 2 * latent * width * count
    hidden_bytes = 2 * rows * width * count
    latent_bytes = 2 * rows * latent

    def call(kernel, ins, outs, out_shape, scratch, parts, moved, exps=0):
        return pl.pallas_call(
            kernel,
            grid=(count // pair,),
            in_specs=ins,
            out_specs=outs,
            out_shape=out_shape,
            scratch_shapes=scratch,
            compiler_params=pltpu.CompilerParams(
                vmem_limit_bytes=(40 if rows <= 1024 else 56) * 1024 * 1024
            ),
            cost_estimate=pl.CostEstimate(
                flops=parts * units, bytes_accessed=moved, transcendentals=exps
            ),
        )

    hid = shaped(rows, count * width)
    lat = shaped(rows, latent)
    col = shaped(count, latent, width)
    forward = call(
        forward_kernel,
        [whole, gate_spec, col_proj, col_proj, row_proj],
        [hidden, hidden, hidden, whole],
        [hid, hid, hid, lat],
        [joined, total],
        3,
        3 * weight_bytes + 3 * hidden_bytes + 2 * latent_bytes,
        rows * width * count,
    )
    backward = call(
        backward_kernel,
        [whole, hidden, hidden, col_proj, col_proj, row_proj],
        [hidden2, whole],
        [shaped(rows, 2 * count * width), lat],
        [joined, total],
        3,
        3 * weight_bytes + 4 * hidden_bytes + 2 * latent_bytes,
    )
    down_grads = call(
        down_grad_kernel,
        [hidden, whole],
        row_proj,
        shaped(count * width, latent),
        [],
        1,
        weight_bytes + hidden_bytes + latent_bytes,
    )
    input_grads = call(
        input_grad_kernel,
        [whole, hidden2],
        [col_proj, col_proj],
        [col, col],
        [],
        2,
        2 * weight_bytes + 2 * hidden_bytes + latent_bytes,
    )

    def gate_blocks(gate_columns):
        return gate_columns.reshape(rows, count // pair, pair).transpose(1, 0, 2)

    return forward, backward, down_grads, input_grads, gate_blocks


def local(tokens, down_weight, up_weight, gate_proj, up_proj, down_proj, routes, gates, cotangent):
    n_expert = lax.axis_size("expert")
    n_group = lax.axis_size("group")
    own = lax.axis_index("expert")
    t = lax.axis_index("tensor")
    tok_rows = tokens.shape[0]
    half_rows = tok_rows // 2
    quarter_d = tokens.shape[1] // 4
    exp_local, latent, width = gate_proj.shape
    shard = down_weight.shape[1]

    nh = n_expert // 4
    h, q = own // 4, own % 4
    cols = latent // nh
    shared = n_group % 2 == 0
    g = lax.axis_index("group") % 2

    def to_peer(v, r):
        return lax.ppermute(v, "expert", [(e, e ^ r) for e in range(n_expert)])

    def t_swap(v):
        return lax.ppermute(v, "tensor", [(0, 1), (1, 0)])

    def g_swap(v):
        return lax.ppermute(v, "group", [(i, i ^ 1) for i in range(n_group)])

    def up(v):
        return lax.ppermute(v, "expert", [(e, (e + 4) % n_expert) for e in range(n_expert)])

    def down(v):
        return lax.ppermute(v, "expert", [((e + 4) % n_expert, e) for e in range(n_expert)])

    def add(*terms):
        return sum(v.astype(f32) for v in terms).astype(bf16)

    def after(v, *done):
        return lax.optimization_barrier((v, *done))[0]

    def turn(blocks):
        result = []
        for k in range(nh):
            block = blocks[-k % nh]
            for i in range(1, nh):
                block = jnp.where(h == i, blocks[(i - k) % nh], block)
            result.append(block)
        return result

    def by_quarter(parts):
        low = [jnp.where(q % 2 == 0, parts[i], parts[i ^ 1]) for i in range(4)]
        return [jnp.where(q < 2, low[i], low[i ^ 2]) for i in range(4)]

    def flip(v, index, axis):
        first, second = jnp.split(v, 2, axis=axis)
        return jnp.where(index == 0, v, jnp.concatenate([second, first], axis=axis))

    def exchange(block_for):
        return [block_for(0)] + [to_peer(block_for(r), r) for r in (1, 2, 3)]

    def together(*values):
        return lax.optimization_barrier(values)

    def gather_h(v):
        parts = [v]
        for _ in range(nh - 1):
            parts.append(up(parts[-1]))
        return parts

    def to_square(v, k, r):
        perm = [(e, (e // 4 + k) % nh * 4 + (e % 4 ^ r)) for e in range(n_expert)]
        return lax.ppermute(v, "expert", perm)

    def pair_rows(v):
        def quarters(i):
            parts = [(2 * j + i) * quarter_d for j in (0, 1)]
            parts = [lax.dynamic_slice_in_dim(v, at, quarter_d, 1) for at in parts]
            return jnp.concatenate(parts, axis=1)

        return quarters(q % 2), to_peer(quarters(1 - q % 2), 1)

    def by_half(v):
        mine = lax.dynamic_slice_in_dim(v, q // 2 * quarter_d, quarter_d, 1)
        return mine, lax.dynamic_slice_in_dim(v, (1 - q // 2) * quarter_d, quarter_d, 1)

    def far_rows(mine, other):
        return [(to_square(mine, k, 0), to_square(other, k, 2)) for k in range(1, nh)]

    def near_rows(v):
        size = 2 * quarter_d
        mine = lax.dynamic_slice_in_dim(v, q // 2 * size, size, 1)
        other = lax.dynamic_slice_in_dim(v, (1 - q // 2) * size, size, 1)
        return mine, to_peer(other, 2)

    def near_quarters(mine, theirs):
        v = jnp.concatenate([mine, theirs], axis=0)
        mine = lax.dynamic_slice_in_dim(v, q % 2 * quarter_d, quarter_d, 1)
        other = lax.dynamic_slice_in_dim(v, (1 - q % 2) * quarter_d, quarter_d, 1)
        return mine, to_peer(other, 1)

    def join_rows(mine, theirs):
        parts = [v[i * tok_rows : (i + 1) * tok_rows] for i in (0, 1) for v in (mine, theirs)]
        return jnp.concatenate(parts, axis=0)

    def join_pairs(parts):
        return [jnp.concatenate(v, axis=0) for v in parts]

    def square_weight(v):
        size = quarter_d // 2 if shared else quarter_d
        first = g * size if shared else 0
        parts = exchange(
            lambda r: lax.dynamic_slice_in_dim(v, (q ^ r) * quarter_d + first, size, 0)
        )
        return parts

    def join_quarters(parts):
        return jnp.concatenate(by_quarter(parts), axis=1)

    def first_weight(v):
        size = quarter_d // 2 if shared else quarter_d
        first = g * size if shared else 0

        def half(i):
            starts = [(2 * i + j) * quarter_d + first for j in (0, 1)]
            return jnp.stack([lax.dynamic_slice_in_dim(v, at, size, 0) for at in starts])

        return half(q // 2), to_peer(half(1 - q // 2), 2)

    def second_weight(mine, theirs):
        both = jnp.concatenate([mine, theirs], axis=2)
        other = lax.dynamic_index_in_dim(both, 1 - q % 2, 0, keepdims=False)
        return lax.dynamic_index_in_dim(both, q % 2, 0, keepdims=False), to_peer(other, 1)

    def join_steps(mine, theirs):
        return join_quarters([v[:, i * shard : (i + 1) * shard] for i in (0, 1) for v in (mine, theirs)])

    def swap_features(v):
        return g_swap(v) if shared else v

    def all_features(v, theirs):
        return flip(jnp.concatenate([v, theirs], axis=0), g, 0) if shared else v

    def project(rows, weight):
        parts = [dot(v, weight).astype(bf16).reshape(4, 2, half_rows, cols) for v in rows]
        part = jnp.stack(parts, axis=1)
        mine = lax.dynamic_index_in_dim(part, t, 2, keepdims=False)
        return mine, lax.dynamic_index_in_dim(part, 1 - t, 2, keepdims=False)

    def project_square(rows, weights):
        parts = [dot(rows, weight).astype(bf16) for weight in weights]
        part = jnp.concatenate(parts, axis=1).reshape(4, 2, half_rows, latent)
        mine = lax.dynamic_index_in_dim(part, t, 1, keepdims=False)
        return mine, lax.dynamic_index_in_dim(part, 1 - t, 1, keepdims=False)

    def own_latent(pieces):
        rows = []
        for k in range(nh):
            blocks = turn([pieces[j][(k - j) % nh] for j in range(nh)])
            rows.append(jnp.concatenate(blocks, axis=1))
        return jnp.stack(rows)

    def sum_tensor(part):
        part = part.reshape(2, 4, nh, half_rows, latent)
        return add(part[0], t_swap(part[1]))

    def sum_squares(part):
        if nh == 2:
            return part, up(part)
        total = part[nh - 1]
        for k in range(nh - 2, -1, -1):
            total = add(down(total), part[k])
        return part, jnp.stack(gather_h(total))

    def join_squares(part, theirs):
        rows = [add(part[0], theirs[1]), add(part[1], theirs[0])] if nh == 2 else list(theirs)
        split = [turn(jnp.split(v, nh, axis=1)) for v in rows]
        return jnp.concatenate(split[0] + [v[0] for v in split[1:]], axis=1)

    def square_blocks(part):
        part = flip(jnp.stack([part, t_swap(part)], axis=1), t, 1)
        return jnp.split(part.reshape(4 * tok_rows, -1), 2 * nh - 1, axis=1)

    def products(blocks, rows, weights):
        grad = sum(dot(v, block, TN) for v, block in zip(rows, blocks[:1] + blocks[nh:]))
        whole = sum(dot(block, weight, NT) for block, weight in zip(blocks, weights))
        return grad.astype(bf16), whole.astype(bf16)

    def send_products(grad, whole):
        whole = whole.reshape(4, tok_rows, quarter_d)
        grads = exchange(lambda r: lax.dynamic_slice_in_dim(grad, (q ^ r) * shard, shard, 1))
        return grads, exchange(lambda r: whole[r])

    def join_products(grads, wholes):
        grad = jnp.concatenate(by_quarter(grads), axis=0).astype(f32)
        return jnp.concatenate(by_quarter(wholes), axis=1), grad

    local_ids = own * exp_local + jnp.arange(exp_local, dtype=jnp.int32)
    hit = routes[:, :, None] == local_ids[None, None, :]
    gate_all = jnp.sum(jnp.where(hit, gates[:, :, None], 0), axis=1).astype(f32) * gate_unit
    gate_all = gate_all.reshape(nh, 4, 2, half_rows, exp_local)
    gate_all = jnp.stack(turn(list(gate_all)))
    gate_all = jnp.stack(by_quarter([gate_all[:, i] for i in range(4)]))
    gate_all = flip(gate_all, t, 2)
    gate_columns = gate_all.transpose(2, 0, 1, 3, 4).reshape(-1, exp_local)

    group_rows = n_expert * tok_rows
    forward, backward, down_grads, input_grads, gate_blocks = expert_calls(
        group_rows, latent, exp_local, width
    )
    down_rows = down_proj.reshape(exp_local * width, latent)

    def rows_with(part, theirs):
        return jnp.stack([part, theirs]).reshape(-1, latent)

    tok_mine, tok_theirs = pair_rows(tokens)
    mine, other = by_half(tok_mine)
    far = far_rows(mine, other)
    down_half = square_weight(down_weight)
    first = (tok_theirs, *down_half[1:])
    up_mine, up_theirs = first_weight(after(up_weight, *first))
    cot_mine, cot_theirs = near_rows(after(cotangent, *down_half[1:]))
    mine2, other2 = by_half(tok_theirs)
    near = to_peer(jnp.concatenate([other, other2], axis=0), 2)
    far2 = far_rows(after(mine2, *far[-1]), after(other2, *far[-1]))
    down_half = join_quarters(down_half)
    down_theirs = swap_features(down_half)
    up_mine, up_theirs = second_weight(up_mine, up_theirs)
    cot_mine, cot_other = near_quarters(cot_mine, cot_theirs)
    near, *far2[-1], down_theirs, up_theirs, cot_other = together(
        near, *far2[-1], down_theirs, up_theirs, cot_other
    )
    token_parts = [(mine, mine2, near)] + [
        (a[0], b[0], a[1], b[1]) for a, b in zip(far, far2)
    ]
    token_parts = join_pairs(token_parts)
    cot_rows = join_rows(cot_mine, cot_other)
    down_own = all_features(down_half, down_theirs)
    up_halves = gather_h(join_steps(up_mine, up_theirs))

    mine, other = project(token_parts, down_own)
    part_x = add(mine, t_swap(other))
    part_x = exchange(lambda r: part_x[r])
    *part_x, up_halves[-1] = together(*part_x, up_halves[-1])
    part_x = gather_h(add(*part_x))
    up_theirs = [swap_features(v) for v in up_halves]
    part_x[-1], up_theirs[-1] = together(part_x[-1], up_theirs[-1])
    up_parts = [all_features(v, w) for v, w in zip(up_halves, up_theirs)]
    part_x = own_latent(part_x)
    part_x = jnp.stack(exchange(lambda r: part_x))
    mine, other = project_square(cot_rows, up_parts)
    part_y = add(mine, t_swap(other))
    part_y = add(*exchange(lambda r: part_y[r]))
    part_y = jnp.concatenate(turn(jnp.split(part_y, nh, axis=1)), axis=1)
    part_y = jnp.stack(gather_h(part_y))
    part_x = after(part_x, part_y)
    latent_in = rows_with(part_x, t_swap(part_x))
    cot_first = gather_h(after(cot_rows[: 2 * tok_rows], part_x))

    hs, cp, cu, out_part = forward(
        latent_in, gate_blocks(gate_columns), gate_proj, up_proj, down_rows
    )
    part_y = exchange(lambda r: part_y)
    *part_y, cot_first[-1], out_part = together(*part_y, cot_first[-1], out_part)
    part_y = jnp.stack(part_y)
    latent_grad = rows_with(part_y, t_swap(part_y))
    down_far = gather_h(after(down_half, cot_first[-1]))[1:]
    cot_second = gather_h(after(cot_rows[2 * tok_rows :], cot_first[-1]))
    out_part = sum_tensor(out_part)
    dpu, in_part = backward(
        after(latent_grad, out_part), cp, cu, gate_proj, up_proj, down_rows
    )
    out_part = exchange(lambda r: out_part[r])
    *out_part, down_far[-1], cot_second[-1], in_part = together(
        *out_part, down_far[-1], cot_second[-1], in_part
    )
    down_theirs = [swap_features(v) for v in down_far]
    cot_parts = join_pairs(zip(cot_first, cot_second))
    out_part = add(*out_part)
    in_part = sum_tensor(in_part)
    gate_proj_grad, up_proj_grad = input_grads(latent_in, after(dpu, in_part))
    in_part = exchange(lambda r: in_part[r])
    *in_part, out_theirs, down_theirs[-1], gate_proj_grad = together(
        *in_part, sum_squares(out_part)[1], down_theirs[-1], gate_proj_grad
    )
    down_parts = [down_own] + [all_features(v, w) for v, w in zip(down_far, down_theirs)]
    out_part = join_squares(out_part, out_theirs)
    in_part, in_theirs = sum_squares(add(*in_part))
    out_part = exchange(lambda r: out_part)
    down_proj_grad = down_grads(hs, after(latent_grad, in_part))
    *out_part, in_theirs, down_proj_grad = together(*out_part, in_theirs, down_proj_grad)
    out_part = jnp.stack(out_part)
    in_part = join_squares(in_part, in_theirs)
    in_part = exchange(lambda r: in_part)
    out_products = products(square_blocks(out_part), cot_parts, up_parts)
    in_part = jnp.stack(together(*in_part, *out_products)[:4])
    out_sent = send_products(*out_products)
    in_products = products(square_blocks(in_part), token_parts, down_parts)
    received = together(*out_sent[0], *out_sent[1], *in_products)
    out, up_grad = join_products(received[:4], received[4:8])
    tokens_grad, down_grad = join_products(*send_products(*in_products))
    down_proj_grad = down_proj_grad.reshape(down_proj.shape)
    return (out, tokens_grad, gate_proj_grad, up_proj_grad, down_proj_grad, down_grad, up_grad)


def solution(mesh):
    in_specs = (
        P(("group", "expert"), "tensor"),
        P("tensor", "expert"),
        P("tensor", "expert"),
        P("expert", None, "tensor"),
        P("expert", None, "tensor"),
        P("expert", "tensor", None),
        P("group", None),
        P("group", None),
        P(("group", "expert"), "tensor"),
    )
    out_specs = (
        P(("group", "expert"), "tensor"),
        P(("group", "expert"), "tensor"),
        P(("group", "expert"), None, "tensor"),
        P(("group", "expert"), None, "tensor"),
        P(("group", "expert"), "tensor", None),
        P(("group", "tensor"), "expert"),
        P(("group", "tensor"), "expert"),
    )
    return jax.shard_map(local, mesh=mesh, in_specs=in_specs, out_specs=out_specs, check_vma=False)
```

```python
import jax
import jax.numpy as jnp
from jax import lax
from jax.experimental import pallas as pl
from jax.experimental.pallas import tpu as pltpu
from jax.sharding import PartitionSpec as P

gate_unit = 2.0 ** (-15)
bf16 = jnp.bfloat16
f32 = jnp.float32

NN = (((1,), (0,)), ((), ()))
NT = (((1,), (1,)), ((), ()))
TN = (((0,), (0,)), ((), ()))


def dot(a, b, dims=NN):
    return lax.dot_general(a, b, dims, preferred_element_type=f32)


def join_projections(wg_ref, wu_ref, wgu):
    pair, _, width = wg_ref.shape
    for j in range(pair):
        wgu[:, 2 * j * width : (2 * j + 1) * width] = wg_ref[j]
        wgu[:, (2 * j + 1) * width : (2 * j + 2) * width] = wu_ref[j]


def forward_kernel(
    x_ref, g_ref, wg_ref, wu_ref, wd_ref, hs_ref, cp_ref, cu_ref, lo_ref, wgu, lo_acc
):
    step = pl.program_id(0)
    pair, _, width = wg_ref.shape
    block = 512
    join_projections(wg_ref, wu_ref, wgu)

    @pl.when(step == 0)
    def _():
        lo_acc[...] = jnp.zeros_like(lo_acc)

    for i in range(x_ref.shape[0] // block):
        rows = slice(i * block, (i + 1) * block)
        x = x_ref[rows, :]
        for j in range(pair):
            cols = slice(j * width, (j + 1) * width)
            both = dot(x, wgu[:, 2 * j * width : (2 * j + 2) * width])
            gate_pre, up_pre = both[:, :width], both[:, width:]
            gate = g_ref[0, rows, j : j + 1]
            sig = jax.nn.sigmoid(gate_pre)
            act = gate_pre * sig * gate
            hs_ref[rows, cols] = (act * up_pre).astype(bf16)
            cu_ref[rows, cols] = act.astype(bf16)
            slope = up_pre * (sig * (1.0 + gate_pre * (1.0 - sig)))
            cp_ref[rows, cols] = (slope * gate).astype(bf16)
        lo_acc[rows, :] += dot(hs_ref[rows, :], wd_ref[...])

    @pl.when(step == pl.num_programs(0) - 1)
    def _():
        lo_ref[...] = lo_acc[...].astype(bf16)


def backward_kernel(
    y_ref, cp_ref, cu_ref, wg_ref, wu_ref, wd_ref, dpu_ref, lig_ref, wgu, lig_acc
):
    step = pl.program_id(0)
    pair, _, width = wg_ref.shape
    block = 512
    join_projections(wg_ref, wu_ref, wgu)

    @pl.when(step == 0)
    def _():
        lig_acc[...] = jnp.zeros_like(lig_acc)

    for i in range(y_ref.shape[0] // block):
        rows = slice(i * block, (i + 1) * block)
        hidden_grad = dot(y_ref[rows, :], wd_ref[...], NT)
        for j in range(pair):
            cols = slice(j * width, (j + 1) * width)
            hg = hidden_grad[:, cols]
            dp = hg * cp_ref[rows, cols].astype(f32)
            du = hg * cu_ref[rows, cols].astype(f32)
            dpu_ref[rows, 2 * j * width : (2 * j + 1) * width] = dp.astype(bf16)
            dpu_ref[rows, (2 * j + 1) * width : (2 * j + 2) * width] = du.astype(bf16)
        lig_acc[rows, :] += dot(dpu_ref[rows, :], wgu[...], NT)

    @pl.when(step == pl.num_programs(0) - 1)
    def _():
        lig_ref[...] = lig_acc[...].astype(bf16)


def down_grad_kernel(hs_ref, y_ref, dwd_ref):
    dwd_ref[...] = dot(hs_ref[...], y_ref[...], TN).astype(bf16)


def input_grad_kernel(x_ref, dpu_ref, dwg_ref, dwu_ref):
    pair, latent, width = dwg_ref.shape
    block = 256

    for i in range(latent // block):
        cols = slice(i * block, (i + 1) * block)
        grads = dot(x_ref[:, cols], dpu_ref[...], TN)
        for j in range(pair):
            dwg_ref[j, cols, :] = grads[:, 2 * j * width : (2 * j + 1) * width].astype(bf16)
            dwu_ref[j, cols, :] = grads[:, (2 * j + 1) * width : (2 * j + 2) * width].astype(bf16)


def shaped(*shape):
    return jax.ShapeDtypeStruct(shape, bf16)


def expert_calls(rows, latent, count, width):
    pair = 2 if rows <= 1024 and count % 2 == 0 else 1
    whole = pl.BlockSpec((rows, latent), lambda i: (0, 0))
    col_proj = pl.BlockSpec((pair, latent, width), lambda i: (i, 0, 0))
    row_proj = pl.BlockSpec((pair * width, latent), lambda i: (i, 0))
    hidden = pl.BlockSpec((rows, pair * width), lambda i: (0, i))
    hidden2 = pl.BlockSpec((rows, 2 * pair * width), lambda i: (0, i))
    gate_spec = pl.BlockSpec((1, rows, pair), lambda i: (i, 0, 0))
    joined = pltpu.VMEM((latent, 2 * pair * width), bf16)
    total = pltpu.VMEM((rows, latent), f32)
    units = 2 * rows * latent * width * count
    weight_bytes = 2 * latent * width * count
    hidden_bytes = 2 * rows * width * count
    latent_bytes = 2 * rows * latent

    def call(kernel, ins, outs, out_shape, scratch, parts, moved, exps=0):
        return pl.pallas_call(
            kernel,
            grid=(count // pair,),
            in_specs=ins,
            out_specs=outs,
            out_shape=out_shape,
            scratch_shapes=scratch,
            compiler_params=pltpu.CompilerParams(
                vmem_limit_bytes=(40 if rows <= 1024 else 56) * 1024 * 1024
            ),
            cost_estimate=pl.CostEstimate(
                flops=parts * units, bytes_accessed=moved, transcendentals=exps
            ),
        )

    hid = shaped(rows, count * width)
    lat = shaped(rows, latent)
    col = shaped(count, latent, width)
    forward = call(
        forward_kernel,
        [whole, gate_spec, col_proj, col_proj, row_proj],
        [hidden, hidden, hidden, whole],
        [hid, hid, hid, lat],
        [joined, total],
        3,
        3 * weight_bytes + 3 * hidden_bytes + 2 * latent_bytes,
        rows * width * count,
    )
    backward = call(
        backward_kernel,
        [whole, hidden, hidden, col_proj, col_proj, row_proj],
        [hidden2, whole],
        [shaped(rows, 2 * count * width), lat],
        [joined, total],
        3,
        3 * weight_bytes + 4 * hidden_bytes + 2 * latent_bytes,
    )
    down_grads = call(
        down_grad_kernel,
        [hidden, whole],
        row_proj,
        shaped(count * width, latent),
        [],
        1,
        weight_bytes + hidden_bytes + latent_bytes,
    )
    input_grads = call(
        input_grad_kernel,
        [whole, hidden2],
        [col_proj, col_proj],
        [col, col],
        [],
        2,
        2 * weight_bytes + 2 * hidden_bytes + latent_bytes,
    )

    def gate_blocks(gate_columns):
        return gate_columns.reshape(rows, count // pair, pair).transpose(1, 0, 2)

    return forward, backward, down_grads, input_grads, gate_blocks


def local(tokens, down_weight, up_weight, gate_proj, up_proj, down_proj, routes, gates, cotangent):
    n_expert = lax.axis_size("expert")
    n_group = lax.axis_size("group")
    own = lax.axis_index("expert")
    t = lax.axis_index("tensor")
    tok_rows = tokens.shape[0]
    half_rows = tok_rows // 2
    quarter_d = tokens.shape[1] // 4
    exp_local, latent, width = gate_proj.shape
    shard = down_weight.shape[1]

    nh = n_expert // 4
    h, q = own // 4, own % 4
    cols = latent // nh
    shared = n_group % 2 == 0
    g = lax.axis_index("group") % 2

    def to_peer(v, r):
        return lax.ppermute(v, "expert", [(e, e ^ r) for e in range(n_expert)])

    def t_swap(v):
        return lax.ppermute(v, "tensor", [(0, 1), (1, 0)])

    def g_swap(v):
        return lax.ppermute(v, "group", [(i, i ^ 1) for i in range(n_group)])

    def up(v):
        return lax.ppermute(v, "expert", [(e, (e + 4) % n_expert) for e in range(n_expert)])

    def down(v):
        return lax.ppermute(v, "expert", [((e + 4) % n_expert, e) for e in range(n_expert)])

    def add(*terms):
        return sum(v.astype(f32) for v in terms).astype(bf16)

    def after(v, *done):
        return lax.optimization_barrier((v, *done))[0]

    def turn(blocks):
        result = []
        for k in range(nh):
            block = blocks[-k % nh]
            for i in range(1, nh):
                block = jnp.where(h == i, blocks[(i - k) % nh], block)
            result.append(block)
        return result

    def by_quarter(parts):
        low = [jnp.where(q % 2 == 0, parts[i], parts[i ^ 1]) for i in range(4)]
        return [jnp.where(q < 2, low[i], low[i ^ 2]) for i in range(4)]

    def flip(v, index, axis):
        first, second = jnp.split(v, 2, axis=axis)
        return jnp.where(index == 0, v, jnp.concatenate([second, first], axis=axis))

    def exchange(block_for):
        return [block_for(0)] + [to_peer(block_for(r), r) for r in (1, 2, 3)]

    def together(*values):
        return lax.optimization_barrier(values)

    def gather_h(v):
        parts = [v]
        for _ in range(nh - 1):
            parts.append(up(parts[-1]))
        return parts

    def to_square(v, k, r):
        perm = [(e, (e // 4 + k) % nh * 4 + (e % 4 ^ r)) for e in range(n_expert)]
        return lax.ppermute(v, "expert", perm)

    def pair_rows(v):
        def quarters(i):
            parts = [(2 * j + i) * quarter_d for j in (0, 1)]
            parts = [lax.dynamic_slice_in_dim(v, at, quarter_d, 1) for at in parts]
            return jnp.concatenate(parts, axis=1)

        return quarters(q % 2), to_peer(quarters(1 - q % 2), 1)

    def by_half(v):
        mine = lax.dynamic_slice_in_dim(v, q // 2 * quarter_d, quarter_d, 1)
        return mine, lax.dynamic_slice_in_dim(v, (1 - q // 2) * quarter_d, quarter_d, 1)

    def far_rows(mine, other):
        return [(to_square(mine, k, 0), to_square(other, k, 2)) for k in range(1, nh)]

    def near_rows(v):
        size = 2 * quarter_d
        mine = lax.dynamic_slice_in_dim(v, q // 2 * size, size, 1)
        other = lax.dynamic_slice_in_dim(v, (1 - q // 2) * size, size, 1)
        return mine, to_peer(other, 2)

    def near_quarters(mine, theirs):
        v = jnp.concatenate([mine, theirs], axis=0)
        mine = lax.dynamic_slice_in_dim(v, q % 2 * quarter_d, quarter_d, 1)
        other = lax.dynamic_slice_in_dim(v, (1 - q % 2) * quarter_d, quarter_d, 1)
        return mine, to_peer(other, 1)

    def join_rows(mine, theirs):
        parts = [v[i * tok_rows : (i + 1) * tok_rows] for i in (0, 1) for v in (mine, theirs)]
        return jnp.concatenate(parts, axis=0)

    def join_pairs(parts):
        return [jnp.concatenate(v, axis=0) for v in parts]

    def square_weight(v):
        size = quarter_d // 2 if shared else quarter_d
        first = g * size if shared else 0
        parts = exchange(
            lambda r: lax.dynamic_slice_in_dim(v, (q ^ r) * quarter_d + first, size, 0)
        )
        return parts

    def join_quarters(parts):
        return jnp.concatenate(by_quarter(parts), axis=1)

    def first_weight(v):
        size = quarter_d // 2 if shared else quarter_d
        first = g * size if shared else 0

        def half(i):
            starts = [(2 * i + j) * quarter_d + first for j in (0, 1)]
            return jnp.stack([lax.dynamic_slice_in_dim(v, at, size, 0) for at in starts])

        return half(q // 2), to_peer(half(1 - q // 2), 2)

    def second_weight(mine, theirs):
        both = jnp.concatenate([mine, theirs], axis=2)
        other = lax.dynamic_index_in_dim(both, 1 - q % 2, 0, keepdims=False)
        return lax.dynamic_index_in_dim(both, q % 2, 0, keepdims=False), to_peer(other, 1)

    def join_steps(mine, theirs):
        return join_quarters([v[:, i * shard : (i + 1) * shard] for i in (0, 1) for v in (mine, theirs)])

    def swap_features(v):
        return g_swap(v) if shared else v

    def all_features(v, theirs):
        return flip(jnp.concatenate([v, theirs], axis=0), g, 0) if shared else v

    def project(rows, weight):
        parts = [dot(v, weight).astype(bf16).reshape(4, 2, half_rows, cols) for v in rows]
        part = jnp.stack(parts, axis=1)
        mine = lax.dynamic_index_in_dim(part, t, 2, keepdims=False)
        return mine, lax.dynamic_index_in_dim(part, 1 - t, 2, keepdims=False)

    def project_square(rows, weights):
        parts = [dot(rows, weight).astype(bf16) for weight in weights]
        part = jnp.concatenate(parts, axis=1).reshape(4, 2, half_rows, latent)
        mine = lax.dynamic_index_in_dim(part, t, 1, keepdims=False)
        return mine, lax.dynamic_index_in_dim(part, 1 - t, 1, keepdims=False)

    def own_latent(pieces):
        rows = []
        for k in range(nh):
            blocks = turn([pieces[j][(k - j) % nh] for j in range(nh)])
            rows.append(jnp.concatenate(blocks, axis=1))
        return jnp.stack(rows)

    def sum_tensor(part):
        part = part.reshape(2, 4, nh, half_rows, latent)
        return add(part[0], t_swap(part[1]))

    def sum_squares(part):
        if nh == 2:
            return part, up(part)
        total = part[nh - 1]
        for k in range(nh - 2, -1, -1):
            total = add(down(total), part[k])
        return part, jnp.stack(gather_h(total))

    def join_squares(part, theirs):
        rows = [add(part[0], theirs[1]), add(part[1], theirs[0])] if nh == 2 else list(theirs)
        split = [turn(jnp.split(v, nh, axis=1)) for v in rows]
        return jnp.concatenate(split[0] + [v[0] for v in split[1:]], axis=1)

    def square_blocks(part):
        part = flip(jnp.stack([part, t_swap(part)], axis=1), t, 1)
        return jnp.split(part.reshape(4 * tok_rows, -1), 2 * nh - 1, axis=1)

    def products(blocks, rows, weights):
        grad = sum(dot(v, block, TN) for v, block in zip(rows, blocks[:1] + blocks[nh:]))
        whole = sum(dot(block, weight, NT) for block, weight in zip(blocks, weights))
        return grad.astype(bf16), whole.astype(bf16)

    def send_products(grad, whole):
        slabs = [whole[:, i : i + shard] for i in range(0, quarter_d, shard)]
        slabs = jnp.stack([v.reshape(4, tok_rows, shard) for v in slabs], axis=1)
        slabs = slabs.reshape(4, -1, shard)

        def block_for(r):
            part = lax.dynamic_slice_in_dim(grad, (q ^ r) * shard, shard, 1)
            return jnp.concatenate([part, slabs[r]], axis=0)

        return exchange(block_for)

    def join_products(parts):
        grad = jnp.concatenate(by_quarter([v[:quarter_d] for v in parts]), axis=0).astype(f32)
        wholes = by_quarter([v[quarter_d:] for v in parts])
        slabs = [v[i : i + tok_rows] for v in wholes for i in range(0, v.shape[0], tok_rows)]
        return jnp.concatenate(slabs, axis=1), grad

    local_ids = own * exp_local + jnp.arange(exp_local, dtype=jnp.int32)
    hit = routes[:, :, None] == local_ids[None, None, :]
    gate_all = jnp.sum(jnp.where(hit, gates[:, :, None], 0), axis=1).astype(f32) * gate_unit
    gate_all = gate_all.reshape(nh, 4, 2, half_rows, exp_local)
    gate_all = jnp.stack(turn(list(gate_all)))
    gate_all = jnp.stack(by_quarter([gate_all[:, i] for i in range(4)]))
    gate_all = flip(gate_all, t, 2)
    gate_columns = gate_all.transpose(2, 0, 1, 3, 4).reshape(-1, exp_local)

    group_rows = n_expert * tok_rows
    forward, backward, down_grads, input_grads, gate_blocks = expert_calls(
        group_rows, latent, exp_local, width
    )
    down_rows = down_proj.reshape(exp_local * width, latent)

    def rows_with(part, theirs):
        return jnp.stack([part, theirs]).reshape(-1, latent)

    tok_mine, tok_theirs = pair_rows(tokens)
    mine, other = by_half(tok_mine)
    far = far_rows(mine, other)
    down_half = square_weight(after(down_weight, tok_theirs))
    first = (tok_theirs, *down_half[1:])
    up_mine, up_theirs = first_weight(after(up_weight, *first))
    cot_mine, cot_theirs = near_rows(after(cotangent, tok_theirs))
    mine2, other2 = by_half(tok_theirs)
    near = to_peer(jnp.concatenate([other, other2], axis=0), 2)
    far2 = far_rows(after(mine2, *far[-1]), after(other2, *far[-1]))
    down_half = join_quarters(down_half)
    down_theirs = swap_features(down_half)
    up_mine, up_theirs = second_weight(up_mine, up_theirs)
    cot_mine, cot_other = near_quarters(cot_mine, cot_theirs)
    near, *far2[-1], down_theirs, up_theirs, cot_other = together(
        near, *far2[-1], down_theirs, up_theirs, cot_other
    )
    token_parts = [(mine, mine2, near)] + [
        (a[0], b[0], a[1], b[1]) for a, b in zip(far, far2)
    ]
    token_parts = join_pairs(token_parts)
    cot_rows = join_rows(cot_mine, cot_other)
    down_own = all_features(down_half, down_theirs)
    up_halves = gather_h(join_steps(up_mine, up_theirs))

    mine, other = project(token_parts, down_own)
    part_x = add(mine, t_swap(other))
    part_x = exchange(lambda r: part_x[r])
    *part_x, up_halves[-1] = together(*part_x, up_halves[-1])
    part_x = gather_h(add(*part_x))
    up_theirs = [swap_features(v) for v in up_halves]
    part_x[-1], up_theirs[-1] = together(part_x[-1], up_theirs[-1])
    up_parts = [all_features(v, w) for v, w in zip(up_halves, up_theirs)]
    part_x = own_latent(part_x)
    part_x = jnp.stack(exchange(lambda r: part_x))
    mine, other = project_square(cot_rows, up_parts)
    part_y = add(mine, t_swap(other))
    part_y = add(*exchange(lambda r: part_y[r]))
    part_y = jnp.concatenate(turn(jnp.split(part_y, nh, axis=1)), axis=1)
    part_y = jnp.stack(gather_h(part_y))
    part_x = after(part_x, part_y)
    latent_in = rows_with(part_x, t_swap(part_x))
    cot_first = gather_h(after(cot_rows[: 2 * tok_rows], part_x))

    hs, cp, cu, out_part = forward(
        latent_in, gate_blocks(gate_columns), gate_proj, up_proj, down_rows
    )
    part_y = exchange(lambda r: part_y)
    *part_y, cot_first[-1], out_part = together(*part_y, cot_first[-1], out_part)
    part_y = jnp.stack(part_y)
    latent_grad = rows_with(part_y, t_swap(part_y))
    down_far = gather_h(after(down_half, cot_first[-1]))[1:]
    cot_second = gather_h(after(cot_rows[2 * tok_rows :], cot_first[-1]))
    out_part = sum_tensor(out_part)
    dpu, in_part = backward(
        after(latent_grad, out_part), cp, cu, gate_proj, up_proj, down_rows
    )
    out_part = exchange(lambda r: out_part[r])
    *out_part, down_far[-1], cot_second[-1], in_part = together(
        *out_part, down_far[-1], cot_second[-1], in_part
    )
    down_theirs = [swap_features(v) for v in down_far]
    cot_parts = join_pairs(zip(cot_first, cot_second))
    out_part = add(*out_part)
    in_part = sum_tensor(in_part)
    gate_proj_grad, up_proj_grad = input_grads(latent_in, after(dpu, in_part))
    in_part = exchange(lambda r: in_part[r])
    *in_part, out_theirs, down_theirs[-1], gate_proj_grad = together(
        *in_part, sum_squares(out_part)[1], down_theirs[-1], gate_proj_grad
    )
    down_parts = [down_own] + [all_features(v, w) for v, w in zip(down_far, down_theirs)]
    out_part = join_squares(out_part, out_theirs)
    in_part, in_theirs = sum_squares(add(*in_part))
    out_part = exchange(lambda r: out_part)
    down_proj_grad = down_grads(hs, after(latent_grad, in_part))
    *out_part, in_theirs, down_proj_grad = together(*out_part, in_theirs, down_proj_grad)
    out_part = jnp.stack(out_part)
    in_part = join_squares(in_part, in_theirs)
    in_part = exchange(lambda r: in_part)
    out_products = products(square_blocks(out_part), cot_parts, up_parts)
    in_part = jnp.stack(together(*in_part, *out_products)[:4])
    out_sent = send_products(*out_products)
    in_products = products(square_blocks(in_part), token_parts, down_parts)
    received = together(*out_sent, *in_products)
    out, up_grad = join_products(received[:4])
    tokens_grad, down_grad = join_products(send_products(*in_products))
    down_proj_grad = down_proj_grad.reshape(down_proj.shape)
    return (out, tokens_grad, gate_proj_grad, up_proj_grad, down_proj_grad, down_grad, up_grad)


def solution(mesh):
    in_specs = (
        P(("group", "expert"), "tensor"),
        P("tensor", "expert"),
        P("tensor", "expert"),
        P("expert", None, "tensor"),
        P("expert", None, "tensor"),
        P("expert", "tensor", None),
        P("group", None),
        P("group", None),
        P(("group", "expert"), "tensor"),
    )
    out_specs = (
        P(("group", "expert"), "tensor"),
        P(("group", "expert"), "tensor"),
        P(("group", "expert"), None, "tensor"),
        P(("group", "expert"), None, "tensor"),
        P(("group", "expert"), "tensor", None),
        P(("group", "tensor"), "expert"),
        P(("group", "tensor"), "expert"),
    )
    return jax.shard_map(local, mesh=mesh, in_specs=in_specs, out_specs=out_specs, check_vma=False)
```

```python
import jax
import jax.numpy as jnp
from jax import lax
from jax.experimental import pallas as pl
from jax.experimental.pallas import tpu as pltpu
from jax.sharding import PartitionSpec as P

gate_unit = 2.0 ** (-15)
bf16 = jnp.bfloat16
f32 = jnp.float32

NN = (((1,), (0,)), ((), ()))
NT = (((1,), (1,)), ((), ()))
TN = (((0,), (0,)), ((), ()))


def dot(a, b, dims=NN):
    return lax.dot_general(a, b, dims, preferred_element_type=f32)


def join_projections(wg_ref, wu_ref, wgu):
    pair, _, width = wg_ref.shape
    for j in range(pair):
        wgu[:, 2 * j * width : (2 * j + 1) * width] = wg_ref[j]
        wgu[:, (2 * j + 1) * width : (2 * j + 2) * width] = wu_ref[j]


def accumulate(total, rows, part, step):
    total[rows, :] = jnp.where(step > 0, total[rows, :] + part, part)


def forward_kernel(
    x_ref, g_ref, wg_ref, wu_ref, wd_ref, hs_ref, cp_ref, cu_ref, lo_ref, wgu, lo_acc
):
    step = pl.program_id(0)
    pair, _, width = wg_ref.shape
    block = 512
    join_projections(wg_ref, wu_ref, wgu)

    for i in range(x_ref.shape[0] // block):
        rows = slice(i * block, (i + 1) * block)
        x = x_ref[rows, :]
        for j in range(pair):
            cols = slice(j * width, (j + 1) * width)
            both = dot(x, wgu[:, 2 * j * width : (2 * j + 2) * width])
            gate_pre, up_pre = both[:, :width], both[:, width:]
            gate = g_ref[0, rows, j : j + 1]
            sig = 0.5 * jnp.tanh(0.5 * gate_pre) + 0.5
            act = gate_pre * sig
            scaled = up_pre * gate
            hs_ref[rows, cols] = (act * scaled).astype(bf16)
            cu_ref[rows, cols] = (act * gate).astype(bf16)
            cp_ref[rows, cols] = (scaled * (sig + act * (1.0 - sig))).astype(bf16)
        accumulate(lo_acc, rows, dot(hs_ref[rows, :], wd_ref[...]), step)

    @pl.when(step == pl.num_programs(0) - 1)
    def _():
        lo_ref[...] = lo_acc[...].astype(bf16)


def backward_kernel(
    y_ref, cp_ref, cu_ref, wg_ref, wu_ref, wd_ref, dpu_ref, lig_ref, wgu, lig_acc
):
    step = pl.program_id(0)
    pair, _, width = wg_ref.shape
    block = 512
    join_projections(wg_ref, wu_ref, wgu)

    for i in range(y_ref.shape[0] // block):
        rows = slice(i * block, (i + 1) * block)
        hidden_grad = dot(y_ref[rows, :], wd_ref[...], NT)
        for j in range(pair):
            cols = slice(j * width, (j + 1) * width)
            hg = hidden_grad[:, cols]
            dp = hg * cp_ref[rows, cols].astype(f32)
            du = hg * cu_ref[rows, cols].astype(f32)
            dpu_ref[rows, 2 * j * width : (2 * j + 1) * width] = dp.astype(bf16)
            dpu_ref[rows, (2 * j + 1) * width : (2 * j + 2) * width] = du.astype(bf16)
        accumulate(lig_acc, rows, dot(dpu_ref[rows, :], wgu[...], NT), step)

    @pl.when(step == pl.num_programs(0) - 1)
    def _():
        lig_ref[...] = lig_acc[...].astype(bf16)


def down_grad_kernel(hs_ref, y_ref, dwd_ref):
    dwd_ref[...] = dot(hs_ref[...], y_ref[...], TN).astype(bf16)


def input_grad_kernel(x_ref, dpu_ref, dwg_ref, dwu_ref):
    pair, latent, width = dwg_ref.shape
    block = 256

    for i in range(latent // block):
        cols = slice(i * block, (i + 1) * block)
        grads = dot(x_ref[:, cols], dpu_ref[...], TN)
        for j in range(pair):
            dwg_ref[j, cols, :] = grads[:, 2 * j * width : (2 * j + 1) * width].astype(bf16)
            dwu_ref[j, cols, :] = grads[:, (2 * j + 1) * width : (2 * j + 2) * width].astype(bf16)


def shaped(*shape):
    return jax.ShapeDtypeStruct(shape, bf16)


def expert_calls(rows, latent, count, width):
    pair = 2 if rows <= 1024 and count % 2 == 0 else 1
    whole = pl.BlockSpec((rows, latent), lambda i: (0, 0))
    col_proj = pl.BlockSpec((pair, latent, width), lambda i: (i, 0, 0))
    row_proj = pl.BlockSpec((pair * width, latent), lambda i: (i, 0))
    hidden = pl.BlockSpec((rows, pair * width), lambda i: (0, i))
    hidden2 = pl.BlockSpec((rows, 2 * pair * width), lambda i: (0, i))
    gate_spec = pl.BlockSpec((1, rows, pair), lambda i: (i, 0, 0))
    joined = pltpu.VMEM((latent, 2 * pair * width), bf16)
    total = pltpu.VMEM((rows, latent), f32)
    units = 2 * rows * latent * width * count
    weight_bytes = 2 * latent * width * count
    hidden_bytes = 2 * rows * width * count
    latent_bytes = 2 * rows * latent

    def call(kernel, ins, outs, out_shape, scratch, parts, moved, exps=0):
        return pl.pallas_call(
            kernel,
            grid=(count // pair,),
            in_specs=ins,
            out_specs=outs,
            out_shape=out_shape,
            scratch_shapes=scratch,
            compiler_params=pltpu.CompilerParams(
                vmem_limit_bytes=(40 if rows <= 1024 else 56) * 1024 * 1024
            ),
            cost_estimate=pl.CostEstimate(
                flops=parts * units, bytes_accessed=moved, transcendentals=exps
            ),
        )

    hid = shaped(rows, count * width)
    lat = shaped(rows, latent)
    col = shaped(count, latent, width)
    forward = call(
        forward_kernel,
        [whole, gate_spec, col_proj, col_proj, row_proj],
        [hidden, hidden, hidden, whole],
        [hid, hid, hid, lat],
        [joined, total],
        3,
        3 * weight_bytes + 3 * hidden_bytes + 2 * latent_bytes,
        rows * width * count,
    )
    backward = call(
        backward_kernel,
        [whole, hidden, hidden, col_proj, col_proj, row_proj],
        [hidden2, whole],
        [shaped(rows, 2 * count * width), lat],
        [joined, total],
        3,
        3 * weight_bytes + 4 * hidden_bytes + 2 * latent_bytes,
    )
    down_grads = call(
        down_grad_kernel,
        [hidden, whole],
        row_proj,
        shaped(count * width, latent),
        [],
        1,
        weight_bytes + hidden_bytes + latent_bytes,
    )
    input_grads = call(
        input_grad_kernel,
        [whole, hidden2],
        [col_proj, col_proj],
        [col, col],
        [],
        2,
        2 * weight_bytes + 2 * hidden_bytes + latent_bytes,
    )

    def gate_blocks(gate_columns):
        return gate_columns.reshape(rows, count // pair, pair).transpose(1, 0, 2)

    return forward, backward, down_grads, input_grads, gate_blocks


def local(tokens, down_weight, up_weight, gate_proj, up_proj, down_proj, routes, gates, cotangent):
    n_expert = lax.axis_size("expert")
    n_group = lax.axis_size("group")
    own = lax.axis_index("expert")
    t = lax.axis_index("tensor")
    tok_rows = tokens.shape[0]
    half_rows = tok_rows // 2
    quarter_d = tokens.shape[1] // 4
    exp_local, latent, width = gate_proj.shape
    shard = down_weight.shape[1]

    nh = n_expert // 4
    h, q = own // 4, own % 4
    cols = latent // nh
    shared = n_group % 2 == 0
    g = lax.axis_index("group") % 2

    def to_peer(v, r):
        return lax.ppermute(v, "expert", [(e, e ^ r) for e in range(n_expert)])

    def t_swap(v):
        return lax.ppermute(v, "tensor", [(0, 1), (1, 0)])

    def g_swap(v):
        return lax.ppermute(v, "group", [(i, i ^ 1) for i in range(n_group)])

    def up(v):
        return lax.ppermute(v, "expert", [(e, (e + 4) % n_expert) for e in range(n_expert)])

    def down(v):
        return lax.ppermute(v, "expert", [((e + 4) % n_expert, e) for e in range(n_expert)])

    def add(*terms):
        return sum(v.astype(f32) for v in terms).astype(bf16)

    def after(v, *done):
        return lax.optimization_barrier((v, *done))[0]

    def turn(blocks):
        result = []
        for k in range(nh):
            block = blocks[-k % nh]
            for i in range(1, nh):
                block = jnp.where(h == i, blocks[(i - k) % nh], block)
            result.append(block)
        return result

    def by_quarter(parts):
        low = [jnp.where(q % 2 == 0, parts[i], parts[i ^ 1]) for i in range(4)]
        return [jnp.where(q < 2, low[i], low[i ^ 2]) for i in range(4)]

    def flip(v, index, axis):
        first, second = jnp.split(v, 2, axis=axis)
        return jnp.where(index == 0, v, jnp.concatenate([second, first], axis=axis))

    def exchange(block_for):
        return [block_for(0)] + [to_peer(block_for(r), r) for r in (1, 2, 3)]

    def together(*values):
        return lax.optimization_barrier(values)

    def gather_h(v):
        parts = [v]
        for _ in range(nh - 1):
            parts.append(up(parts[-1]))
        return parts

    def to_square(v, k, r):
        perm = [(e, (e // 4 + k) % nh * 4 + (e % 4 ^ r)) for e in range(n_expert)]
        return lax.ppermute(v, "expert", perm)

    def pair_rows(v):
        def quarters(i):
            parts = [(2 * j + i) * quarter_d for j in (0, 1)]
            parts = [lax.dynamic_slice_in_dim(v, at, quarter_d, 1) for at in parts]
            return jnp.concatenate(parts, axis=1)

        return quarters(q % 2), to_peer(quarters(1 - q % 2), 1)

    def by_half(v):
        mine = lax.dynamic_slice_in_dim(v, q // 2 * quarter_d, quarter_d, 1)
        return mine, lax.dynamic_slice_in_dim(v, (1 - q // 2) * quarter_d, quarter_d, 1)

    def far_rows(mine, other):
        return [(to_square(mine, k, 0), to_square(other, k, 2)) for k in range(1, nh)]

    def near_rows(v):
        size = 2 * quarter_d
        mine = lax.dynamic_slice_in_dim(v, q // 2 * size, size, 1)
        other = lax.dynamic_slice_in_dim(v, (1 - q // 2) * size, size, 1)
        return mine, to_peer(other, 2)

    def near_quarters(mine, theirs):
        v = jnp.concatenate([mine, theirs], axis=0)
        mine = lax.dynamic_slice_in_dim(v, q % 2 * quarter_d, quarter_d, 1)
        other = lax.dynamic_slice_in_dim(v, (1 - q % 2) * quarter_d, quarter_d, 1)
        return mine, to_peer(other, 1)

    def join_rows(mine, theirs):
        parts = [v[i * tok_rows : (i + 1) * tok_rows] for i in (0, 1) for v in (mine, theirs)]
        return jnp.concatenate(parts, axis=0)

    def join_pairs(parts):
        return [jnp.concatenate(v, axis=0) for v in parts]

    def square_weight(v):
        size = quarter_d // 2 if shared else quarter_d
        first = g * size if shared else 0
        parts = exchange(
            lambda r: lax.dynamic_slice_in_dim(v, (q ^ r) * quarter_d + first, size, 0)
        )
        return parts

    def join_quarters(parts):
        return jnp.concatenate(by_quarter(parts), axis=1)

    def first_weight(v):
        size = quarter_d // 2 if shared else quarter_d
        first = g * size if shared else 0

        def half(i):
            starts = [(2 * i + j) * quarter_d + first for j in (0, 1)]
            return jnp.stack([lax.dynamic_slice_in_dim(v, at, size, 0) for at in starts])

        return half(q // 2), to_peer(half(1 - q // 2), 2)

    def second_weight(mine, theirs):
        both = jnp.concatenate([mine, theirs], axis=2)
        other = lax.dynamic_index_in_dim(both, 1 - q % 2, 0, keepdims=False)
        return lax.dynamic_index_in_dim(both, q % 2, 0, keepdims=False), to_peer(other, 1)

    def join_steps(mine, theirs):
        return join_quarters([v[:, i * shard : (i + 1) * shard] for i in (0, 1) for v in (mine, theirs)])

    def swap_features(v):
        return g_swap(v) if shared else v

    def all_features(v, theirs):
        return flip(jnp.concatenate([v, theirs], axis=0), g, 0) if shared else v

    def project(rows, weight):
        parts = [dot(v, weight).astype(bf16).reshape(4, 2, half_rows, cols) for v in rows]
        part = jnp.stack(parts, axis=1)
        mine = lax.dynamic_index_in_dim(part, t, 2, keepdims=False)
        return mine, lax.dynamic_index_in_dim(part, 1 - t, 2, keepdims=False)

    def project_square(rows, weights):
        parts = [dot(rows, weight).astype(bf16) for weight in weights]
        part = jnp.concatenate(parts, axis=1).reshape(4, 2, half_rows, latent)
        mine = lax.dynamic_index_in_dim(part, t, 1, keepdims=False)
        return mine, lax.dynamic_index_in_dim(part, 1 - t, 1, keepdims=False)

    def own_latent(pieces):
        rows = []
        for k in range(nh):
            blocks = turn([pieces[j][(k - j) % nh] for j in range(nh)])
            rows.append(jnp.concatenate(blocks, axis=1))
        return jnp.stack(rows)

    def sum_tensor(part):
        part = part.reshape(2, 4, nh, half_rows, latent)
        return add(part[0], t_swap(part[1]))

    def sum_squares(part):
        if nh == 2:
            return part, up(part)
        total = part[nh - 1]
        for k in range(nh - 2, -1, -1):
            total = add(down(total), part[k])
        return part, jnp.stack(gather_h(total))

    def join_squares(part, theirs):
        rows = [add(part[0], theirs[1]), add(part[1], theirs[0])] if nh == 2 else list(theirs)
        split = [turn(jnp.split(v, nh, axis=1)) for v in rows]
        return jnp.concatenate(split[0] + [v[0] for v in split[1:]], axis=1)

    def square_blocks(part):
        part = flip(jnp.stack([part, t_swap(part)], axis=1), t, 1)
        return jnp.split(part.reshape(4 * tok_rows, -1), 2 * nh - 1, axis=1)

    def products(blocks, rows, weights):
        grad = sum(dot(v, block, TN) for v, block in zip(rows, blocks[:1] + blocks[nh:]))
        whole = sum(dot(block, weight, NT) for block, weight in zip(blocks, weights))
        return grad.astype(bf16), whole.astype(bf16)

    def send_products(grad, whole):
        whole = whole.reshape(4, tok_rows, quarter_d)
        grads = exchange(lambda r: lax.dynamic_slice_in_dim(grad, (q ^ r) * shard, shard, 1))
        return grads, exchange(lambda r: whole[r])

    def join_products(grads, wholes):
        grad = jnp.concatenate(by_quarter(grads), axis=0).astype(f32)
        return jnp.concatenate(by_quarter(wholes), axis=1), grad

    local_ids = own * exp_local + jnp.arange(exp_local, dtype=jnp.int32)
    hit = routes[:, :, None] == local_ids[None, None, :]
    gate_all = jnp.sum(jnp.where(hit, gates[:, :, None], 0), axis=1).astype(f32) * gate_unit
    gate_all = gate_all.reshape(nh, 4, 2, half_rows, exp_local)
    gate_all = jnp.stack(turn(list(gate_all)))
    gate_all = jnp.stack(by_quarter([gate_all[:, i] for i in range(4)]))
    gate_all = flip(gate_all, t, 2)
    gate_columns = gate_all.transpose(2, 0, 1, 3, 4).reshape(-1, exp_local)

    group_rows = n_expert * tok_rows
    forward, backward, down_grads, input_grads, gate_blocks = expert_calls(
        group_rows, latent, exp_local, width
    )
    down_rows = down_proj.reshape(exp_local * width, latent)

    def rows_with(part, theirs):
        return jnp.stack([part, theirs]).reshape(-1, latent)

    tok_mine, tok_theirs = pair_rows(tokens)
    mine, other = by_half(tok_mine)
    far = far_rows(mine, other)
    down_half = square_weight(down_weight)
    first = (tok_theirs, *down_half[1:])
    up_mine, up_theirs = first_weight(after(up_weight, *first))
    cot_mine, cot_theirs = near_rows(after(cotangent, *down_half[1:]))
    mine2, other2 = by_half(tok_theirs)
    near = to_peer(jnp.concatenate([other, other2], axis=0), 2)
    far2 = far_rows(after(mine2, *far[-1]), after(other2, *far[-1]))
    down_half = join_quarters(down_half)
    down_theirs = swap_features(down_half)
    up_mine, up_theirs = second_weight(up_mine, up_theirs)
    cot_mine, cot_other = near_quarters(cot_mine, cot_theirs)
    near, *far2[-1], down_theirs, up_theirs, cot_other = together(
        near, *far2[-1], down_theirs, up_theirs, cot_other
    )
    token_parts = [(mine, mine2, near)] + [
        (a[0], b[0], a[1], b[1]) for a, b in zip(far, far2)
    ]
    token_parts = join_pairs(token_parts)
    cot_rows = join_rows(cot_mine, cot_other)
    down_own = all_features(down_half, down_theirs)
    up_halves = gather_h(join_steps(up_mine, up_theirs))

    mine, other = project(token_parts, down_own)
    part_x = add(mine, t_swap(other))
    part_x = exchange(lambda r: part_x[r])
    *part_x, up_halves[-1] = together(*part_x, up_halves[-1])
    part_x = gather_h(add(*part_x))
    up_theirs = [swap_features(v) for v in up_halves]
    part_x[-1], up_theirs[-1] = together(part_x[-1], up_theirs[-1])
    up_parts = [all_features(v, w) for v, w in zip(up_halves, up_theirs)]
    part_x = own_latent(part_x)
    cot_first = after(cot_rows[: 2 * tok_rows], part_x)
    part_x = jnp.stack(exchange(lambda r: part_x))
    mine, other = project_square(cot_rows, up_parts)
    part_y = add(mine, t_swap(other))
    part_y = add(*exchange(lambda r: part_y[r]))
    part_y = jnp.concatenate(turn(jnp.split(part_y, nh, axis=1)), axis=1)
    part_y = jnp.stack(gather_h(part_y))
    part_x = after(part_x, part_y)
    latent_in = rows_with(part_x, t_swap(part_x))
    cot_first = gather_h(cot_first)

    hs, cp, cu, out_part = forward(
        latent_in, gate_blocks(gate_columns), gate_proj, up_proj, down_rows
    )
    part_y = exchange(lambda r: part_y)
    *part_y, cot_first[-1], out_part = together(*part_y, cot_first[-1], out_part)
    part_y = jnp.stack(part_y)
    latent_grad = rows_with(part_y, t_swap(part_y))
    down_far = gather_h(after(down_half, cot_first[-1]))[1:]
    cot_second = gather_h(after(cot_rows[2 * tok_rows :], cot_first[-1]))
    out_part = sum_tensor(out_part)
    dpu, in_part = backward(
        after(latent_grad, out_part), cp, cu, gate_proj, up_proj, down_rows
    )
    out_part = exchange(lambda r: out_part[r])
    *out_part, down_far[-1], cot_second[-1], in_part = together(
        *out_part, down_far[-1], cot_second[-1], in_part
    )
    down_theirs = [swap_features(v) for v in down_far]
    cot_parts = join_pairs(zip(cot_first, cot_second))
    out_part = add(*out_part)
    in_part = sum_tensor(in_part)
    gate_proj_grad, up_proj_grad = input_grads(latent_in, after(dpu, in_part))
    in_part = exchange(lambda r: in_part[r])
    *in_part, out_theirs, down_theirs[-1], gate_proj_grad = together(
        *in_part, sum_squares(out_part)[1], down_theirs[-1], gate_proj_grad
    )
    down_parts = [down_own] + [all_features(v, w) for v, w in zip(down_far, down_theirs)]
    out_part = join_squares(out_part, out_theirs)
    in_part, in_theirs = sum_squares(add(*in_part))
    out_part = exchange(lambda r: out_part)
    down_proj_grad = down_grads(hs, after(latent_grad, in_part))
    *out_part, in_theirs, down_proj_grad = together(*out_part, in_theirs, down_proj_grad)
    out_part = jnp.stack(out_part)
    in_part = join_squares(in_part, in_theirs)
    in_part = exchange(lambda r: in_part)
    out_products = products(square_blocks(out_part), cot_parts, up_parts)
    in_part = jnp.stack(together(*in_part, *out_products)[:4])
    out_sent = send_products(*out_products)
    in_products = products(square_blocks(in_part), token_parts, down_parts)
    received = together(*out_sent[0], *out_sent[1], *in_products)
    out, up_grad = join_products(received[:4], received[4:8])
    tokens_grad, down_grad = join_products(*send_products(*in_products))
    down_proj_grad = down_proj_grad.reshape(down_proj.shape)
    return (out, tokens_grad, gate_proj_grad, up_proj_grad, down_proj_grad, down_grad, up_grad)


def solution(mesh):
    in_specs = (
        P(("group", "expert"), "tensor"),
        P("tensor", "expert"),
        P("tensor", "expert"),
        P("expert", None, "tensor"),
        P("expert", None, "tensor"),
        P("expert", "tensor", None),
        P("group", None),
        P("group", None),
        P(("group", "expert"), "tensor"),
    )
    out_specs = (
        P(("group", "expert"), "tensor"),
        P(("group", "expert"), "tensor"),
        P(("group", "expert"), None, "tensor"),
        P(("group", "expert"), None, "tensor"),
        P(("group", "expert"), "tensor", None),
        P(("group", "tensor"), "expert"),
        P(("group", "tensor"), "expert"),
    )
    return jax.shard_map(local, mesh=mesh, in_specs=in_specs, out_specs=out_specs, check_vma=False)
```

```python
import jax
import jax.numpy as jnp
from jax import lax
from jax.experimental import pallas as pl
from jax.experimental.pallas import tpu as pltpu
from jax.sharding import PartitionSpec as P

gate_unit = 2.0 ** (-15)
bf16 = jnp.bfloat16
f32 = jnp.float32

NN = (((1,), (0,)), ((), ()))
NT = (((1,), (1,)), ((), ()))
TN = (((0,), (0,)), ((), ()))


def dot(a, b, dims=NN):
    return lax.dot_general(a, b, dims, preferred_element_type=f32)


def join_projections(wg_ref, wu_ref, wgu):
    pair, _, width = wg_ref.shape
    for j in range(pair):
        wgu[:, 2 * j * width : (2 * j + 1) * width] = wg_ref[j]
        wgu[:, (2 * j + 1) * width : (2 * j + 2) * width] = wu_ref[j]


def accumulate(total, rows, part, step):
    total[rows, :] = jnp.where(step > 0, total[rows, :] + part, part)


def forward_kernel(
    x_ref, g_ref, wg_ref, wu_ref, wd_ref, hs_ref, cp_ref, cu_ref, lo_ref, wgu, lo_acc
):
    step = pl.program_id(0)
    pair, _, width = wg_ref.shape
    block = 512
    join_projections(wg_ref, wu_ref, wgu)

    for i in range(x_ref.shape[0] // block):
        rows = slice(i * block, (i + 1) * block)
        x = x_ref[rows, :]
        for j in range(pair):
            cols = slice(j * width, (j + 1) * width)
            both = dot(x, wgu[:, 2 * j * width : (2 * j + 2) * width])
            gate_pre, up_pre = both[:, :width], both[:, width:]
            gate = g_ref[0, rows, j : j + 1]
            sig = 0.5 * jnp.tanh(0.5 * gate_pre) + 0.5
            act = gate_pre * sig
            scaled = up_pre * gate
            hs_ref[rows, cols] = (act * scaled).astype(bf16)
            cu_ref[rows, cols] = (act * gate).astype(bf16)
            cp_ref[rows, cols] = (scaled * (sig + act * (1.0 - sig))).astype(bf16)
        accumulate(lo_acc, rows, dot(hs_ref[rows, :], wd_ref[...]), step)

    @pl.when(step == pl.num_programs(0) - 1)
    def _():
        lo_ref[...] = lo_acc[...].astype(bf16)


def backward_kernel(
    y_ref, cp_ref, cu_ref, wg_ref, wu_ref, wd_ref, dpu_ref, lig_ref, wgu, lig_acc
):
    step = pl.program_id(0)
    pair, _, width = wg_ref.shape
    block = 512
    join_projections(wg_ref, wu_ref, wgu)

    for i in range(y_ref.shape[0] // block):
        rows = slice(i * block, (i + 1) * block)
        hidden_grad = dot(y_ref[rows, :], wd_ref[...], NT)
        for j in range(pair):
            cols = slice(j * width, (j + 1) * width)
            hg = hidden_grad[:, cols]
            dp = hg * cp_ref[rows, cols].astype(f32)
            du = hg * cu_ref[rows, cols].astype(f32)
            dpu_ref[rows, 2 * j * width : (2 * j + 1) * width] = dp.astype(bf16)
            dpu_ref[rows, (2 * j + 1) * width : (2 * j + 2) * width] = du.astype(bf16)
        accumulate(lig_acc, rows, dot(dpu_ref[rows, :], wgu[...], NT), step)

    @pl.when(step == pl.num_programs(0) - 1)
    def _():
        lig_ref[...] = lig_acc[...].astype(bf16)


def down_grad_kernel(hs_ref, y_ref, dwd_ref):
    dwd_ref[...] = dot(hs_ref[...], y_ref[...], TN).astype(bf16)


def input_grad_kernel(x_ref, dpu_ref, dwg_ref, dwu_ref):
    pair, latent, width = dwg_ref.shape
    block = 256

    for i in range(latent // block):
        cols = slice(i * block, (i + 1) * block)
        grads = dot(x_ref[:, cols], dpu_ref[...], TN)
        for j in range(pair):
            dwg_ref[j, cols, :] = grads[:, 2 * j * width : (2 * j + 1) * width].astype(bf16)
            dwu_ref[j, cols, :] = grads[:, (2 * j + 1) * width : (2 * j + 2) * width].astype(bf16)


def shaped(*shape):
    return jax.ShapeDtypeStruct(shape, bf16)


def expert_calls(rows, latent, count, width):
    pair = 2 if rows <= 1024 and count % 2 == 0 else 1
    whole = pl.BlockSpec((rows, latent), lambda i: (0, 0))
    col_proj = pl.BlockSpec((pair, latent, width), lambda i: (i, 0, 0))
    row_proj = pl.BlockSpec((pair * width, latent), lambda i: (i, 0))
    hidden = pl.BlockSpec((rows, pair * width), lambda i: (0, i))
    hidden2 = pl.BlockSpec((rows, 2 * pair * width), lambda i: (0, i))
    gate_spec = pl.BlockSpec((1, rows, pair), lambda i: (i, 0, 0))
    joined = pltpu.VMEM((latent, 2 * pair * width), bf16)
    total = pltpu.VMEM((rows, latent), f32)
    units = 2 * rows * latent * width * count
    weight_bytes = 2 * latent * width * count
    hidden_bytes = 2 * rows * width * count
    latent_bytes = 2 * rows * latent

    def call(kernel, ins, outs, out_shape, scratch, parts, moved, exps=0):
        return pl.pallas_call(
            kernel,
            grid=(count // pair,),
            in_specs=ins,
            out_specs=outs,
            out_shape=out_shape,
            scratch_shapes=scratch,
            compiler_params=pltpu.CompilerParams(
                vmem_limit_bytes=(40 if rows <= 1024 else 56) * 1024 * 1024
            ),
            cost_estimate=pl.CostEstimate(
                flops=parts * units, bytes_accessed=moved, transcendentals=exps
            ),
        )

    hid = shaped(rows, count * width)
    lat = shaped(rows, latent)
    col = shaped(count, latent, width)
    forward = call(
        forward_kernel,
        [whole, gate_spec, col_proj, col_proj, row_proj],
        [hidden, hidden, hidden, whole],
        [hid, hid, hid, lat],
        [joined, total],
        3,
        3 * weight_bytes + 3 * hidden_bytes + 2 * latent_bytes,
        rows * width * count,
    )
    backward = call(
        backward_kernel,
        [whole, hidden, hidden, col_proj, col_proj, row_proj],
        [hidden2, whole],
        [shaped(rows, 2 * count * width), lat],
        [joined, total],
        3,
        3 * weight_bytes + 4 * hidden_bytes + 2 * latent_bytes,
    )
    down_grads = call(
        down_grad_kernel,
        [hidden, whole],
        row_proj,
        shaped(count * width, latent),
        [],
        1,
        weight_bytes + hidden_bytes + latent_bytes,
    )
    input_grads = call(
        input_grad_kernel,
        [whole, hidden2],
        [col_proj, col_proj],
        [col, col],
        [],
        2,
        2 * weight_bytes + 2 * hidden_bytes + latent_bytes,
    )

    def gate_blocks(gate_columns):
        return gate_columns.reshape(rows, count // pair, pair).transpose(1, 0, 2)

    return forward, backward, down_grads, input_grads, gate_blocks


def local(tokens, down_weight, up_weight, gate_proj, up_proj, down_proj, routes, gates, cotangent):
    n_expert = lax.axis_size("expert")
    n_group = lax.axis_size("group")
    own = lax.axis_index("expert")
    t = lax.axis_index("tensor")
    tok_rows = tokens.shape[0]
    half_rows = tok_rows // 2
    quarter_d = tokens.shape[1] // 4
    exp_local, latent, width = gate_proj.shape
    shard = down_weight.shape[1]

    nh = n_expert // 4
    h, q = own // 4, own % 4
    cols = latent // nh
    shared = n_group % 2 == 0
    g = lax.axis_index("group") % 2

    def to_peer(v, r):
        return lax.ppermute(v, "expert", [(e, e ^ r) for e in range(n_expert)])

    def t_swap(v):
        return lax.ppermute(v, "tensor", [(0, 1), (1, 0)])

    def g_swap(v):
        return lax.ppermute(v, "group", [(i, i ^ 1) for i in range(n_group)])

    def up(v):
        return lax.ppermute(v, "expert", [(e, (e + 4) % n_expert) for e in range(n_expert)])

    def down(v):
        return lax.ppermute(v, "expert", [((e + 4) % n_expert, e) for e in range(n_expert)])

    def add(*terms):
        return sum(v.astype(f32) for v in terms).astype(bf16)

    def after(v, *done):
        return lax.optimization_barrier((v, *done))[0]

    def turn(blocks):
        result = []
        for k in range(nh):
            block = blocks[-k % nh]
            for i in range(1, nh):
                block = jnp.where(h == i, blocks[(i - k) % nh], block)
            result.append(block)
        return result

    def by_quarter(parts):
        low = [jnp.where(q % 2 == 0, parts[i], parts[i ^ 1]) for i in range(4)]
        return [jnp.where(q < 2, low[i], low[i ^ 2]) for i in range(4)]

    def flip(v, index, axis):
        first, second = jnp.split(v, 2, axis=axis)
        return jnp.where(index == 0, v, jnp.concatenate([second, first], axis=axis))

    def exchange(block_for):
        return [block_for(0)] + [to_peer(block_for(r), r) for r in (1, 2, 3)]

    def together(*values):
        return lax.optimization_barrier(values)

    def gather_h(v):
        parts = [v]
        for _ in range(nh - 1):
            parts.append(up(parts[-1]))
        return parts

    def to_square(v, k, r):
        perm = [(e, (e // 4 + k) % nh * 4 + (e % 4 ^ r)) for e in range(n_expert)]
        return lax.ppermute(v, "expert", perm)

    def pair_rows(v):
        def quarters(i):
            parts = [(2 * j + i) * quarter_d for j in (0, 1)]
            parts = [lax.dynamic_slice_in_dim(v, at, quarter_d, 1) for at in parts]
            return jnp.concatenate(parts, axis=1)

        return quarters(q % 2), to_peer(quarters(1 - q % 2), 1)

    def by_half(v):
        mine = lax.dynamic_slice_in_dim(v, q // 2 * quarter_d, quarter_d, 1)
        return mine, lax.dynamic_slice_in_dim(v, (1 - q // 2) * quarter_d, quarter_d, 1)

    def far_rows(mine, other):
        return [(to_square(mine, k, 0), to_square(other, k, 2)) for k in range(1, nh)]

    def near_rows(v):
        size = 2 * quarter_d
        mine = lax.dynamic_slice_in_dim(v, q // 2 * size, size, 1)
        other = lax.dynamic_slice_in_dim(v, (1 - q // 2) * size, size, 1)
        return mine, to_peer(other, 2)

    def near_quarters(mine, theirs):
        v = jnp.concatenate([mine, theirs], axis=0)
        mine = lax.dynamic_slice_in_dim(v, q % 2 * quarter_d, quarter_d, 1)
        other = lax.dynamic_slice_in_dim(v, (1 - q % 2) * quarter_d, quarter_d, 1)
        return mine, to_peer(other, 1)

    def join_rows(mine, theirs):
        parts = [v[i * tok_rows : (i + 1) * tok_rows] for i in (0, 1) for v in (mine, theirs)]
        return jnp.concatenate(parts, axis=0)

    def join_pairs(parts):
        return [jnp.concatenate(v, axis=0) for v in parts]

    def square_weight(v):
        size = quarter_d // 2 if shared else quarter_d
        first = g * size if shared else 0
        parts = exchange(
            lambda r: lax.dynamic_slice_in_dim(v, (q ^ r) * quarter_d + first, size, 0)
        )
        return parts

    def join_quarters(parts):
        return jnp.concatenate(by_quarter(parts), axis=1)

    def first_weight(v):
        size = quarter_d // 2 if shared else quarter_d
        first = g * size if shared else 0

        def half(i):
            starts = [(2 * i + j) * quarter_d + first for j in (0, 1)]
            return jnp.stack([lax.dynamic_slice_in_dim(v, at, size, 0) for at in starts])

        return half(q // 2), to_peer(half(1 - q // 2), 2)

    def second_weight(mine, theirs):
        both = jnp.concatenate([mine, theirs], axis=2)
        other = lax.dynamic_index_in_dim(both, 1 - q % 2, 0, keepdims=False)
        return lax.dynamic_index_in_dim(both, q % 2, 0, keepdims=False), to_peer(other, 1)

    def join_steps(mine, theirs):
        return join_quarters([v[:, i * shard : (i + 1) * shard] for i in (0, 1) for v in (mine, theirs)])

    def swap_features(v):
        return g_swap(v) if shared else v

    def all_features(v, theirs):
        return flip(jnp.concatenate([v, theirs], axis=0), g, 0) if shared else v

    def project(rows, weight):
        parts = [dot(v, weight).astype(bf16).reshape(4, 2, half_rows, cols) for v in rows]
        part = jnp.stack(parts, axis=1)
        mine = lax.dynamic_index_in_dim(part, t, 2, keepdims=False)
        return mine, lax.dynamic_index_in_dim(part, 1 - t, 2, keepdims=False)

    def project_square(rows, weights):
        parts = [dot(rows, weight).astype(bf16) for weight in weights]
        part = jnp.concatenate(parts, axis=1).reshape(4, 2, half_rows, latent)
        mine = lax.dynamic_index_in_dim(part, t, 1, keepdims=False)
        return mine, lax.dynamic_index_in_dim(part, 1 - t, 1, keepdims=False)

    def own_latent(pieces):
        rows = []
        for k in range(nh):
            blocks = turn([pieces[j][(k - j) % nh] for j in range(nh)])
            rows.append(jnp.concatenate(blocks, axis=1))
        return jnp.stack(rows)

    def sum_tensor(part):
        part = part.reshape(2, 4, nh, half_rows, latent)
        return add(part[0], t_swap(part[1]))

    def sum_squares(part):
        if nh == 2:
            return part, up(part)
        total = part[nh - 1]
        for k in range(nh - 2, -1, -1):
            total = add(down(total), part[k])
        return part, jnp.stack(gather_h(total))

    def join_squares(part, theirs):
        rows = [add(part[0], theirs[1]), add(part[1], theirs[0])] if nh == 2 else list(theirs)
        split = [turn(jnp.split(v, nh, axis=1)) for v in rows]
        return jnp.concatenate(split[0] + [v[0] for v in split[1:]], axis=1)

    def square_blocks(part):
        part = flip(jnp.stack([part, t_swap(part)], axis=1), t, 1)
        return jnp.split(part.reshape(4 * tok_rows, -1), 2 * nh - 1, axis=1)

    def products(blocks, rows, weights):
        grad = sum(dot(v, block, TN) for v, block in zip(rows, blocks[:1] + blocks[nh:]))
        whole = sum(dot(block, weight, NT) for block, weight in zip(blocks, weights))
        return grad.astype(bf16), whole.astype(bf16)

    def send_products(grad, whole):
        whole = whole.reshape(4, tok_rows, quarter_d)
        grads = exchange(lambda r: lax.dynamic_slice_in_dim(grad, (q ^ r) * shard, shard, 1))
        return grads, exchange(lambda r: whole[r])

    def join_products(grads, wholes):
        grad = jnp.concatenate(by_quarter(grads), axis=0).astype(f32)
        return jnp.concatenate(by_quarter(wholes), axis=1), grad

    local_ids = own * exp_local + jnp.arange(exp_local, dtype=jnp.int32)
    hit = routes[:, :, None] == local_ids[None, None, :]
    gate_all = jnp.sum(jnp.where(hit, gates[:, :, None], 0), axis=1).astype(f32) * gate_unit
    gate_all = gate_all.reshape(nh, 4, 2, half_rows, exp_local)
    gate_all = jnp.stack(turn(list(gate_all)))
    gate_all = jnp.stack(by_quarter([gate_all[:, i] for i in range(4)]))
    gate_all = flip(gate_all, t, 2)
    gate_columns = gate_all.transpose(2, 0, 1, 3, 4).reshape(-1, exp_local)

    group_rows = n_expert * tok_rows
    forward, backward, down_grads, input_grads, gate_blocks = expert_calls(
        group_rows, latent, exp_local, width
    )
    down_rows = down_proj.reshape(exp_local * width, latent)

    def rows_with(part, theirs):
        return jnp.stack([part, theirs]).reshape(-1, latent)

    tok_mine, tok_theirs = pair_rows(tokens)
    mine, other = by_half(tok_mine)
    far = far_rows(mine, other)
    down_half = square_weight(down_weight)
    first = (tok_theirs, *down_half[1:])
    up_mine, up_theirs = first_weight(after(up_weight, *first))
    cot_mine, cot_theirs = near_rows(after(cotangent, *down_half[1:]))
    mine2, other2 = by_half(tok_theirs)
    near = to_peer(jnp.concatenate([other, other2], axis=0), 2)
    far2 = far_rows(after(mine2, *far[-1]), after(other2, *far[-1]))
    down_half = join_quarters(down_half)
    down_theirs = swap_features(down_half)
    up_mine, up_theirs = second_weight(up_mine, up_theirs)
    cot_mine, cot_other = near_quarters(cot_mine, cot_theirs)
    near, *far2[-1], down_theirs, up_theirs, cot_other = together(
        near, *far2[-1], down_theirs, up_theirs, cot_other
    )
    token_parts = [(mine, mine2, near)] + [
        (a[0], b[0], a[1], b[1]) for a, b in zip(far, far2)
    ]
    token_parts = join_pairs(token_parts)
    cot_rows = join_rows(cot_mine, cot_other)
    down_own = all_features(down_half, down_theirs)
    up_halves = gather_h(join_steps(up_mine, up_theirs))

    mine, other = project(token_parts, down_own)
    part_x = add(mine, t_swap(other))
    part_x = exchange(lambda r: part_x[r])
    *part_x, up_halves[-1] = together(*part_x, up_halves[-1])
    part_x = gather_h(add(*part_x))
    up_theirs = [swap_features(v) for v in up_halves]
    part_x[-1], up_theirs[-1] = together(part_x[-1], up_theirs[-1])
    up_parts = [all_features(v, w) for v, w in zip(up_halves, up_theirs)]
    part_x = own_latent(part_x)
    cot_first = after(cot_rows[: 2 * tok_rows], part_x)
    part_x = jnp.stack(exchange(lambda r: part_x))
    mine, other = project_square(cot_rows, up_parts)
    part_y = add(mine, t_swap(other))
    part_y = add(*exchange(lambda r: part_y[r]))
    part_y = jnp.concatenate(turn(jnp.split(part_y, nh, axis=1)), axis=1)
    part_y = jnp.stack(gather_h(part_y))
    part_x = after(part_x, part_y)
    latent_in = rows_with(part_x, t_swap(part_x))
    cot_first = gather_h(cot_first)

    hs, cp, cu, out_part = forward(
        latent_in, gate_blocks(gate_columns), gate_proj, up_proj, down_rows
    )
    part_y = exchange(lambda r: part_y)
    *part_y, cot_first[-1], out_part = together(*part_y, cot_first[-1], out_part)
    part_y = jnp.stack(part_y)
    latent_grad = rows_with(part_y, t_swap(part_y))
    cot_second = gather_h(after(cot_rows[2 * tok_rows :], cot_first[-1]))
    out_part = sum_tensor(out_part)
    dpu, in_part = backward(
        after(latent_grad, out_part), cp, cu, gate_proj, up_proj, down_rows
    )
    out_part = exchange(lambda r: out_part[r])
    *out_part, cot_second[-1], in_part = together(*out_part, cot_second[-1], in_part)
    down_far = gather_h(after(down_half, in_part))[1:]
    cot_parts = join_pairs(zip(cot_first, cot_second))
    out_part = add(*out_part)
    in_part = sum_tensor(in_part)
    gate_proj_grad, up_proj_grad = input_grads(latent_in, after(dpu, in_part))
    in_part = exchange(lambda r: in_part[r])
    *in_part, out_theirs, down_far[-1], gate_proj_grad = together(
        *in_part, sum_squares(out_part)[1], down_far[-1], gate_proj_grad
    )
    down_theirs = [swap_features(v) for v in down_far]
    out_part = join_squares(out_part, out_theirs)
    in_part, in_theirs = sum_squares(add(*in_part))
    out_part = exchange(lambda r: out_part)
    down_proj_grad = down_grads(hs, after(latent_grad, in_part))
    *out_part, in_theirs, down_theirs[-1], down_proj_grad = together(
        *out_part, in_theirs, down_theirs[-1], down_proj_grad
    )
    down_parts = [down_own] + [all_features(v, w) for v, w in zip(down_far, down_theirs)]
    out_part = jnp.stack(out_part)
    in_part = join_squares(in_part, in_theirs)
    in_part = exchange(lambda r: in_part)
    out_products = products(square_blocks(out_part), cot_parts, up_parts)
    in_part = jnp.stack(together(*in_part, *out_products)[:4])
    out_sent = send_products(*out_products)
    in_products = products(square_blocks(in_part), token_parts, down_parts)
    received = together(*out_sent[0], *out_sent[1], *in_products)
    out, up_grad = join_products(received[:4], received[4:8])
    tokens_grad, down_grad = join_products(*send_products(*in_products))
    down_proj_grad = down_proj_grad.reshape(down_proj.shape)
    return (out, tokens_grad, gate_proj_grad, up_proj_grad, down_proj_grad, down_grad, up_grad)


def solution(mesh):
    in_specs = (
        P(("group", "expert"), "tensor"),
        P("tensor", "expert"),
        P("tensor", "expert"),
        P("expert", None, "tensor"),
        P("expert", None, "tensor"),
        P("expert", "tensor", None),
        P("group", None),
        P("group", None),
        P(("group", "expert"), "tensor"),
    )
    out_specs = (
        P(("group", "expert"), "tensor"),
        P(("group", "expert"), "tensor"),
        P(("group", "expert"), None, "tensor"),
        P(("group", "expert"), None, "tensor"),
        P(("group", "expert"), "tensor", None),
        P(("group", "tensor"), "expert"),
        P(("group", "tensor"), "expert"),
    )
    return jax.shard_map(local, mesh=mesh, in_specs=in_specs, out_specs=out_specs, check_vma=False)
```
